128 devices in a mesh: fsdp: 128 (over x, z, y, core).
Axes of the slice: x: 4, y: 4, z: 4, core: 2. Of those that a mesh axis runs over, the one named last changes fastest.
Arguments:
- tokens_in: bfloat16 [32768, 1536], P('fsdp'), may hold values from -24 to 24
- cotangent: bfloat16 [32768, 1536], P('fsdp'), may hold values from -6 to 6
- segment_ids: int32 [32768], P('fsdp'), may hold values from 0 to 3, as said below
- proj_qkv: float32 [1536, 3072], P('fsdp'), may hold values from -0.15625 to 0.15625
- proj_out: float32 [1536, 1536], P('fsdp'), may hold values from -0.625 to 0.625
- proj_up: float32 [1536, 8192], P('fsdp'), may hold values from -0.15625 to 0.15625
- proj_down: float32 [4096, 1536], P('fsdp'), may hold values from -0.09375 to 0.09375
- norm_gains: float32 [1536, 2], P('fsdp'), may hold values from 0.5 to 1.5
- first_qkv: float32 [1536, 3072], P('fsdp')
- first_out: float32 [1536, 1536], P('fsdp')
- first_up: float32 [1536, 8192], P('fsdp')
- first_down: float32 [4096, 1536], P('fsdp')
- first_gains: float32 [1536, 2], P('fsdp')
- second_qkv: float32 [1536, 3072], P('fsdp'), may hold values from 1724 to 6898
- second_out: float32 [1536, 1536], P('fsdp'), may hold values from 155 to 621
- second_up: float32 [1536, 8192], P('fsdp'), may hold values from 211 to 845
- second_down: float32 [4096, 1536], P('fsdp'), may hold values from 618 to 2473
- second_gains: float32 [1536, 2], P('fsdp'), may hold values from 2520 to 10082
Outputs:
- block_output: bfloat16 [32768, 1536], P('fsdp')
- input_grad: float32 [32768, 1536], P('fsdp')
- new_qkv: float32 [1536, 3072], P('fsdp')
- new_out: float32 [1536, 1536], P('fsdp')
- new_up: float32 [1536, 8192], P('fsdp')
- new_down: float32 [4096, 1536], P('fsdp')
- new_gains: float32 [1536, 2], P('fsdp')
- new_first_qkv: float32 [1536, 3072], P('fsdp')
- new_first_out: float32 [1536, 1536], P('fsdp')
- new_first_up: float32 [1536, 8192], P('fsdp')
- new_first_down: float32 [4096, 1536], P('fsdp')
- new_first_gains: float32 [1536, 2], P('fsdp')
- new_second_qkv: float32 [1536, 3072], P('fsdp')
- new_second_out: float32 [1536, 1536], P('fsdp')
- new_second_up: float32 [1536, 8192], P('fsdp')
- new_second_down: float32 [4096, 1536], P('fsdp')
- new_second_gains: float32 [1536, 2], P('fsdp')
The draws below stay inside these ranges and needn't reach their ends.
Inputs may be any that keep to these rules, and one draw needn't show every extreme that they name: `segment_ids`: within each sequence of 256 tokens the ids begin at 0, never fall and rise by one at each document start; documents have 256 // 4 to 191 tokens, save the last of a sequence, which the sequence's end may cut.
All inputs are finite; a program needn't handle non-finite values.
Results may differ from the reference program's by a relative error of at most 0.023.
Values may be sent and summed in bfloat16 or wider, within the bound.
A program may use at most 320 MiB of HBM per device.

```python
import math
import jax
import jax.numpy as jnp
from jax import lax

D = 1536
H = 16
KVH = 8
HD = 96
FF = 4096
TOK_DEV = 256
STEP = 10
TOKENS = 32768


def moment_draw(key, shape, level):
    spread = level * (1.0 - 0.9) / 0.9 * math.sqrt(TOKENS)
    return spread * jax.random.normal(key, shape, jnp.float32)


def draw_segment_ids(key, part):
    key = jax.random.fold_in(key, 7)
    shortest = max(1, TOK_DEV // 4)
    longest = max(shortest + 1, 3 * TOK_DEV // 4)
    slots = TOK_DEV // shortest + 1
    seq_count = TOKENS // TOK_DEV
    lengths = jax.random.randint(key, (seq_count, slots), shortest, longest, dtype=jnp.int32)
    chosen = jax.random.randint(jax.random.fold_in(key, 1), (), 0, seq_count, dtype=jnp.int32)
    chosen_rows = jnp.arange(seq_count, dtype=jnp.int32) == chosen
    first_three = jnp.arange(slots, dtype=jnp.int32) < 3
    lengths = jnp.where(jnp.logical_and(chosen_rows[:, None], first_three[None, :]), shortest, lengths)
    ends = jnp.cumsum(lengths, axis=1)
    places = jnp.arange(TOK_DEV, dtype=jnp.int32)
    segments = jnp.sum((ends[:, None, :] <= places[None, :, None]).astype(jnp.int32), axis=2)
    return segments.reshape(TOKENS)


def draw_first_qkv(key, part):
    key = jax.random.fold_in(key, 21)
    return moment_draw(key, (D, (H + 2 * KVH) * HD), 1.0)


def draw_first_out(key, part):
    key = jax.random.fold_in(key, 22)
    return moment_draw(key, (H * HD, D), 0.3)


def draw_first_up(key, part):
    key = jax.random.fold_in(key, 23)
    return moment_draw(key, (D, 2 * FF), 0.35)


def draw_first_down(key, part):
    key = jax.random.fold_in(key, 24)
    return moment_draw(key, (FF, D), 0.6)


def draw_first_gains(key, part):
    key = jax.random.fold_in(key, 25)
    return moment_draw(key, (D, 2), 1.2)


def with_spikes(values, stream_key, source, target, shards_of, factor):
    owner, partner = [(jnp.arange(values.shape[axis_at]) // (values.shape[axis_at] // shards_of)).reshape([-1 if axis == axis_at else 1 for axis in range(values.ndim)]) for axis_at in (source, target)]
    chosen = jax.random.permutation(stream_key, shards_of)[partner]
    strong = (owner == chosen) | (owner == (partner + shards_of // 2) % shards_of)
    return jnp.where(strong, factor * values, values)


def level_of(own_key, shape, split, smallest, high):
    level = 1.0
    for dim, blocks in split:
        draws = jax.random.uniform(jax.random.fold_in(jax.random.fold_in(own_key, 6), dim), (blocks,), jnp.float32, smallest / len(split), high / len(split))
        level = level * jnp.repeat(jnp.exp(draws), shape[dim] // blocks).reshape((-1,) + (1,) * (len(shape) - 1 - dim))
    return level


def normal_values(rng, shape, scale, reach, shards=(), kind=jnp.bfloat16):
    level = level_of(rng, shape, shards, -0.22, 0.18) if shards else 1.0
    values = jax.random.normal(rng, shape, jnp.float32) * scale * level
    return jnp.minimum(jnp.maximum(values, -reach), reach).astype(kind)


def gaussian_with(stream_key, shape, deviation, bound, cuts, heavy, kind=jnp.bfloat16):
    array = deviation * jax.random.normal(stream_key, shape, jnp.float32)
    if cuts:
        array = array * level_of(stream_key, shape, cuts, -0.22, 0.18)
    return jnp.clip(with_spikes(array, jax.random.fold_in(stream_key, 3), *heavy), -bound, bound).astype(kind)


def setup_inputs(seed: int = 0) -> dict:
    key_list = jax.random.split(jax.random.key(seed), 19)
    return {
        "tokens_in": gaussian_with(key_list[0], (TOKENS, D), 1.0, 24.0, ((0, 128),), (0, 1, 128, 5.5)),
        "cotangent": normal_values(key_list[1], (TOKENS, D), 1.0, 6.0, ((0, 128),)),
        "segment_ids": draw_segment_ids(jax.random.fold_in(key_list[18], 71), 0),
        "proj_qkv": normal_values(key_list[3], (D, (H + 2 * KVH) * HD), D ** -0.5, 0.15625, ((0, 128),), jnp.float32),
        "proj_out": normal_values(key_list[4], (H * HD, D), (H * HD // 16) ** -0.5, 0.625, ((0, 128),), jnp.float32),
        "proj_up": normal_values(key_list[5], (D, 2 * FF), D ** -0.5, 0.15625, ((0, 128),), jnp.float32),
        "proj_down": normal_values(key_list[6], (FF, D), FF ** -0.5, 0.09375, ((0, 128),), jnp.float32),
        "norm_gains": jnp.clip(1.0 + 0.1 * jax.random.normal(key_list[7], (D, 2), jnp.float32), 0.5, 1.5),
        "first_qkv": draw_first_qkv(jax.random.fold_in(key_list[18], 71), 0),
        "first_out": draw_first_out(jax.random.fold_in(key_list[18], 71), 0),
        "first_up": draw_first_up(jax.random.fold_in(key_list[18], 71), 0),
        "first_down": draw_first_down(jax.random.fold_in(key_list[18], 71), 0),
        "first_gains": draw_first_gains(jax.random.fold_in(key_list[18], 71), 0),
        "second_qkv": jnp.clip(jnp.exp(math.log(6898.0) - 1.3865843422731479 * jax.random.uniform(key_list[13], (D, (H + 2 * KVH) * HD), jnp.float32) ** level_of(key_list[13], (D, (H + 2 * KVH) * HD), ((0, 128),), -0.2, 0.2)), 1724.0, 6898.0),
        "second_out": jnp.clip(jnp.exp(math.log(621.0) - 1.387906 * jax.random.uniform(key_list[14], (H * HD, D), jnp.float32) ** level_of(key_list[14], (H * HD, D), ((0, 128),), -0.2, 0.2)), 155.0, 621.0),
        "second_up": jnp.clip(jnp.exp(math.log(845.0) - 1.3874785 * jax.random.uniform(key_list[15], (D, 2 * FF), jnp.float32) ** level_of(key_list[15], (D, 2 * FF), ((0, 128),), -0.2, 0.2)), 211.0, 845.0),
        "second_down": jnp.clip(jnp.exp(math.log(2473.0) - 1.3866988 * jax.random.uniform(key_list[16], (FF, D), jnp.float32) ** level_of(key_list[16], (FF, D), ((0, 128),), -0.2, 0.2)), 618.0, 2473.0),
        "second_gains": jnp.clip(jnp.exp(math.log(10082.0) - 1.38649275 * jax.random.uniform(key_list[17], (D, 2), jnp.float32) ** level_of(key_list[17], (D, 2), ((0, 128),), -0.2, 0.2)), 2520.0, 10082.0),
    }


@jax.custom_vjp
def low(v):
    return lax.optimization_barrier(v.astype(jnp.bfloat16)).astype(jnp.float32)

@jax.custom_vjp
def low_back(v):
    return v

def low_keep(v):
    return (low(v), None)

def low_pass(kept, grad):
    return (grad,)

def back_keep(v):
    return (v, None)

def back_low(kept, grad):
    return (low(grad),)
low.defvjp(low_keep, low_pass)
low_back.defvjp(back_keep, back_low)
EPSILON = 1e-05
THETA = 100000.0
BETA_ONE = 0.9
BETA_TWO = 0.95
ADAM_EPSILON = 1e-08
RATES = (0.08, 0.3, 0.08, 0.05, 1.0)
DECAYS = (0.1, 0.1, 0.1, 0.1, 0.0)
MASKED = -1e+30

def matmul(left, right):
    return jnp.dot(left, right, precision=lax.Precision.HIGHEST, preferred_element_type=jnp.float32)

def layout(segment_row):
    length = segment_row.shape[0]
    places = jnp.arange(length, dtype=jnp.int32)
    same_doc = segment_row[:, None] == segment_row[None, :]
    starts = lax.optimization_barrier(jnp.min(jnp.where(same_doc, places[None, :], length), axis=1))
    offsets = (places - starts).astype(jnp.float32)
    allowed = jnp.logical_and(same_doc, places[None, :] <= places[:, None])
    exponents = jnp.arange(0, HD, 2, dtype=jnp.float32) / HD
    angles = offsets[:, None] * (THETA ** (-exponents))[None, :]
    return (allowed, jnp.cos(angles), jnp.sin(angles))

def rotate(head_values, cos_table, sin_table):
    half_width = head_values.shape[-1] // 2
    front_half = head_values[..., :half_width]
    back_half = head_values[..., half_width:]
    cos_row = cos_table[:, None, :]
    sin_row = sin_table[:, None, :]
    return jnp.concatenate([front_half * cos_row - back_half * sin_row, back_half * cos_row + front_half * sin_row], axis=-1)

def normalize(values, gain_row):
    scaled = values * lax.rsqrt(lax.optimization_barrier(jnp.mean(values * values, axis=-1, keepdims=True)) + EPSILON)
    return scaled * gain_row

def forward_one(params, tokens, allowed, cos_table, sin_table):
    proj_qkv, proj_out, proj_up, proj_down, norm_gains = params
    gains_low = low(norm_gains)
    length = tokens.shape[0]
    normed_one = low(normalize(tokens, gains_low[:, 0]))
    mixed = matmul(normed_one, low(proj_qkv))
    queries = low_back(mixed[:, :H * HD]).reshape(length, H, HD)
    keys_raw = low_back(mixed[:, H * HD:(H + KVH) * HD]).reshape(length, KVH, HD)
    values = low_back(low(mixed[:, (H + KVH) * HD:])).reshape(length, KVH, HD)
    queries = low(rotate(queries, cos_table, sin_table)).reshape(length, KVH, H // KVH, HD)
    keys_rot = low(rotate(keys_raw, cos_table, sin_table))
    scores = jnp.einsum('skgd,tkd->kgst', queries, keys_rot, precision=lax.Precision.HIGHEST) * (1.0 / math.sqrt(HD))
    scores = jnp.where(allowed[None, None], low_back(scores), MASKED)
    row_max = lax.optimization_barrier(jnp.max(scores, axis=-1, keepdims=True))
    exponent = jnp.exp(scores - row_max)
    attention_weights = low(exponent / lax.optimization_barrier(jnp.sum(exponent, axis=-1, keepdims=True)))
    attended = jnp.einsum('kgst,tkd->skgd', attention_weights, values, precision=lax.Precision.HIGHEST)
    attended = low_back(low(attended.reshape(length, H * HD)))
    middle = tokens + low_back(matmul(attended, low(proj_out)))
    normed_two = low(normalize(middle, gains_low[:, 1]))
    gate_up = low_back(matmul(normed_two, low(proj_up)))
    hidden = low(jax.nn.silu(gate_up[:, :FF]) * gate_up[:, FF:])
    return middle + matmul(hidden, low(proj_down))

def adamw_step(weight, moment_one, moment_two, gradient, rate, decay):
    first_new = BETA_ONE * moment_one + (1.0 - BETA_ONE) * gradient
    second_new = BETA_TWO * moment_two + (1.0 - BETA_TWO) * gradient * gradient
    unbiased_one = first_new / (1.0 - BETA_ONE ** STEP)
    unbiased_two = second_new / (1.0 - BETA_TWO ** STEP)
    weight_new = weight - rate * (unbiased_one / (jnp.sqrt(unbiased_two) + ADAM_EPSILON) + decay * weight)
    return (weight_new, first_new, second_new)

def reference(tokens_in, cotangent, segment_ids, proj_qkv, proj_out, proj_up, proj_down, norm_gains, first_qkv, first_out, first_up, first_down, first_gains, second_qkv, second_out, second_up, second_down, second_gains):
    params = tuple((master.astype(jnp.float32) for master in (proj_qkv, proj_out, proj_up, proj_down, norm_gains)))
    seq_count = TOKENS // TOK_DEV
    group_size = math.gcd(seq_count, max(1, 4096 // TOK_DEV))
    scan_steps = seq_count // group_size
    token_blocks = tokens_in.astype(jnp.float32).reshape(scan_steps, group_size, TOK_DEV, D)
    cotangent_blocks = cotangent.astype(jnp.float32).reshape(scan_steps, group_size, TOK_DEV, D)
    segment_blocks = segment_ids.reshape(scan_steps, group_size, TOK_DEV)

    def visit_block(running, inputs):
        block_tokens, block_cotangent, block_segments = inputs
        allowed, cos_table, sin_table = jax.vmap(layout)(block_segments)

        def run_block(weights_in, tokens_block):
            return jax.vmap(forward_one, in_axes=(None, 0, 0, 0, 0))(weights_in, tokens_block, allowed, cos_table, sin_table)
        outputs, pullback = jax.vjp(run_block, params, block_tokens)
        param_grads, token_grads = pullback(block_cotangent)
        running = jax.tree.map(jnp.add, running, param_grads)
        return (running, (outputs.astype(jnp.bfloat16), token_grads))
    zero_grads = jax.tree.map(jnp.zeros_like, params)
    gradients, (outputs, token_grads) = lax.scan(visit_block, zero_grads, (token_blocks, cotangent_blocks, segment_blocks))
    firsts = (first_qkv, first_out, first_up, first_down, first_gains)
    seconds = (second_qkv, second_out, second_up, second_down, second_gains)
    updated = [adamw_step(params[number], firsts[number], seconds[number], gradients[number], RATES[number], DECAYS[number]) for number in range(5)]
    return (outputs.reshape(TOKENS, D), token_grads.reshape(TOKENS, D), updated[0][0], updated[1][0], updated[2][0], updated[3][0], updated[4][0], updated[0][1], updated[1][1], updated[2][1], updated[3][1], updated[4][1], updated[0][2], updated[1][2], updated[2][2], updated[3][2], updated[4][2])
```

```python
import functools
import math

import jax
import jax.numpy as jnp
from jax import lax
from jax.experimental import pallas as pl
from jax.experimental.pallas import tpu as pltpu
from jax.sharding import PartitionSpec as P

H = 16
KVH = 8
HD = 96
FF = 4096
STEP = 10
D = 1536
TOK = 256


EPSILON = 1e-05
THETA = 100000.0
BETA_ONE = 0.9
BETA_TWO = 0.95
ADAM_EPSILON = 1e-08
RATES = (0.08, 0.3, 0.08, 0.05, 1.0)
DECAYS = (0.1, 0.1, 0.1, 0.1, 0.0)
MASKED = -1e30

MESH = pl.DeviceIdType.MESH
BF16 = jnp.bfloat16
F32 = jnp.float32
MIB = 1024 * 1024

CUBE = ("xb", "xa", "zb", "za", "yb", "ya")
LINKS = ("xa", "xb", "za", "zb", "ya", "yb")
QUAD_LINKS = ("xa", "xb", "za", "zb", "yb")
GRAY = (0, 1, 3, 2)


class Place:
    def __init__(self):
        me = lax.axis_index("fsdp")
        self.me = me
        self.c = lax.rem(me, 2)
        self.y = lax.rem(me // 2, 4)
        self.z = lax.rem(me // 8, 4)
        self.x = me // 32
        self.bit = {"c": self.c}
        for name in "xyz":
            at = getattr(self, name)
            self.bit[name + "b"] = at // 2
            self.bit[name + "a"] = lax.rem(at + at // 2, 2)

    def partner(self, *dims):
        at = {"x": self.x, "y": self.y, "z": self.z, "c": self.c}
        for dim in dims:
            name = dim[0]
            if dim == "c":
                at["c"] = 1 - at["c"]
            elif dim[1] == "a":
                at[name] = at[name] + 1 - 2 * lax.rem(at[name], 2)
            else:
                at[name] = 3 - at[name]
        return ((at["x"] * 4 + at["z"]) * 4 + at["y"]) * 2 + at["c"]


def greet(devices):
    barrier = pltpu.get_barrier_semaphore()
    for device in devices:
        pl.semaphore_signal(barrier, inc=1, device_id=(device,), device_id_type=MESH)
    pl.semaphore_wait(barrier, len(devices))


class Sems:
    def __init__(self, send, recv):
        self.send, self.recv, self.used = send, recv, 0

    def copy(self, src, dst, device):
        at = self.used
        self.used += 1
        return pltpu.make_async_remote_copy(
            src_ref=src,
            dst_ref=dst,
            send_sem=self.send.at[at],
            recv_sem=self.recv.at[at],
            device_id=(device,),
            device_id_type=MESH,
        )


def spot(place, dims, done=(), flip=None):
    return tuple(
        pl.ds(0, 2) if dim in done else (1 - place.bit[dim] if dim == flip else place.bit[dim])
        for dim in dims
    )


def rotated(links, by):
    return links[by:] + links[:by]


ATT_PARTS = tuple(
    ((0, 48), (start * 128, count * 128), by)
    for by, start, count in ((0, 0, 1), (1, 1, 1), (2, 2, 2), (3, 4, 2), (4, 6, 1), (5, 7, 2))
)
GAIN_PARTS = (((0, 16), (0, 128), 0),)
UP_PARTS = tuple(
    ((start * 16, count * 16), (0, 512), by)
    for by, start, count in ((0, 0, 3), (1, 3, 3), (2, 6, 2), (3, 8, 2), (4, 10, 2))
)
DOWN_PARTS = tuple(
    ((0, 32), (start * 128, count * 128), by)
    for by, start, count in ((0, 0, 2), (1, 2, 2), (2, 4, 2), (3, 6, 3), (4, 9, 3))
)


def cut(part):
    rows, columns, _ = part
    return (pl.ds(*rows), pl.ds(*columns))


class Gather:
    def __init__(self, place, sems, ref, dims, links, part, forward=False):
        self.place, self.sems, self.ref, self.dims = place, sems, ref, dims
        self.order, self.part = rotated(links, part[2]), part
        self.forward, self.copies, self.others = forward, [], []

    def pass_on(self, index):
        if self.forward:
            view = self.ref.at[index + cut(self.part)]
            copy = self.sems.copy(view, view, self.place.partner("c"))
            copy.start()
            self.others.append(copy)

    def step(self, number):
        if number == 0:
            self.pass_on(spot(self.place, self.dims))
        else:
            self.copies[number - 1].wait_recv()
        if number < len(self.order):
            done = self.order[:number]
            view = self.ref.at[spot(self.place, self.dims, done) + cut(self.part)]
            copy = self.sems.copy(view, view, self.place.partner(self.order[number]))
            copy.start()
            self.copies.append(copy)
        if number > 0:
            link = self.order[number - 1]
            self.pass_on(spot(self.place, self.dims, self.order[: number - 1], flip=link))

    def end(self):
        for copy in self.copies:
            copy.wait_send()
        for copy in self.others:
            copy.wait()


def gather_kernel(att_in, gain_in, up_in, down_in, att, gain, up, down, send, recv, local):
    place = Place()
    sems = Sems(send, recv)
    quad = {(0, 1): place.partner("c"), (1, 0): place.partner("ya"), (1, 1): place.partner("ya", "c")}
    greet([place.partner(link) for link in LINKS] + [quad[0, 1], quad[1, 1]])
    dims7 = CUBE + ("c",)
    dims5 = CUBE[:5]
    home7 = spot(place, dims7)
    home5 = spot(place, dims5)
    ya, c = place.bit["ya"], place.c
    own_rows = (2 * ya + c) * 48
    mine = pl.ds(pl.multiple_of(own_rows, 16), 48)
    starts = [
        pltpu.make_async_copy(att_in, att.at[home7], local.at[0]),
        pltpu.make_async_copy(gain_in, gain.at[home7], local.at[1]),
        pltpu.make_async_copy(down_in, down.at[home5], local.at[2]),
        pltpu.make_async_copy(up_in.at[2 * ya + c], up.at[home5 + (mine,)], local.at[3]),
    ]
    for copy in starts:
        copy.start()
    scatter = []
    for (dya, dc), device in quad.items():
        to_ya = 1 - ya if dya else ya
        to_c = 1 - c if dc else c
        copy = sems.copy(up_in.at[2 * to_ya + to_c], up.at[home5 + (mine,)], device)
        copy.start()
        scatter.append(copy)
    for copy in starts:
        copy.wait()
    first = [Gather(place, sems, gain, dims7, LINKS, part, True) for part in GAIN_PARTS]
    first += [Gather(place, sems, att, dims7, LINKS, part, True) for part in ATT_PARTS]
    second = [Gather(place, sems, down, dims5, QUAD_LINKS, part) for part in DOWN_PARTS]
    second += [Gather(place, sems, up, dims5, QUAD_LINKS, part) for part in UP_PARTS]
    for number in range(7):
        for job in first:
            job.step(number)
        if number == 0:
            for copy in scatter:
                copy.wait()
        if number < 6:
            for job in second:
                job.step(number)
    for job in first + second:
        job.end()


def quad_gather_kernel(n2, dy, n2_all, dy_all, send, recv, local):
    place = Place()
    sems = Sems(send, recv)
    sibling, across = place.partner("c"), place.partner("ya")
    greet([sibling, across])
    ya, c = place.bit["ya"], place.c
    copies = []
    for number, (src, dst) in enumerate(((n2, n2_all), (dy, dy_all))):
        far = sems.copy(src, dst.at[ya, c], across)
        far.start()
        near = sems.copy(src, dst.at[ya, c], sibling)
        near.start()
        own = pltpu.make_async_copy(src, dst.at[ya, c], local.at[number])
        own.start()
        copies.append((far, near, own, dst))
    for far, near, own, dst in copies:
        far.wait_recv()
        onward = sems.copy(dst.at[1 - ya, c], dst.at[1 - ya, c], sibling)
        onward.start()
        far.wait_send()
        near.wait()
        own.wait()
        onward.wait()


def add_rows(total, terms, rows=256, step=64):
    @pl.loop(0, rows // step)
    def _(i):
        at = pl.ds(pl.multiple_of(i * step, step), step)
        value = terms[0][at, :].astype(F32)
        for term in terms[1:]:
            value = value + term[at, :].astype(F32)
        total[at, :] = value.astype(total.dtype)


def quad_reduce_kernel(y, dn, y_sum, dn_sum, mixed, got, send, recv):
    place = Place()
    sems = Sems(send, recv)
    sibling, across = place.partner("c"), place.partner("ya")
    greet([sibling, across])
    ya, c = place.bit["ya"], place.c
    work = []
    for number, part in enumerate((y, dn)):
        away = sems.copy(part.at[1 - ya, 1 - c], got.at[number, 0], sibling)
        away.start()
        near = sems.copy(part.at[ya, 1 - c], got.at[number, 1], sibling)
        near.start()
        work.append((away, near))
    far = []
    for number, part in enumerate((y, dn)):
        work[number][0].wait_recv()
        add_rows(mixed.at[number], [part.at[1 - ya, c], got.at[number, 0]])
        copy = sems.copy(mixed.at[number], got.at[number, 2], across)
        copy.start()
        far.append(copy)
    for number, (part, total) in enumerate(((y, y_sum), (dn, dn_sum))):
        work[number][1].wait_recv()
        far[number].wait_recv()
        add_rows(total, [part.at[ya, c], got.at[number, 1], got.at[number, 2]])
        work[number][0].wait_send()
        work[number][1].wait_send()
        far[number].wait_send()


def each_block(place, dims, free, visit):
    count = 2 ** len(free)

    def at(i):
        index = []
        weight = count
        for dim in dims:
            if dim in free:
                weight //= 2
                index.append(lax.rem(i // weight, 2))
            else:
                index.append(place.bit[dim])
        return tuple(index)

    @pl.loop(0, count)
    def _(i):
        visit(at(i))


class Scatter:
    def __init__(self, place, sems, ref, got, dims, links, part, extra=()):
        self.place, self.sems, self.ref, self.got = place, sems, ref, got
        self.dims, self.part, self.extra = dims, part, extra
        self.order = tuple(reversed(rotated(links, part[2])))
        self.copies = []

    def add(self, number):
        link = self.order[number]
        free = self.order[number + 1 :]
        flip = self.dims.index(link)

        def visit(index):
            other = index[:flip] + (1 - index[flip],) + index[flip + 1 :]
            own = index + self.extra + cut(self.part)
            value = self.ref[own].astype(F32) + self.got[other + cut(self.part)].astype(F32)
            self.ref[own] = value.astype(BF16)

        each_block(self.place, self.dims, free, visit)

    def step(self, number):
        if number > 0:
            self.copies[number - 1].wait_recv()
            self.add(number - 1)
        if number < len(self.order):
            link = self.order[number]
            free = self.order[number + 1 :]
            src = self.ref.at[
                spot(self.place, self.dims, free, flip=link) + self.extra + cut(self.part)
            ]
            dst = self.got.at[spot(self.place, self.dims, free) + cut(self.part)]
            copy = self.sems.copy(src, dst, self.place.partner(link))
            copy.start()
            self.copies.append(copy)

    def end(self):
        for copy in self.copies:
            copy.wait_send()


def scatter_kernel(
    att_in, gain_in, up_in, down_in, att_out, gain_out, up_out, down_out,
    att, gain, up, down, att_side, gain_side, att_got, gain_got, up_got, down_got, up_land,
    send, recv, local,
):
    place = Place()
    sems = Sems(send, recv)
    quad = {(0, 1): place.partner("c"), (1, 0): place.partner("ya"), (1, 1): place.partner("ya", "c")}
    greet([place.partner(link) for link in LINKS] + [quad[0, 1], quad[1, 1]])
    ya, c = place.bit["ya"], place.c
    starts = [
        pltpu.make_async_copy(src, dst, local.at[number])
        for number, (src, dst) in enumerate(
            ((att_in, att), (gain_in, gain), (up_in, up), (down_in, down))
        )
    ]
    for copy in starts:
        copy.start()
    for copy in starts:
        copy.wait()
    whole = (pl.ds(0, 2),) * 6
    dims5 = CUBE[:5]
    second = [Scatter(place, sems, down, down_got, dims5, QUAD_LINKS, part) for part in DOWN_PARTS]
    second += [Scatter(place, sems, up, up_got, dims5, QUAD_LINKS, part) for part in UP_PARTS]
    sides = []
    for ref, side, parts in ((gain, gain_side, GAIN_PARTS), (att, att_side, ATT_PARTS)):
        for part in parts:
            copy = sems.copy(
                ref.at[whole + (1 - c,) + cut(part)], side.at[whole + cut(part)], place.partner("c")
            )
            copy.start()
            sides.append((copy, ref, side, part))
    for job in second:
        job.step(0)
    for copy, ref, side, part in sides:
        copy.wait_recv()

        def visit(index, ref=ref, side=side, part=part):
            own = index + (c,) + cut(part)
            value = ref[own].astype(F32) + side[index + cut(part)].astype(F32)
            ref[own] = value.astype(BF16)

        each_block(place, CUBE, CUBE, visit)
    first = [Scatter(place, sems, gain, gain_got, CUBE, LINKS, part, (c,)) for part in GAIN_PARTS]
    first += [Scatter(place, sems, att, att_got, CUBE, LINKS, part, (c,)) for part in ATT_PARTS]
    for number in range(7):
        for job in first:
            job.step(number)
        if 0 < number < 6:
            for job in second:
                job.step(number)
    home5 = spot(place, dims5)
    home6 = spot(place, CUBE)
    last = []
    for (dya, dc), device in quad.items():
        to_ya = 1 - ya if dya else ya
        to_c = 1 - c if dc else c
        rows = pl.ds(pl.multiple_of((2 * to_ya + to_c) * 48, 16), 48)
        copy = sems.copy(up.at[home5 + (rows,)], up_land.at[2 * ya + c], device)
        copy.start()
        last.append(copy)
    att_out[...] = att[home6 + (c,)].astype(F32)
    gain_out[...] = gain[home6 + (c,)].astype(F32)
    down_out[...] = down[home5].astype(F32)
    own = pl.ds(pl.multiple_of((2 * ya + c) * 48, 16), 48)
    up_out[2 * ya + c] = up[home5 + (own,)].astype(F32)
    for copy in last:
        copy.wait()
    for dya, dc in quad:
        to = 2 * (1 - ya if dya else ya) + (1 - c if dc else c)
        up_out[to] = up_land[to].astype(F32)
    for job in first + second:
        job.end()
    for copy, *_ in sides:
        copy.wait_send()


ANY = pl.BlockSpec(memory_space=pl.ANY)
VMEM = pl.BlockSpec(memory_space=pltpu.VMEM)
TWO5 = (2,) * 5
TWO6 = (2,) * 6
TWO7 = (2,) * 7


def shape(dims, kind=BF16):
    return jax.ShapeDtypeStruct(dims, kind)


def params(number, mib=56):
    return pltpu.CompilerParams(
        collective_id=number, has_side_effects=True, vmem_limit_bytes=mib * MIB
    )


def dma(count):
    return pltpu.SemaphoreType.DMA((count,))


def gather_weights(att, gain, up, down):
    return pl.pallas_call(
        gather_kernel,
        name="gather_weights",
        out_shape=(
            shape(TWO7 + (48, 1152)),
            shape(TWO7 + (16, 128)),
            shape(TWO5 + (192, 512)),
            shape(TWO5 + (32, 1536)),
        ),
        in_specs=[ANY] * 4,
        out_specs=[ANY] * 4,
        scratch_shapes=[dma(160), dma(160), dma(4)],
        compiler_params=params(0, 8),
    )(att, gain, up, down)


def quad_gather(n2, dy):
    return pl.pallas_call(
        quad_gather_kernel,
        name="quad_gather",
        out_shape=(shape((2, 2, TOK, D)), shape((2, 2, TOK, D))),
        in_specs=[ANY] * 2,
        out_specs=[ANY] * 2,
        scratch_shapes=[dma(6), dma(6), dma(2)],
        compiler_params=params(1, 8),
    )(n2, dy)


def quad_reduce(y, dn):
    return pl.pallas_call(
        quad_reduce_kernel,
        name="quad_reduce",
        out_shape=(shape((TOK, D), F32), shape((TOK, D), F32)),
        in_specs=[VMEM] * 2,
        out_specs=[VMEM] * 2,
        scratch_shapes=[
            pltpu.VMEM((2, TOK, D), BF16),
            pltpu.VMEM((2, 3, TOK, D), BF16),
            dma(6),
            dma(6),
        ],
        compiler_params=params(2),
    )(y, dn)


def scatter_grads(att, gain, up, down):
    return pl.pallas_call(
        scatter_kernel,
        name="scatter_grads",
        out_shape=(
            shape((48, 1152), F32),
            shape((16, 128), F32),
            shape((4, 48, 512), F32),
            shape((32, 1536), F32),
        ),
        in_specs=[ANY] * 4,
        out_specs=[VMEM] * 4,
        scratch_shapes=[
            pltpu.VMEM(TWO7 + (48, 1152), BF16),
            pltpu.VMEM(TWO7 + (16, 128), BF16),
            pltpu.VMEM(TWO5 + (192, 512), BF16),
            pltpu.VMEM(TWO5 + (32, 1536), BF16),
            pltpu.VMEM(TWO6 + (48, 1152), BF16),
            pltpu.VMEM(TWO6 + (16, 128), BF16),
            pltpu.VMEM(TWO6 + (48, 1152), BF16),
            pltpu.VMEM(TWO6 + (16, 128), BF16),
            pltpu.VMEM(TWO5 + (192, 512), BF16),
            pltpu.VMEM(TWO5 + (32, 1536), BF16),
            pltpu.VMEM((4, 48, 512), BF16),
            dma(120),
            dma(120),
            dma(4),
        ],
        compiler_params=params(3, 60),
    )(att, gain, up, down)


def gray(array, axes):
    for axis in axes:
        pieces = jnp.split(array, 4, axis=axis)
        array = jnp.concatenate([pieces[at] for at in GRAY], axis=axis)
    return array


def fold(weight, lead=()):
    columns = weight.shape[-1] // 4
    parts = [weight[..., at * columns : (at + 1) * columns] for at in range(4)]
    return jnp.concatenate(parts, axis=-2)


def unfold(block):
    parts = [block[..., at * 12 : (at + 1) * 12, :] for at in range(4)]
    return jnp.concatenate(parts, axis=-1)


def rank_columns(up):
    split = gray(up.reshape(12, 2, 4, 4, 4, 2, 32), (2, 3, 4)).reshape(12, 2, 4, 4, 2, 2, 2, 32)
    return split.transpose(5, 6, 0, 1, 2, 3, 4, 7).reshape(4, 12, 2048)


def natural_columns(pieces):
    split = pieces.reshape(2, 2, 12, 2, 4, 4, 2, 32).transpose(2, 3, 4, 5, 6, 0, 1, 7)
    return gray(split.reshape(12, 2, 4, 4, 4, 2, 32), (2, 3, 4)).reshape(12, 8192)


def open_rows(gathered, columns):
    split = gray(gathered.reshape(4, 4, 4, 2, 48, columns // 4), (0, 1, 2))
    split = split.reshape(128, 4, 12, columns // 4).transpose(0, 2, 1, 3)
    return split.reshape(1536, columns)


def close_rows(grad):
    columns = grad.shape[1] // 4
    split = grad.reshape(128, 12, 4, columns).transpose(0, 2, 1, 3)
    return gray(split.reshape(4, 4, 4, 2, 48, columns), (0, 1, 2)).reshape(128, 48, columns)


def layout(segment_row):
    length = segment_row.shape[0]
    places = jnp.arange(length, dtype=jnp.int32)
    same_doc = segment_row[:, None] == segment_row[None, :]
    starts = jnp.min(jnp.where(same_doc, places[None, :], length), axis=1)
    offsets = (places - starts).astype(jnp.float32)
    allowed = jnp.logical_and(same_doc, places[None, :] <= places[:, None])
    exponents = jnp.arange(0, HD, 2, dtype=jnp.float32) / HD
    angles = offsets[:, None] * (THETA ** (-exponents))[None, :]
    return (allowed, jnp.cos(angles), jnp.sin(angles))


def rotate(head_values, cos_table, sin_table):
    half_width = head_values.shape[-1] // 2
    front_half = head_values[..., :half_width]
    back_half = head_values[..., half_width:]
    cos_row = cos_table[:, None, :]
    sin_row = sin_table[:, None, :]
    return jnp.concatenate(
        [front_half * cos_row - back_half * sin_row, back_half * cos_row + front_half * sin_row],
        axis=-1,
    )


def unrotate(head_grads, cos_table, sin_table):
    return rotate(head_grads, cos_table, -sin_table)


def norm_parts(values):
    inverse = lax.rsqrt(jnp.mean(values * values, axis=-1, keepdims=True) + EPSILON)
    return (values * inverse, inverse)


def norm_back(grad_scaled, scaled, inverse):
    return inverse * (grad_scaled - scaled * jnp.mean(scaled * grad_scaled, axis=-1, keepdims=True))


def product(left, right):
    return jnp.dot(left, right, preferred_element_type=jnp.float32)


def left_product(left, right):
    return lax.dot_general(
        left, right, (((0,), (0,)), ((), ())), preferred_element_type=jnp.float32
    )


def right_product(left, right):
    return lax.dot_general(
        left, right, (((1,), (1,)), ((), ())), preferred_element_type=jnp.float32
    )


def masked_scores(queries, keys_rot, allowed):
    raw = jnp.einsum("skgd,tkd->kgst", queries, keys_rot, preferred_element_type=jnp.float32) * (
        1.0 / math.sqrt(HD)
    )
    return jnp.where(allowed[None, None], raw, MASKED)


def adamw_step(weight, moment_one, moment_two, gradient, rate, decay):
    first_new = BETA_ONE * moment_one + (1.0 - BETA_ONE) * gradient
    second_new = BETA_TWO * moment_two + (1.0 - BETA_TWO) * gradient * gradient
    unbiased_one = first_new / (1.0 - BETA_ONE**STEP)
    unbiased_two = second_new / (1.0 - BETA_TWO**STEP)
    weight_new = weight - rate * (
        unbiased_one / (jnp.sqrt(unbiased_two) + ADAM_EPSILON) + decay * weight
    )
    return (weight_new, first_new, second_new)


def body(
    tokens_in,
    cotangent,
    segment_ids,
    proj_qkv,
    proj_out,
    proj_up,
    proj_down,
    norm_gains,
    first_qkv,
    first_out,
    first_up,
    first_down,
    first_gains,
    second_qkv,
    second_out,
    second_up,
    second_down,
    second_gains,
):
    masters = (proj_qkv, proj_out, proj_up, proj_down, norm_gains)
    low_qkv, low_out, low_up, low_down, low_gains = (part.astype(BF16) for part in masters)
    att_block = jnp.concatenate([fold(low_qkv), fold(low_out)], axis=1)
    gain_block = jnp.pad(low_gains.T, ((0, 14), (0, 116)))
    up_blocks = fold(rank_columns(low_up))
    att_all, gain_all, up_all, down_all = gather_weights(att_block, gain_block, up_blocks, low_down)
    att_all = att_all.reshape(128, 48, 1152)
    full_qkv = open_rows(att_all[:, :, :768], 3072)
    full_out = open_rows(att_all[:, :, 768:], 1536)
    rank_up = open_rows(up_all.reshape(128, 48, 512), 2048)
    rank_down = down_all.reshape(1024, 1536)
    gains = gray(gain_all.reshape(4, 4, 4, 2, 16, 128), (0, 1, 2)).reshape(128, 16, 128)
    gain_one = gains[:, 0, :12].reshape(1536).astype(F32)
    gain_two = gains[:, 1, :12].reshape(1536).astype(F32)

    length = tokens_in.shape[0]
    group_size = H // KVH
    scale_factor = 1.0 / math.sqrt(HD)
    allowed, cos_table, sin_table = layout(segment_ids)
    tokens = tokens_in.astype(F32)
    scaled_one, inverse_one = norm_parts(tokens)
    normed_one = (scaled_one * gain_one).astype(BF16)
    mixed = product(normed_one, full_qkv)
    queries = rotate(mixed[:, : H * HD].reshape(length, H, HD), cos_table, sin_table)
    queries = queries.astype(BF16).reshape(length, KVH, group_size, HD)
    keys_rot = rotate(
        mixed[:, H * HD : (H + KVH) * HD].reshape(length, KVH, HD), cos_table, sin_table
    ).astype(BF16)
    values = mixed[:, (H + KVH) * HD :].astype(BF16).reshape(length, KVH, HD)
    scores = masked_scores(queries, keys_rot, allowed)
    row_max = jnp.max(scores, axis=-1, keepdims=True)
    exponent = jnp.exp(scores - row_max)
    row_total = jnp.sum(exponent, axis=-1, keepdims=True)
    log_total = row_max + jnp.log(row_total)
    attended = jnp.einsum(
        "kgst,tkd->skgd",
        (exponent / row_total).astype(BF16),
        values,
        preferred_element_type=F32,
    )
    attended = attended.reshape(length, H * HD).astype(BF16)
    middle = tokens + product(attended, full_out)
    scaled_two, inverse_two = norm_parts(middle)
    normed_two = (scaled_two * gain_two).astype(BF16)

    n2_all, dy_all = quad_gather(normed_two, cotangent)
    n2_all = n2_all.reshape(4 * TOK, D)
    dy_all = dy_all.reshape(4 * TOK, D)
    gate_up = product(n2_all, rank_up)
    gate_part = gate_up[:, : FF // 4]
    up_part = gate_up[:, FF // 4 :]
    sigmoid_gate = jax.nn.sigmoid(gate_part)
    silu_gate = gate_part * sigmoid_gate
    hidden = (silu_gate * up_part).astype(BF16)
    y_part = product(hidden, rank_down).astype(BF16)
    grad_down = left_product(hidden, dy_all)
    grad_hidden = right_product(dy_all, rank_down)
    grad_gate = grad_hidden * up_part * sigmoid_gate * (1.0 + gate_part * (1.0 - sigmoid_gate))
    grad_upward = grad_hidden * silu_gate
    grad_gate_up = jnp.concatenate([grad_gate, grad_upward], axis=1).astype(BF16)
    grad_up = left_product(n2_all, grad_gate_up)
    dn2_part = right_product(grad_gate_up, rank_up).astype(BF16)
    y_sum, grad_normed_two = quad_reduce(
        y_part.reshape(2, 2, TOK, D), dn2_part.reshape(2, 2, TOK, D)
    )
    block_output = (middle + y_sum).astype(BF16)

    grad_gain_two = jnp.sum(grad_normed_two * scaled_two, axis=0)
    grad_middle = cotangent.astype(F32) + norm_back(
        grad_normed_two * gain_two, scaled_two, inverse_two
    )
    grad_middle_low = grad_middle.astype(BF16)
    grad_out = left_product(attended, grad_middle_low)
    grad_attended = (
        right_product(grad_middle_low, full_out)
        .astype(BF16)
        .reshape(length, KVH, group_size, HD)
    )
    scores = masked_scores(queries, keys_rot, allowed)
    attention_weights = jnp.exp(scores - log_total)
    weights_low = attention_weights.astype(BF16)
    grad_values = jnp.einsum(
        "kgst,skgd->tkd", weights_low, grad_attended, preferred_element_type=F32
    )
    grad_weights = jnp.einsum(
        "skgd,tkd->kgst", grad_attended, values, preferred_element_type=F32
    )
    grad_scores = attention_weights * (
        grad_weights - jnp.sum(attention_weights * grad_weights, axis=-1, keepdims=True)
    )
    grad_scores = grad_scores.astype(BF16)
    grad_queries = (
        jnp.einsum("kgst,tkd->skgd", grad_scores, keys_rot, preferred_element_type=F32)
        * scale_factor
    )
    grad_keys = (
        jnp.einsum("kgst,skgd->tkd", grad_scores, queries, preferred_element_type=F32)
        * scale_factor
    )
    grad_mixed = jnp.concatenate(
        [
            unrotate(grad_queries.reshape(length, H, HD), cos_table, sin_table).reshape(
                length, H * HD
            ),
            unrotate(grad_keys, cos_table, sin_table).reshape(length, KVH * HD),
            grad_values.reshape(length, KVH * HD),
        ],
        axis=1,
    ).astype(BF16)
    grad_qkv = left_product(normed_one, grad_mixed)
    grad_normed_one = right_product(grad_mixed, full_qkv)
    grad_gain_one = jnp.sum(grad_normed_one * scaled_one, axis=0)
    input_grad = grad_middle + norm_back(grad_normed_one * gain_one, scaled_one, inverse_one)

    att_grad = jnp.concatenate(
        [close_rows(grad_qkv.astype(BF16)), close_rows(grad_out.astype(BF16))], axis=2
    )
    gain_grad = jnp.stack([grad_gain_one, grad_gain_two], axis=0).astype(BF16)
    gain_grad = gain_grad.reshape(2, 128, 12).transpose(1, 0, 2)
    gain_grad = gray(gain_grad.reshape(4, 4, 4, 2, 2, 12), (0, 1, 2)).reshape(128, 2, 12)
    gain_grad = jnp.pad(gain_grad, ((0, 0), (0, 14), (0, 116)))
    up_grad = close_rows(grad_up.astype(BF16)).reshape(32, 192, 512)
    att_sum, gain_sum, up_sum, down_sum = scatter_grads(
        att_grad.reshape(TWO7 + (48, 1152)),
        gain_grad.reshape(TWO7 + (16, 128)),
        up_grad.reshape(TWO5 + (192, 512)),
        grad_down.astype(BF16).reshape(TWO5 + (32, 1536)),
    )
    shard_grads = (
        unfold(att_sum[:, :768]),
        unfold(att_sum[:, 768:]),
        natural_columns(unfold(up_sum)),
        down_sum,
        gain_sum[:2, :12].T,
    )
    firsts = (first_qkv, first_out, first_up, first_down, first_gains)
    seconds = (second_qkv, second_out, second_up, second_down, second_gains)
    updated = [
        adamw_step(
            masters[number],
            firsts[number],
            seconds[number],
            shard_grads[number],
            RATES[number],
            DECAYS[number],
        )
        for number in range(5)
    ]
    return (
        block_output,
        input_grad,
        *(update[0] for update in updated),
        *(update[1] for update in updated),
        *(update[2] for update in updated),
    )


def solution(mesh):
    rows = P("fsdp", None)
    return jax.shard_map(
        body,
        mesh=mesh,
        in_specs=(rows, rows, P("fsdp")) + (rows,) * 15,
        out_specs=(rows,) * 17,
        check_vma=False,
    )
```

```python
import functools
import math

import jax
import jax.numpy as jnp
import numpy as np
from jax import lax
from jax.experimental import pallas as pl
from jax.experimental.pallas import tpu as pltpu
from jax.sharding import PartitionSpec as P

H = 16
KVH = 8
HD = 96
FF = 4096
STEP = 10
D = 1536
TOK = 256


EPSILON = 1e-05
THETA = 100000.0
BETA_ONE = 0.9
BETA_TWO = 0.95
ADAM_EPSILON = 1e-08
RATES = (0.08, 0.3, 0.08, 0.05, 1.0)
DECAYS = (0.1, 0.1, 0.1, 0.1, 0.0)
MASKED = -1e30

MESH = pl.DeviceIdType.MESH
BF16 = jnp.bfloat16
F32 = jnp.float32
MIB = 1024 * 1024

CUBE = ("xb", "xa", "zb", "za", "yb", "ya")
LINKS = ("xa", "xb", "za", "zb", "ya", "yb")
QUAD_LINKS = ("xa", "xb", "za", "zb", "yb")
GRAY = (0, 1, 3, 2)


class Place:
    def __init__(self):
        me = lax.axis_index("fsdp")
        self.me = me
        self.c = lax.rem(me, 2)
        self.y = lax.rem(me // 2, 4)
        self.z = lax.rem(me // 8, 4)
        self.x = me // 32
        self.bit = {"c": self.c}
        for name in "xyz":
            at = getattr(self, name)
            self.bit[name + "b"] = at // 2
            self.bit[name + "a"] = lax.rem(at + at // 2, 2)

    def partner(self, *dims):
        at = {"x": self.x, "y": self.y, "z": self.z, "c": self.c}
        for dim in dims:
            name = dim[0]
            if dim == "c":
                at["c"] = 1 - at["c"]
            elif dim[1] == "a":
                at[name] = at[name] + 1 - 2 * lax.rem(at[name], 2)
            else:
                at[name] = 3 - at[name]
        return ((at["x"] * 4 + at["z"]) * 4 + at["y"]) * 2 + at["c"]


def greet(devices):
    barrier = pltpu.get_barrier_semaphore()
    for device in devices:
        pl.semaphore_signal(barrier, inc=1, device_id=(device,), device_id_type=MESH)
    pl.semaphore_wait(barrier, len(devices))


class Sems:
    def __init__(self, send, recv):
        self.send, self.recv, self.used = send, recv, 0

    def copy(self, src, dst, device):
        at = self.used
        self.used += 1
        return pltpu.make_async_remote_copy(
            src_ref=src,
            dst_ref=dst,
            send_sem=self.send.at[at],
            recv_sem=self.recv.at[at],
            device_id=(device,),
            device_id_type=MESH,
        )


def spot(place, dims, done=(), flip=None):
    return tuple(
        pl.ds(0, 2) if dim in done else (1 - place.bit[dim] if dim == flip else place.bit[dim])
        for dim in dims
    )


def rotated(links, by):
    return links[by:] + links[:by]


ATT_PARTS = tuple(
    ((0, 48), (start * 128, count * 128), by)
    for by, start, count in ((0, 0, 1), (1, 1, 1), (2, 2, 2), (3, 4, 2), (4, 6, 1), (5, 7, 2))
)
GAIN_PARTS = (((0, 16), (0, 128), 0),)
UP_PARTS = tuple(
    ((start * 16, count * 16), (0, 512), by)
    for by, start, count in ((0, 0, 3), (1, 3, 3), (2, 6, 2), (3, 8, 2), (4, 10, 2))
)
DOWN_PARTS = tuple(
    ((0, 32), (start * 128, count * 128), by)
    for by, start, count in ((0, 0, 2), (1, 2, 2), (2, 4, 2), (3, 6, 3), (4, 9, 3))
)


def cut(part):
    rows, columns, _ = part
    return (pl.ds(*rows), pl.ds(*columns))


class Gather:
    def __init__(self, place, sems, ref, dims, links, part, forward=False):
        self.place, self.sems, self.ref, self.dims = place, sems, ref, dims
        self.order, self.part = rotated(links, part[2]), part
        self.forward, self.copies, self.others = forward, [], []

    def pass_on(self, index):
        if self.forward:
            view = self.ref.at[index + cut(self.part)]
            copy = self.sems.copy(view, view, self.place.partner("c"))
            copy.start()
            self.others.append(copy)

    def step(self, number):
        if number == 0:
            self.pass_on(spot(self.place, self.dims))
        else:
            self.copies[number - 1].wait_recv()
        if number < len(self.order):
            done = self.order[:number]
            view = self.ref.at[spot(self.place, self.dims, done) + cut(self.part)]
            copy = self.sems.copy(view, view, self.place.partner(self.order[number]))
            copy.start()
            self.copies.append(copy)
        if number > 0:
            link = self.order[number - 1]
            self.pass_on(spot(self.place, self.dims, self.order[: number - 1], flip=link))

    def end(self):
        for copy in self.copies:
            copy.wait_send()
        for copy in self.others:
            copy.wait()


def gather_kernel(att_in, gain_in, up_in, down_in, att, gain, up, down, send, recv, local):
    place = Place()
    sems = Sems(send, recv)
    quad = {(0, 1): place.partner("c"), (1, 0): place.partner("ya"), (1, 1): place.partner("ya", "c")}
    greet([place.partner(link) for link in LINKS] + [quad[0, 1], quad[1, 1]])
    dims7 = CUBE + ("c",)
    dims5 = CUBE[:5]
    home7 = spot(place, dims7)
    home5 = spot(place, dims5)
    ya, c = place.bit["ya"], place.c
    own_rows = (2 * ya + c) * 48
    mine = pl.ds(pl.multiple_of(own_rows, 16), 48)
    starts = [
        pltpu.make_async_copy(att_in, att.at[home7], local.at[0]),
        pltpu.make_async_copy(gain_in, gain.at[home7], local.at[1]),
        pltpu.make_async_copy(down_in, down.at[home5], local.at[2]),
        pltpu.make_async_copy(up_in.at[2 * ya + c], up.at[home5 + (mine,)], local.at[3]),
    ]
    for copy in starts:
        copy.start()
    scatter = []
    for (dya, dc), device in quad.items():
        to_ya = 1 - ya if dya else ya
        to_c = 1 - c if dc else c
        copy = sems.copy(up_in.at[2 * to_ya + to_c], up.at[home5 + (mine,)], device)
        copy.start()
        scatter.append(copy)
    for copy in starts:
        copy.wait()
    first = [Gather(place, sems, gain, dims7, LINKS, part, True) for part in GAIN_PARTS]
    first += [Gather(place, sems, att, dims7, LINKS, part, True) for part in ATT_PARTS]
    second = [Gather(place, sems, down, dims5, QUAD_LINKS, part) for part in DOWN_PARTS]
    second += [Gather(place, sems, up, dims5, QUAD_LINKS, part) for part in UP_PARTS]
    for number in range(7):
        for job in first:
            job.step(number)
        if number == 0:
            for copy in scatter:
                copy.wait()
        if number < 6:
            for job in second:
                job.step(number)
    for job in first + second:
        job.end()


def quad_gather_kernel(n2, dy, n2_all, dy_all, send, recv, local):
    place = Place()
    sems = Sems(send, recv)
    sibling, across = place.partner("c"), place.partner("ya")
    greet([sibling, across])
    ya, c = place.bit["ya"], place.c
    copies = []
    for number, (src, dst) in enumerate(((n2, n2_all), (dy, dy_all))):
        far = sems.copy(src, dst.at[ya, c], across)
        far.start()
        near = sems.copy(src, dst.at[ya, c], sibling)
        near.start()
        own = pltpu.make_async_copy(src, dst.at[ya, c], local.at[number])
        own.start()
        copies.append((far, near, own, dst))
    for far, near, own, dst in copies:
        far.wait_recv()
        onward = sems.copy(dst.at[1 - ya, c], dst.at[1 - ya, c], sibling)
        onward.start()
        far.wait_send()
        near.wait()
        own.wait()
        onward.wait()


def add_rows(total, terms, rows=256, step=64):
    @pl.loop(0, rows // step)
    def _(i):
        at = pl.ds(pl.multiple_of(i * step, step), step)
        value = terms[0][at, :].astype(F32)
        for term in terms[1:]:
            value = value + term[at, :].astype(F32)
        total[at, :] = value.astype(total.dtype)


def quad_reduce_kernel(y, dn, y_sum, dn_sum, mixed, got, send, recv):
    place = Place()
    sems = Sems(send, recv)
    sibling, across = place.partner("c"), place.partner("ya")
    greet([sibling, across])
    ya, c = place.bit["ya"], place.c
    work = []
    for number, part in enumerate((y, dn)):
        away = sems.copy(part.at[1 - ya, 1 - c], got.at[number, 0], sibling)
        away.start()
        near = sems.copy(part.at[ya, 1 - c], got.at[number, 1], sibling)
        near.start()
        work.append((away, near))
    far = []
    for number, part in enumerate((y, dn)):
        work[number][0].wait_recv()
        add_rows(mixed.at[number], [part.at[1 - ya, c], got.at[number, 0]])
        copy = sems.copy(mixed.at[number], got.at[number, 2], across)
        copy.start()
        far.append(copy)
    for number, (part, total) in enumerate(((y, y_sum), (dn, dn_sum))):
        work[number][1].wait_recv()
        far[number].wait_recv()
        add_rows(total, [part.at[ya, c], got.at[number, 1], got.at[number, 2]])
        work[number][0].wait_send()
        work[number][1].wait_send()
        far[number].wait_send()


def each_block(place, dims, free, visit):
    count = 2 ** len(free)

    def at(i):
        index = []
        weight = count
        for dim in dims:
            if dim in free:
                weight //= 2
                index.append(lax.rem(i // weight, 2))
            else:
                index.append(place.bit[dim])
        return tuple(index)

    @pl.loop(0, count)
    def _(i):
        visit(at(i))


class Scatter:
    def __init__(self, place, sems, ref, got, dims, links, part, extra=()):
        self.place, self.sems, self.ref, self.got = place, sems, ref, got
        self.dims, self.part, self.extra = dims, part, extra
        self.order = tuple(reversed(rotated(links, part[2])))
        self.copies = []

    def add(self, number):
        link = self.order[number]
        free = self.order[number + 1 :]
        flip = self.dims.index(link)

        def visit(index):
            other = index[:flip] + (1 - index[flip],) + index[flip + 1 :]
            own = index + self.extra + cut(self.part)
            value = self.ref[own].astype(F32) + self.got[other + cut(self.part)].astype(F32)
            self.ref[own] = value.astype(BF16)

        each_block(self.place, self.dims, free, visit)

    def step(self, number):
        if number > 0:
            self.copies[number - 1].wait_recv()
            self.add(number - 1)
        if number < len(self.order):
            link = self.order[number]
            free = self.order[number + 1 :]
            src = self.ref.at[
                spot(self.place, self.dims, free, flip=link) + self.extra + cut(self.part)
            ]
            dst = self.got.at[spot(self.place, self.dims, free) + cut(self.part)]
            copy = self.sems.copy(src, dst, self.place.partner(link))
            copy.start()
            self.copies.append(copy)

    def end(self):
        for copy in self.copies:
            copy.wait_send()


def scatter_kernel(
    att_in, gain_in, up_in, down_in, att_out, gain_out, up_out, down_out,
    att, gain, up, down, att_side, gain_side, att_got, gain_got, up_got, down_got, up_land,
    send, recv, local,
):
    place = Place()
    sems = Sems(send, recv)
    quad = {(0, 1): place.partner("c"), (1, 0): place.partner("ya"), (1, 1): place.partner("ya", "c")}
    greet([place.partner(link) for link in LINKS] + [quad[0, 1], quad[1, 1]])
    ya, c = place.bit["ya"], place.c
    starts = [
        pltpu.make_async_copy(src, dst, local.at[number])
        for number, (src, dst) in enumerate(
            ((att_in, att), (gain_in, gain), (up_in, up), (down_in, down))
        )
    ]
    for copy in starts:
        copy.start()
    for copy in starts:
        copy.wait()
    whole = (pl.ds(0, 2),) * 6
    dims5 = CUBE[:5]
    second = [Scatter(place, sems, down, down_got, dims5, QUAD_LINKS, part) for part in DOWN_PARTS]
    second += [Scatter(place, sems, up, up_got, dims5, QUAD_LINKS, part) for part in UP_PARTS]
    sides = []
    for ref, side, parts in ((gain, gain_side, GAIN_PARTS), (att, att_side, ATT_PARTS)):
        for part in parts:
            copy = sems.copy(
                ref.at[whole + (1 - c,) + cut(part)], side.at[whole + cut(part)], place.partner("c")
            )
            copy.start()
            sides.append((copy, ref, side, part))
    for job in second:
        job.step(0)
    for copy, ref, side, part in sides:
        copy.wait_recv()

        def visit(index, ref=ref, side=side, part=part):
            own = index + (c,) + cut(part)
            value = ref[own].astype(F32) + side[index + cut(part)].astype(F32)
            ref[own] = value.astype(BF16)

        each_block(place, CUBE, CUBE, visit)
    first = [Scatter(place, sems, gain, gain_got, CUBE, LINKS, part, (c,)) for part in GAIN_PARTS]
    first += [Scatter(place, sems, att, att_got, CUBE, LINKS, part, (c,)) for part in ATT_PARTS]
    for number in range(7):
        for job in first:
            job.step(number)
        if 0 < number < 6:
            for job in second:
                job.step(number)
    home5 = spot(place, dims5)
    home6 = spot(place, CUBE)
    last = []
    for (dya, dc), device in quad.items():
        to_ya = 1 - ya if dya else ya
        to_c = 1 - c if dc else c
        rows = pl.ds(pl.multiple_of((2 * to_ya + to_c) * 48, 16), 48)
        copy = sems.copy(up.at[home5 + (rows,)], up_land.at[2 * ya + c], device)
        copy.start()
        last.append(copy)
    att_out[...] = att[home6 + (c,)].astype(F32)
    gain_out[...] = gain[home6 + (c,)].astype(F32)
    down_out[...] = down[home5].astype(F32)
    own = pl.ds(pl.multiple_of((2 * ya + c) * 48, 16), 48)
    up_out[2 * ya + c] = up[home5 + (own,)].astype(F32)
    for copy in last:
        copy.wait()
    for dya, dc in quad:
        to = 2 * (1 - ya if dya else ya) + (1 - c if dc else c)
        up_out[to] = up_land[to].astype(F32)
    for job in first + second:
        job.end()
    for copy, *_ in sides:
        copy.wait_send()


ANY = pl.BlockSpec(memory_space=pl.ANY)
VMEM = pl.BlockSpec(memory_space=pltpu.VMEM)
TWO5 = (2,) * 5
TWO6 = (2,) * 6
TWO7 = (2,) * 7


def shape(dims, kind=BF16):
    return jax.ShapeDtypeStruct(dims, kind)


def params(number, mib=56):
    return pltpu.CompilerParams(
        collective_id=number, has_side_effects=True, vmem_limit_bytes=mib * MIB
    )


def dma(count):
    return pltpu.SemaphoreType.DMA((count,))


def gather_weights(att, gain, up, down):
    return pl.pallas_call(
        gather_kernel,
        name="gather_weights",
        out_shape=(
            shape(TWO7 + (48, 1152)),
            shape(TWO7 + (16, 128)),
            shape(TWO5 + (192, 512)),
            shape(TWO5 + (32, 1536)),
        ),
        in_specs=[ANY] * 4,
        out_specs=[ANY] * 4,
        scratch_shapes=[dma(160), dma(160), dma(4)],
        compiler_params=params(0, 8),
    )(att, gain, up, down)


def quad_gather(n2, dy):
    return pl.pallas_call(
        quad_gather_kernel,
        name="quad_gather",
        out_shape=(shape((2, 2, TOK, D)), shape((2, 2, TOK, D))),
        in_specs=[ANY] * 2,
        out_specs=[ANY] * 2,
        scratch_shapes=[dma(6), dma(6), dma(2)],
        compiler_params=params(1, 8),
    )(n2, dy)


def quad_reduce(y, dn):
    return pl.pallas_call(
        quad_reduce_kernel,
        name="quad_reduce",
        out_shape=(shape((TOK, D), F32), shape((TOK, D), F32)),
        in_specs=[VMEM] * 2,
        out_specs=[VMEM] * 2,
        scratch_shapes=[
            pltpu.VMEM((2, TOK, D), BF16),
            pltpu.VMEM((2, 3, TOK, D), BF16),
            dma(6),
            dma(6),
        ],
        compiler_params=params(2),
    )(y, dn)


def scatter_grads(att, gain, up, down):
    return pl.pallas_call(
        scatter_kernel,
        name="scatter_grads",
        out_shape=(
            shape((48, 1152), F32),
            shape((16, 128), F32),
            shape((4, 48, 512), F32),
            shape((32, 1536), F32),
        ),
        in_specs=[ANY] * 4,
        out_specs=[VMEM] * 4,
        scratch_shapes=[
            pltpu.VMEM(TWO7 + (48, 1152), BF16),
            pltpu.VMEM(TWO7 + (16, 128), BF16),
            pltpu.VMEM(TWO5 + (192, 512), BF16),
            pltpu.VMEM(TWO5 + (32, 1536), BF16),
            pltpu.VMEM(TWO6 + (48, 1152), BF16),
            pltpu.VMEM(TWO6 + (16, 128), BF16),
            pltpu.VMEM(TWO6 + (48, 1152), BF16),
            pltpu.VMEM(TWO6 + (16, 128), BF16),
            pltpu.VMEM(TWO5 + (192, 512), BF16),
            pltpu.VMEM(TWO5 + (32, 1536), BF16),
            pltpu.VMEM((4, 48, 512), BF16),
            dma(120),
            dma(120),
            dma(4),
        ],
        compiler_params=params(3, 60),
    )(att, gain, up, down)


def natural_group(g):
    xb, xa = lax.rem(g // 16, 2), lax.rem(g // 8, 2)
    zb, za = lax.rem(g // 4, 2), lax.rem(g // 2, 2)
    yb = lax.rem(g, 2)
    x = 2 * xb + lax.rem(xa + xb, 2)
    z = 2 * zb + lax.rem(za + zb, 2)
    return (xb, xa, zb, za, yb), (x * 4 + z) * 2 + yb


def dot(left, right):
    return lax.dot_general(left, right, (((1,), (0,)), ((), ())), preferred_element_type=F32)


def dot_t(left, right):
    return lax.dot_general(left, right, (((1,), (1,)), ((), ())), preferred_element_type=F32)


def cols(i, width):
    return pl.ds(pl.multiple_of(i * width, width), width)


def stream_groups(fetch, use):
    fetch(0).start()

    @pl.loop(0, 32)
    def _(g):
        @pl.when(g + 1 < 32)
        def _():
            fetch(g + 1).start()

        fetch(g).wait()
        use(g)


def head_pad(value, spread):
    high = value.astype(BF16)
    low = (value - high.astype(F32)).astype(BF16)
    return dot(high, spread) + dot(low, spread)


def turn(value, cos, sin):
    return value * cos + pltpu.roll(value, 64, 1) * sin


def mask_bias(seg_col, seg_row):
    rows = lax.broadcasted_iota(jnp.int32, (TOK, TOK), 0)
    columns = lax.broadcasted_iota(jnp.int32, (TOK, TOK), 1)
    allowed = jnp.logical_and(seg_col == seg_row, columns <= rows)
    return jnp.where(allowed, 0.0, MASKED).astype(F32)


def row_norm(value):
    return lax.rsqrt(jnp.mean(value * value, axis=-1, keepdims=True) + EPSILON)


def each_rows(step, visit, rows=TOK):
    @pl.loop(0, rows // step)
    def _(i):
        visit(pl.ds(pl.multiple_of(i * step, step), step))


def forward_kernel(
    att_in, gain_in, up_in, down_in, x, dy, seg_col, seg_row, cos, sin, perm, spread, pick, owner,
    att, gain, up, down, wq_out, wo_out, wgu_out, n2_out, dy_all, q_out, a_out, n1_out, m_out, g_out, zgu_out,
    wq, wo, wgu, att_stage, up_stage, gain_stage, gains, n1, q, apad, a, m, n2_all, zgu, bias,
    send, recv, local, group_sem, out_sem,
):
    place = Place()
    sems = Sems(send, recv)
    sibling, across = place.partner("c"), place.partner("ya")
    quad = {(0, 1): sibling, (1, 0): across, (1, 1): place.partner("ya", "c")}
    greet([place.partner(link) for link in LINKS] + [quad[0, 1], quad[1, 1]])
    dims7 = CUBE + ("c",)
    dims5 = CUBE[:5]
    home7 = spot(place, dims7)
    home5 = spot(place, dims5)
    ya, c = place.bit["ya"], place.c
    mine = pl.ds(pl.multiple_of((2 * ya + c) * 48, 16), 48)
    starts = [
        pltpu.make_async_copy(att_in, att.at[home7], local.at[0]),
        pltpu.make_async_copy(gain_in, gain.at[home7], local.at[1]),
        pltpu.make_async_copy(down_in, down.at[home5], local.at[2]),
        pltpu.make_async_copy(up_in.at[2 * ya + c], up.at[home5 + (mine,)], local.at[3]),
        pltpu.make_async_copy(dy, dy_all.at[ya, c], local.at[4]),
    ]
    for copy in starts:
        copy.start()
    scatter = []
    for (dya, dc), device in quad.items():
        to_ya = 1 - ya if dya else ya
        to_c = 1 - c if dc else c
        copy = sems.copy(up_in.at[2 * to_ya + to_c], up.at[home5 + (mine,)], device)
        copy.start()
        scatter.append(copy)
    for copy in starts:
        copy.wait()
    first = [Gather(place, sems, gain, dims7, LINKS, part, True) for part in GAIN_PARTS]
    first += [Gather(place, sems, att, dims7, LINKS, part, True) for part in ATT_PARTS]
    second = [Gather(place, sems, down, dims5, QUAD_LINKS, part) for part in DOWN_PARTS]
    second += [Gather(place, sems, up, dims5, QUAD_LINKS, part) for part in UP_PARTS]
    for number in range(7):
        for job in first:
            job.step(number)
        if number == 0:
            bias[...] = mask_bias(seg_col[...], seg_row[...])
            for copy in scatter:
                copy.wait()
        if number >= 2:
            for job in second:
                job.step(number - 2)
    dy_near = sems.copy(dy_all.at[ya, c], dy_all.at[ya, c], sibling)
    dy_near.start()
    dy_far = sems.copy(dy_all.at[ya, c], dy_all.at[ya, c], across)
    for job in first:
        job.end()

    outs = []

    def put(src, dst):
        copy = pltpu.make_async_copy(src, dst, out_sem.at[len(outs)])
        copy.start()
        outs.append(copy)

    gain_copy = pltpu.make_async_copy(gain, gain_stage, local.at[0])
    gain_copy.start()

    def fetch_att(g):
        bits, _ = natural_group(g)
        slot = lax.rem(g, 2)
        return pltpu.make_async_copy(att.at[bits], att_stage.at[slot], group_sem.at[slot])

    def use_att(g):
        bits, n = natural_group(g)
        block = att_stage[lax.rem(g, 2)].reshape(192, 1152)
        order = perm[bits[4]]
        rows = pl.ds(pl.multiple_of(n * 48, 16), 48)
        qkv = dot(order, block[:, :768]).astype(BF16)
        for at in range(4):
            wq[at // 2, rows, (at % 2) * 768 : (at % 2 + 1) * 768] = qkv[48 * at : 48 * at + 48]
        out = dot(order, block[:, 768:]).astype(BF16)
        for at in range(4):
            wo[rows, 384 * at : 384 * at + 384] = out[48 * at : 48 * at + 48]

    stream_groups(fetch_att, use_att)
    put(wq, wq_out)
    put(wo, wo_out)
    gain_copy.wait()
    tiles = gain_stage[...].reshape(128, 16, 128).astype(F32)
    lines = lax.broadcasted_iota(jnp.int32, (128, 16, 128), 1)
    for number in range(2):
        line = jnp.sum(jnp.where(lines == number, tiles, 0.0), axis=1).astype(BF16)
        vector = jnp.sum(dot(line, pick[...]) * owner[...].astype(F32), axis=0, keepdims=True)
        gains[number : number + 1, :] = vector
    gains[2:8, :] = jnp.zeros((6, D), F32)

    def norm_one(at):
        value = x[at, :].astype(F32)
        n1[at, :] = (value * row_norm(value) * gains[0:1, :]).astype(BF16)

    each_rows(64, norm_one)

    def heads(i, rotated_too):
        value = dot(n1[...], wq[i // 4, :, cols(lax.rem(i, 4), 384)])
        padded = head_pad(value, spread[...])
        for at in range(4):
            head = padded[:, 128 * at : 128 * at + 128]
            if rotated_too:
                head = turn(head, cos[...], sin[...])
            lanes = pl.ds(pl.multiple_of(lax.rem(i, 2) * 512 + 128 * at, 128), 128)
            q[cols(i // 2, 256), lanes] = head.astype(BF16)

    pl.loop(0, 6)(lambda i: heads(i, True))
    pl.loop(6, 8)(lambda i: heads(i, False))
    put(q, q_out)

    @pl.loop(0, 8)
    def _(j):
        pair = q[cols(j // 4, 256), cols(lax.rem(j, 4), 256)]
        key = q[512:768, cols(j, 128)]
        value = q[768:1024, cols(j, 128)]
        for at in range(2):
            scores = dot_t(pair[:, 128 * at : 128 * at + 128], key) * (1.0 / math.sqrt(HD))
            scores = scores + bias[...]
            exponent = jnp.exp(scores - jnp.max(scores, axis=-1, keepdims=True))
            weights = exponent / jnp.sum(exponent, axis=-1, keepdims=True)
            lanes = pl.ds(pl.multiple_of(j * 256 + 128 * at, 128), 128)
            apad[:, lanes] = dot(weights.astype(BF16), value).astype(BF16)

    @pl.loop(0, 4)
    def _(i):
        a[:, cols(i, 384)] = dot_t(apad[:, cols(i, 512)], spread[...]).astype(BF16)

    @pl.loop(0, 3)
    def _(i):
        m[:, cols(i, 512)] = x[:, cols(i, 512)].astype(F32) + dot(a[...], wo[:, cols(i, 512)])

    own = n2_all.at[ya, c]

    def norm_two(at):
        value = m[at, :]
        own[at, :] = (value * row_norm(value) * gains[1:2, :]).astype(BF16)

    each_rows(64, norm_two)
    near = sems.copy(own, own, sibling)
    near.start()
    far = sems.copy(own, own, across)
    far.start()
    dy_far.start()
    put(n1, n1_out)
    put(a, a_out)
    put(m, m_out)
    put(gains, g_out)

    for job in second:
        job.step(5)

    def fetch_up(g):
        bits, _ = natural_group(g)
        slot = lax.rem(g, 2)
        return pltpu.make_async_copy(up.at[bits], up_stage.at[slot], group_sem.at[slot])

    def use_up(g):
        bits, n = natural_group(g)
        rows = pl.ds(pl.multiple_of(n * 48, 16), 48)
        block = dot(perm[bits[4]], up_stage[lax.rem(g, 2)]).astype(BF16)
        for at in range(4):
            wgu[rows, 512 * at : 512 * at + 512] = block[48 * at : 48 * at + 48]

    stream_groups(fetch_up, use_up)
    put(wgu, wgu_out)

    def mlp(pair):
        rows = pl.ds(pl.multiple_of(512 * pair, 512), 512)

        @pl.loop(0, 4)
        def _(i):
            left = n2_all[pair].reshape(512, D)
            gate = dot(left, wgu[:, cols(i, 256)])
            upward = dot(left, wgu[:, cols(i + 4, 256)])
            hidden = gate * (1.0 / (1.0 + jnp.exp(-gate))) * upward
            zgu[0, rows, cols(i, 256)] = hidden.astype(BF16)
            zgu[1, rows, cols(i, 256)] = gate.astype(BF16)
            zgu[2, rows, cols(i, 256)] = upward.astype(BF16)

        put(zgu.at[:, rows], zgu_out.at[:, rows])

    near.wait_recv()
    mlp(ya)
    far.wait_recv()
    onward = sems.copy(n2_all.at[1 - ya, c], n2_all.at[1 - ya, c], sibling)
    onward.start()
    dy_far.wait_recv()
    dy_onward = sems.copy(dy_all.at[1 - ya, c], dy_all.at[1 - ya, c], sibling)
    dy_onward.start()
    onward.wait_recv()
    mlp(1 - ya)
    put(n2_all, n2_out)
    near.wait_send()
    far.wait_send()
    onward.wait_send()
    dy_near.wait()
    dy_far.wait_send()
    dy_onward.wait()
    for job in second:
        job.end()
    for copy in outs:
        copy.wait()


def forward(att, gain, up, down, x, dy, seg_col, seg_row, cos, sin, perm, spread, pick, owner):
    return pl.pallas_call(
        forward_kernel,
        name="forward",
        out_shape=(
            shape(TWO7 + (48, 1152)),
            shape(TWO7 + (16, 128)),
            shape(TWO5 + (192, 512)),
            shape(TWO5 + (32, 1536)),
            shape((2, D, D)),
            shape((D, D)),
            shape((D, 2048)),
            shape((2, 2, TOK, D)),
            shape((2, 2, TOK, D)),
            shape((1024, 1024)),
            shape((TOK, D)),
            shape((TOK, D)),
            shape((TOK, D), F32),
            shape((8, D), F32),
            shape((3, 1024, 1024)),
        ),
        in_specs=[ANY] * 4 + [VMEM, ANY] + [VMEM] * 8,
        out_specs=[ANY] * 15,
        scratch_shapes=[
            pltpu.VMEM((2, D, D), BF16),
            pltpu.VMEM((D, D), BF16),
            pltpu.VMEM((D, 2048), BF16),
            pltpu.VMEM((2, 2, 2, 48, 1152), BF16),
            pltpu.VMEM((2, 192, 512), BF16),
            pltpu.VMEM(TWO7 + (16, 128), BF16),
            pltpu.VMEM((8, D), F32),
            pltpu.VMEM((TOK, D), BF16),
            pltpu.VMEM((1024, 1024), BF16),
            pltpu.VMEM((TOK, 2048), BF16),
            pltpu.VMEM((TOK, D), BF16),
            pltpu.VMEM((TOK, D), F32),
            pltpu.VMEM((2, 2, TOK, D), BF16),
            pltpu.VMEM((3, 1024, 1024), BF16),
            pltpu.VMEM((TOK, TOK), F32),
            dma(170),
            dma(170),
            dma(5),
            dma(2),
            dma(16),
        ],
        compiler_params=params(0, 60),
    )(att, gain, up, down, x, dy, seg_col, seg_row, cos, sin, perm, spread, pick, owner)


def tables():
    perm = np.zeros((2, 192, 192), np.float32)
    for yb in range(2):
        for spot_ya in range(2):
            for core in range(2):
                at = 2 * spot_ya + core
                to = 2 * (1 - spot_ya if yb else spot_ya) + core
                for quarter in range(4):
                    for row in range(12):
                        perm[yb, quarter * 48 + to * 12 + row, at * 48 + quarter * 12 + row] = 1
    spread = np.zeros((384, 512), np.float32)
    for head in range(4):
        for lane in range(96):
            spread[head * 96 + lane, head * 128 + lane + (16 if lane >= 48 else 0)] = 1
    pick = np.zeros((128, D), np.float32)
    pick[np.arange(D) % 12, np.arange(D)] = 1
    owner = np.zeros((128, D), np.float32)
    order = np.array(GRAY)
    for gx in range(4):
        for gz in range(4):
            for gy in range(4):
                for core in range(2):
                    at = ((gx * 4 + gz) * 4 + gy) * 2 + core
                    device = ((order[gx] * 4 + order[gz]) * 4 + order[gy]) * 2 + core
                    owner[at, device * 12 : device * 12 + 12] = 1
    return [jnp.asarray(table, BF16) for table in (perm, spread, pick, owner)]


def padded_tables(cos_table, sin_table):
    gap = jnp.zeros((TOK, 16), F32)
    cos = jnp.concatenate([cos_table, gap, cos_table, gap], axis=1)
    sin = jnp.concatenate([-sin_table, gap, sin_table, gap], axis=1)
    return cos, sin


def gray(array, axes):
    for axis in axes:
        pieces = jnp.split(array, 4, axis=axis)
        array = jnp.concatenate([pieces[at] for at in GRAY], axis=axis)
    return array


def fold(weight, lead=()):
    columns = weight.shape[-1] // 4
    parts = [weight[..., at * columns : (at + 1) * columns] for at in range(4)]
    return jnp.concatenate(parts, axis=-2)


def unfold(block):
    parts = [block[..., at * 12 : (at + 1) * 12, :] for at in range(4)]
    return jnp.concatenate(parts, axis=-1)


def rank_columns(up):
    split = gray(up.reshape(12, 2, 4, 4, 4, 2, 32), (2, 3, 4)).reshape(12, 2, 4, 4, 2, 2, 2, 32)
    return split.transpose(5, 6, 0, 1, 2, 3, 4, 7).reshape(4, 12, 2048)


def natural_columns(pieces):
    split = pieces.reshape(2, 2, 12, 2, 4, 4, 2, 32).transpose(2, 3, 4, 5, 6, 0, 1, 7)
    return gray(split.reshape(12, 2, 4, 4, 4, 2, 32), (2, 3, 4)).reshape(12, 8192)


def open_rows(gathered, columns):
    split = gray(gathered.reshape(4, 4, 4, 2, 48, columns // 4), (0, 1, 2))
    split = split.reshape(128, 4, 12, columns // 4).transpose(0, 2, 1, 3)
    return split.reshape(1536, columns)


def close_rows(grad):
    columns = grad.shape[1] // 4
    split = grad.reshape(128, 12, 4, columns).transpose(0, 2, 1, 3)
    return gray(split.reshape(4, 4, 4, 2, 48, columns), (0, 1, 2)).reshape(128, 48, columns)


def layout(segment_row):
    length = segment_row.shape[0]
    places = jnp.arange(length, dtype=jnp.int32)
    same_doc = segment_row[:, None] == segment_row[None, :]
    starts = jnp.min(jnp.where(same_doc, places[None, :], length), axis=1)
    offsets = (places - starts).astype(jnp.float32)
    allowed = jnp.logical_and(same_doc, places[None, :] <= places[:, None])
    exponents = jnp.arange(0, HD, 2, dtype=jnp.float32) / HD
    angles = offsets[:, None] * (THETA ** (-exponents))[None, :]
    return (allowed, jnp.cos(angles), jnp.sin(angles))


def rotate(head_values, cos_table, sin_table):
    half_width = head_values.shape[-1] // 2
    front_half = head_values[..., :half_width]
    back_half = head_values[..., half_width:]
    cos_row = cos_table[:, None, :]
    sin_row = sin_table[:, None, :]
    return jnp.concatenate(
        [front_half * cos_row - back_half * sin_row, back_half * cos_row + front_half * sin_row],
        axis=-1,
    )


def unrotate(head_grads, cos_table, sin_table):
    return rotate(head_grads, cos_table, -sin_table)


def norm_parts(values):
    inverse = lax.rsqrt(jnp.mean(values * values, axis=-1, keepdims=True) + EPSILON)
    return (values * inverse, inverse)


def norm_back(grad_scaled, scaled, inverse):
    return inverse * (grad_scaled - scaled * jnp.mean(scaled * grad_scaled, axis=-1, keepdims=True))


def product(left, right):
    return jnp.dot(left, right, preferred_element_type=jnp.float32)


def left_product(left, right):
    return lax.dot_general(
        left, right, (((0,), (0,)), ((), ())), preferred_element_type=jnp.float32
    )


def right_product(left, right):
    return lax.dot_general(
        left, right, (((1,), (1,)), ((), ())), preferred_element_type=jnp.float32
    )


def masked_scores(queries, keys_rot, allowed):
    raw = jnp.einsum("skgd,tkd->kgst", queries, keys_rot, preferred_element_type=jnp.float32) * (
        1.0 / math.sqrt(HD)
    )
    return jnp.where(allowed[None, None], raw, MASKED)


def adamw_step(weight, moment_one, moment_two, gradient, rate, decay):
    first_new = BETA_ONE * moment_one + (1.0 - BETA_ONE) * gradient
    second_new = BETA_TWO * moment_two + (1.0 - BETA_TWO) * gradient * gradient
    unbiased_one = first_new / (1.0 - BETA_ONE**STEP)
    unbiased_two = second_new / (1.0 - BETA_TWO**STEP)
    weight_new = weight - rate * (
        unbiased_one / (jnp.sqrt(unbiased_two) + ADAM_EPSILON) + decay * weight
    )
    return (weight_new, first_new, second_new)


def body(
    tokens_in,
    cotangent,
    segment_ids,
    proj_qkv,
    proj_out,
    proj_up,
    proj_down,
    norm_gains,
    first_qkv,
    first_out,
    first_up,
    first_down,
    first_gains,
    second_qkv,
    second_out,
    second_up,
    second_down,
    second_gains,
):
    masters = (proj_qkv, proj_out, proj_up, proj_down, norm_gains)
    low_qkv, low_out, low_up, low_down, low_gains = (part.astype(BF16) for part in masters)
    att_block = jnp.concatenate([fold(low_qkv), fold(low_out)], axis=1)
    gain_block = jnp.pad(low_gains.T, ((0, 14), (0, 116)))
    up_blocks = fold(rank_columns(low_up))
    allowed, cos_table, sin_table = layout(segment_ids)
    cos, sin = padded_tables(cos_table, sin_table)
    perm, spread, pick, owner = tables()
    (
        _, _, _, down_all, wq_halves, full_out, rank_up, n2_all, dy_all, heads, attended, normed_one, middle,
        gains, zgu,
    ) = forward(
        att_block, gain_block, up_blocks, low_down, tokens_in, cotangent, segment_ids.reshape(TOK, 1),
        segment_ids.reshape(1, TOK), cos, sin, perm, spread, pick, owner,
    )
    full_qkv = jnp.concatenate([wq_halves[0], wq_halves[1]], axis=1)
    rank_down = down_all.reshape(1024, 1536)
    gain_one, gain_two = gains[0], gains[1]

    length = tokens_in.shape[0]
    group_size = H // KVH
    scale_factor = 1.0 / math.sqrt(HD)
    tokens = tokens_in.astype(F32)
    scaled_one, inverse_one = norm_parts(tokens)
    scaled_two, inverse_two = norm_parts(middle)
    heads = heads.reshape(4, 256, 8, 128).transpose(0, 2, 1, 3).reshape(32, 256, 128)
    heads = jnp.concatenate([heads[:, :, :48], heads[:, :, 64:112]], axis=2).transpose(1, 0, 2)
    queries = heads[:, :16].reshape(length, KVH, group_size, HD)
    keys_rot = heads[:, 16:24]
    values = heads[:, 24:]
    scores = masked_scores(queries, keys_rot, allowed)
    row_max = jnp.max(scores, axis=-1, keepdims=True)
    log_total = row_max + jnp.log(jnp.sum(jnp.exp(scores - row_max), axis=-1, keepdims=True))
    n2_all = n2_all.reshape(4 * TOK, D)
    dy_all = dy_all.reshape(4 * TOK, D)
    hidden = zgu[0]
    gate_part = zgu[1].astype(F32)
    up_part = zgu[2].astype(F32)
    sigmoid_gate = jax.nn.sigmoid(gate_part)
    silu_gate = gate_part * sigmoid_gate
    y_part = product(hidden, rank_down).astype(BF16)
    grad_down = left_product(hidden, dy_all)
    grad_hidden = right_product(dy_all, rank_down)
    grad_gate = grad_hidden * up_part * sigmoid_gate * (1.0 + gate_part * (1.0 - sigmoid_gate))
    grad_upward = grad_hidden * silu_gate
    grad_gate_up = jnp.concatenate([grad_gate, grad_upward], axis=1).astype(BF16)
    grad_up = left_product(n2_all, grad_gate_up)
    dn2_part = right_product(grad_gate_up, rank_up).astype(BF16)
    y_sum, grad_normed_two = quad_reduce(
        y_part.reshape(2, 2, TOK, D), dn2_part.reshape(2, 2, TOK, D)
    )
    block_output = (middle + y_sum).astype(BF16)

    grad_gain_two = jnp.sum(grad_normed_two * scaled_two, axis=0)
    grad_middle = cotangent.astype(F32) + norm_back(
        grad_normed_two * gain_two, scaled_two, inverse_two
    )
    grad_middle_low = grad_middle.astype(BF16)
    grad_out = left_product(attended, grad_middle_low)
    grad_attended = (
        right_product(grad_middle_low, full_out)
        .astype(BF16)
        .reshape(length, KVH, group_size, HD)
    )
    scores = masked_scores(queries, keys_rot, allowed)
    attention_weights = jnp.exp(scores - log_total)
    weights_low = attention_weights.astype(BF16)
    grad_values = jnp.einsum(
        "kgst,skgd->tkd", weights_low, grad_attended, preferred_element_type=F32
    )
    grad_weights = jnp.einsum(
        "skgd,tkd->kgst", grad_attended, values, preferred_element_type=F32
    )
    grad_scores = attention_weights * (
        grad_weights - jnp.sum(attention_weights * grad_weights, axis=-1, keepdims=True)
    )
    grad_scores = grad_scores.astype(BF16)
    grad_queries = (
        jnp.einsum("kgst,tkd->skgd", grad_scores, keys_rot, preferred_element_type=F32)
        * scale_factor
    )
    grad_keys = (
        jnp.einsum("kgst,skgd->tkd", grad_scores, queries, preferred_element_type=F32)
        * scale_factor
    )
    grad_mixed = jnp.concatenate(
        [
            unrotate(grad_queries.reshape(length, H, HD), cos_table, sin_table).reshape(
                length, H * HD
            ),
            unrotate(grad_keys, cos_table, sin_table).reshape(length, KVH * HD),
            grad_values.reshape(length, KVH * HD),
        ],
        axis=1,
    ).astype(BF16)
    grad_qkv = left_product(normed_one, grad_mixed)
    grad_normed_one = right_product(grad_mixed, full_qkv)
    grad_gain_one = jnp.sum(grad_normed_one * scaled_one, axis=0)
    input_grad = grad_middle + norm_back(grad_normed_one * gain_one, scaled_one, inverse_one)

    att_grad = jnp.concatenate(
        [close_rows(grad_qkv.astype(BF16)), close_rows(grad_out.astype(BF16))], axis=2
    )
    gain_grad = jnp.stack([grad_gain_one, grad_gain_two], axis=0).astype(BF16)
    gain_grad = gain_grad.reshape(2, 128, 12).transpose(1, 0, 2)
    gain_grad = gray(gain_grad.reshape(4, 4, 4, 2, 2, 12), (0, 1, 2)).reshape(128, 2, 12)
    gain_grad = jnp.pad(gain_grad, ((0, 0), (0, 14), (0, 116)))
    up_grad = close_rows(grad_up.astype(BF16)).reshape(32, 192, 512)
    att_sum, gain_sum, up_sum, down_sum = scatter_grads(
        att_grad.reshape(TWO7 + (48, 1152)),
        gain_grad.reshape(TWO7 + (16, 128)),
        up_grad.reshape(TWO5 + (192, 512)),
        grad_down.astype(BF16).reshape(TWO5 + (32, 1536)),
    )
    shard_grads = (
        unfold(att_sum[:, :768]),
        unfold(att_sum[:, 768:]),
        natural_columns(unfold(up_sum)),
        down_sum,
        gain_sum[:2, :12].T,
    )
    firsts = (first_qkv, first_out, first_up, first_down, first_gains)
    seconds = (second_qkv, second_out, second_up, second_down, second_gains)
    updated = [
        adamw_step(
            masters[number],
            firsts[number],
            seconds[number],
            shard_grads[number],
            RATES[number],
            DECAYS[number],
        )
        for number in range(5)
    ]
    return (
        block_output,
        input_grad,
        *(update[0] for update in updated),
        *(update[1] for update in updated),
        *(update[2] for update in updated),
    )


def solution(mesh):
    rows = P("fsdp", None)
    return jax.shard_map(
        body,
        mesh=mesh,
        in_specs=(rows, rows, P("fsdp")) + (rows,) * 15,
        out_specs=(rows,) * 17,
        check_vma=False,
    )
```

```python
import functools
import math

import jax
import jax.numpy as jnp
import numpy as np
from jax import lax
from jax.experimental import pallas as pl
from jax.experimental.pallas import tpu as pltpu
from jax.sharding import PartitionSpec as P

H = 16
KVH = 8
HD = 96
FF = 4096
STEP = 10
D = 1536
TOK = 256


EPSILON = 1e-05
THETA = 100000.0
BETA_ONE = 0.9
BETA_TWO = 0.95
ADAM_EPSILON = 1e-08
RATES = (0.08, 0.3, 0.08, 0.05, 1.0)
DECAYS = (0.1, 0.1, 0.1, 0.1, 0.0)
MASKED = -1e30

MESH = pl.DeviceIdType.MESH
BF16 = jnp.bfloat16
F32 = jnp.float32
MIB = 1024 * 1024

CUBE = ("xb", "xa", "zb", "za", "yb", "ya")
LINKS = ("xa", "xb", "za", "zb", "ya", "yb")
QUAD_LINKS = ("xa", "xb", "za", "zb", "yb")
GRAY = (0, 1, 3, 2)


class Place:
    def __init__(self):
        me = lax.axis_index("fsdp")
        self.me = me
        self.c = lax.rem(me, 2)
        self.y = lax.rem(me // 2, 4)
        self.z = lax.rem(me // 8, 4)
        self.x = me // 32
        self.bit = {"c": self.c}
        for name in "xyz":
            at = getattr(self, name)
            self.bit[name + "b"] = at // 2
            self.bit[name + "a"] = lax.rem(at + at // 2, 2)

    def partner(self, *dims):
        at = {"x": self.x, "y": self.y, "z": self.z, "c": self.c}
        for dim in dims:
            name = dim[0]
            if dim == "c":
                at["c"] = 1 - at["c"]
            elif dim[1] == "a":
                at[name] = at[name] + 1 - 2 * lax.rem(at[name], 2)
            else:
                at[name] = 3 - at[name]
        return ((at["x"] * 4 + at["z"]) * 4 + at["y"]) * 2 + at["c"]


def greet(devices):
    barrier = pltpu.get_barrier_semaphore()
    for device in devices:
        pl.semaphore_signal(barrier, inc=1, device_id=(device,), device_id_type=MESH)
    pl.semaphore_wait(barrier, len(devices))


class Sems:
    def __init__(self, send, recv):
        self.send, self.recv, self.used = send, recv, 0

    def copy(self, src, dst, device):
        at = self.used
        self.used += 1
        return pltpu.make_async_remote_copy(
            src_ref=src,
            dst_ref=dst,
            send_sem=self.send.at[at],
            recv_sem=self.recv.at[at],
            device_id=(device,),
            device_id_type=MESH,
        )


def spot(place, dims, done=(), flip=None):
    return tuple(
        pl.ds(0, 2) if dim in done else (1 - place.bit[dim] if dim == flip else place.bit[dim])
        for dim in dims
    )


def rotated(links, by):
    return links[by:] + links[:by]


ATT_PARTS = ((0, 2), (1, 3), (2, 5), (3, 4), (4, 1))
UP_PARTS = ((0, 0), (1, 1), (2, 2), (3, 3))
DOWN_PARTS = (((0, 128), 0), ((128, 128), 1), ((256, 128), 2), ((384, 128), 3), ((512, 1024), 4))
ATT_CORE = (0, 0, 0, 0, 0, 1, 1, 1, 1)


def down_cut(columns):
    return (pl.ds(0, 32), pl.ds(*columns))


class Gather:
    def __init__(self, place, sems, ref, dims, links, rotation, cut):
        self.place, self.sems, self.ref, self.dims, self.cut = place, sems, ref, dims, cut
        self.order, self.copies = rotated(links, rotation), []

    def step(self, number):
        if number > 0:
            self.copies[number - 1].wait_recv()
        if number < len(self.order):
            view = self.ref.at[spot(self.place, self.dims, self.order[:number]) + self.cut]
            copy = self.sems.copy(view, view, self.place.partner(self.order[number]))
            copy.start()
            self.copies.append(copy)

    def end(self):
        for copy in self.copies:
            copy.wait_send()


def each_block(place, dims, free, visit):
    count = 2 ** len(free)

    def at(i):
        index = []
        weight = count
        for dim in dims:
            if dim in free:
                weight //= 2
                index.append(lax.rem(i // weight, 2))
            else:
                index.append(place.bit[dim])
        return tuple(index)

    if count == 1:
        visit(at(0))
    else:
        pl.loop(0, count)(lambda i: visit(at(i)))


class Scatter:
    def __init__(self, place, sems, ref, far, got, stage, sem, dims, links, rotation, cut):
        self.place, self.sems, self.ref, self.far, self.got = place, sems, ref, far, got
        self.stage, self.sem, self.dims, self.cut = stage, sem, dims, cut
        self.order = tuple(reversed(rotated(links, rotation)))
        self.rest = tuple(dim for dim in dims if dim != self.order[0])
        self.copies = []
        self.prepare(0)

    def prepare(self, number):
        link = self.order[number]
        free = self.order[number + 1 :]
        src = self.ref.at[spot(self.place, self.dims, free, flip=link) + self.cut]
        if number == 0:
            dst = self.far.at[spot(self.place, self.dims, free) + self.cut]
        else:
            dst = self.got.at[spot(self.place, self.rest, free)]
        self.copies.append(self.sems.copy(src, dst, self.place.partner(link)))

    def add(self, number):
        link = self.order[number]
        free = self.order[number + 1 :]
        if number == 0:
            here = self.far.at[spot(self.place, self.dims, free, flip=link) + self.cut]
            copy = pltpu.make_async_copy(here, self.stage, self.sem)
            copy.start()
            copy.wait()

        def visit(index):
            bits = dict(zip(self.dims, index))
            own = index + self.cut
            if number == 0:
                other = self.stage[tuple(bits[dim] for dim in self.rest)]
            else:
                other = self.got[tuple(1 - bits[dim] if dim == link else bits[dim] for dim in self.rest)]
            self.ref[own] = (self.ref[own].astype(F32) + other.astype(F32)).astype(BF16)

        each_block(self.place, self.dims, free, visit)

    def step(self, number):
        if number > 0:
            self.copies[number - 1].wait_recv()
            self.add(number - 1)
        if number < len(self.order):
            if number > 0:
                self.prepare(number)
            self.copies[number].start()

    def end(self):
        for copy in self.copies:
            copy.wait_send()


def natural_group(g):
    xb, xa = lax.rem(g // 16, 2), lax.rem(g // 8, 2)
    zb, za = lax.rem(g // 4, 2), lax.rem(g // 2, 2)
    yb = lax.rem(g, 2)
    x = 2 * xb + lax.rem(xa + xb, 2)
    z = 2 * zb + lax.rem(za + zb, 2)
    return (xb, xa, zb, za, yb), (x * 4 + z) * 2 + yb


def dot(left, right):
    return lax.dot_general(left, right, (((1,), (0,)), ((), ())), preferred_element_type=F32)


def dot_t(left, right):
    return lax.dot_general(left, right, (((1,), (1,)), ((), ())), preferred_element_type=F32)


def cols(i, width):
    return pl.ds(pl.multiple_of(i * width, width), width)


def stream_groups(fetch, use):
    fetch(0).start()

    @pl.loop(0, 32)
    def _(g):
        @pl.when(g + 1 < 32)
        def _():
            fetch(g + 1).start()

        fetch(g).wait()
        use(g)


def head_pad(value, spread):
    high = value.astype(BF16)
    low = (value - high.astype(F32)).astype(BF16)
    return dot(high, spread) + dot(low, spread)


def turn(value, cos, sin):
    return value * cos + pltpu.roll(value, 64, 1) * sin


def mask_bias(seg_col, seg_row):
    rows = lax.broadcasted_iota(jnp.int32, (TOK, TOK), 0)
    columns = lax.broadcasted_iota(jnp.int32, (TOK, TOK), 1)
    allowed = jnp.logical_and(seg_col == seg_row, columns <= rows)
    return jnp.where(allowed, 0.0, MASKED).astype(F32)


def row_norm(value):
    return lax.rsqrt(jnp.mean(value * value, axis=-1, keepdims=True) + EPSILON)


def each_rows(step, visit, rows=TOK):
    @pl.loop(0, rows // step)
    def _(i):
        visit(pl.ds(pl.multiple_of(i * step, step), step))


def sigmoid(value):
    return 1.0 / (1.0 + jnp.exp(-value))


def dot_first(left, right):
    return lax.dot_general(left, right, (((0,), (0,)), ((), ())), preferred_element_type=F32)


class Outs:
    def __init__(self, sems):
        self.sems, self.copies = sems, []

    def put(self, src, dst):
        copy = pltpu.make_async_copy(src, dst, self.sems.at[len(self.copies)])
        copy.start()
        self.copies.append(copy)

    def end(self):
        for copy in self.copies:
            copy.wait()


def quad_of(place):
    return {(0, 1): place.partner("c"), (1, 0): place.partner("ya"), (1, 1): place.partner("ya", "c")}


def forward_kernel(
    att_in, up_in, down_in, x, dy, seg_col, seg_row, cos, sin, perm, spread, pick, owner,
    att, up, down, wq_out, wo_out, wgu_out, n2t_out, dy_all, q_out, at_out, n1t_out, m_out, g_out, gu_out, zt_out,
    y_out,
    wq, wo, wgu, wd, att_stage, up_stage, gain_stage, gains, n1, q, apad, a, m, n2_all, zgu, bias, turned, n2t, zt, y,
    send, recv, local, group_sem, out_sem,
):
    place = Place()
    sems = Sems(send, recv)
    outs = Outs(out_sem)
    quad = quad_of(place)
    sibling, across = quad[0, 1], quad[1, 0]
    greet([place.partner(link) for link in LINKS] + [quad[0, 1], quad[1, 1]])
    dims5 = CUBE[:5]
    home6 = spot(place, CUBE)
    home5 = spot(place, dims5)
    ya, c = place.bit["ya"], place.c
    rank = 2 * ya + c
    five = pl.ds(0, 5)
    swap = sems.copy(att_in.at[pl.ds(5 - 5 * c, 5)], att.at[home6 + (five, c)], sibling)
    swap.start()
    starts = [
        pltpu.make_async_copy(att_in.at[pl.ds(5 * c, 5)], att.at[home6 + (five, c)], local.at[0]),
        pltpu.make_async_copy(down_in, down.at[home5], local.at[1]),
        pltpu.make_async_copy(up_in.at[rank], up.at[home5 + (pl.ds(0, 4), rank)], local.at[2]),
        pltpu.make_async_copy(dy, dy_all.at[ya, c], local.at[3]),
    ]
    for copy in starts:
        copy.start()
    scatter = []
    for (dya, dc), device in quad.items():
        to = 2 * (1 - ya if dya else ya) + (1 - c if dc else c)
        copy = sems.copy(up_in.at[to], up.at[home5 + (pl.ds(0, 4), rank)], device)
        copy.start()
        scatter.append(copy)
    for copy in starts:
        copy.wait()
    swap.wait()
    first = [Gather(place, sems, att, CUBE, LINKS, by, (k,)) for k, by in ATT_PARTS]
    second = [Gather(place, sems, down, dims5, QUAD_LINKS, by, down_cut(at)) for at, by in DOWN_PARTS]
    second += [Gather(place, sems, up, dims5, QUAD_LINKS, by, (k,)) for k, by in UP_PARTS]
    for number in range(7):
        for job in first:
            job.step(number)
        if number == 0:
            bias[...] = mask_bias(seg_col[...], seg_row[...])
            for copy in scatter:
                copy.wait()
        if number >= 3:
            for job in second:
                job.step(number - 3)
    dy_near = sems.copy(dy_all.at[ya, c], dy_all.at[ya, c], sibling)
    dy_near.start()
    dy_far = sems.copy(dy_all.at[ya, c], dy_all.at[ya, c], across)
    dy_far.start()

    def fetch_att(g):
        bits, _ = natural_group(g)
        slot = lax.rem(g, 2)
        return pltpu.make_async_copy(att.at[bits], att_stage.at[slot], group_sem.at[slot])

    wide, narrow = pl.ds(0, 640), pl.ds(640, 128)
    shared = {0: [], 1: []}
    for at in range(4):
        rows = pl.ds(GRAY[at] * 384, 384)
        for core, refs in ((0, [wq.at[:, rows, wide]]), (1, [wq.at[:, rows, narrow], wo.at[rows]])):
            shared[core].append([sems.copy(ref, ref, sibling) for ref in refs])
    gain_share = sems.copy(gains, gains, sibling)

    @pl.when(c == 1)
    def _():
        copy = pltpu.make_async_copy(
            att.at[(pl.ds(0, 2),) * 6 + (4, pl.ds(0, 2), pl.ds(0, 16))], gain_stage, local.at[0]
        )
        copy.start()
        copy.wait()
        tiles = gain_stage[...].reshape(128, 16, 128).astype(F32)
        lines = lax.broadcasted_iota(jnp.int32, (128, 16, 128), 1)
        for number in range(2):
            line = jnp.sum(jnp.where(lines == number, tiles, 0.0), axis=1).astype(BF16)
            vector = jnp.sum(dot(line, pick[...]) * owner[...].astype(F32), axis=0, keepdims=True)
            gains[number : number + 1, :] = vector
        gains[2:8, :] = jnp.zeros((6, D), F32)
        gain_share.start()

    fetch_att(0).start()
    for at in range(4):

        @pl.loop(0, 8)
        def _(part):
            g = at * 8 + part

            @pl.when(g + 1 < 32)
            def _():
                fetch_att(g + 1).start()

            fetch_att(g).wait()
            bits, n = natural_group(g)
            slot = lax.rem(g, 2)
            order = perm[bits[4]]
            rows = pl.ds(pl.multiple_of(n * 48, 16), 48)
            block = jnp.concatenate(
                [att_stage[slot, :, k].reshape(192, 128) for k in range(5)], axis=1
            )

            @pl.when(c == 0)
            def _():
                opened = dot(order, block).astype(BF16)
                for quarter in range(4):
                    wq[quarter, rows, 0:640] = opened[48 * quarter : 48 * quarter + 48]

            @pl.when(c == 1)
            def _():
                opened = dot(order, block[:, :512]).astype(BF16)
                for quarter in range(4):
                    piece = opened[48 * quarter : 48 * quarter + 48]
                    wq[quarter, rows, 640:768] = piece[:, :128]
                    wo[rows, 384 * quarter : 384 * quarter + 384] = piece[:, 128:]

        for core in range(2):

            @pl.when(c == core)
            def _():
                for copy in shared[core][at]:
                    copy.start()

    for job in second:
        job.step(4)

    @pl.when(c == 0)
    def _():
        gain_share.wait_recv()

    def norm_one(at):
        value = x[at, :].astype(F32)
        n1[at, :] = (value * row_norm(value) * gains[0:1, :]).astype(BF16)

    each_rows(64, norm_one)
    for core in range(2):

        @pl.when(c == core)
        def _():
            for at in range(4):
                for copy in shared[1 - core][at]:
                    copy.wait_recv()

    outs.put(wq, wq_out)
    outs.put(wo, wo_out)

    def heads(i, rotated_too):
        value = dot(n1[...], wq[i // 2, :, cols(lax.rem(i, 2), 384)])
        padded = head_pad(value, spread[...])
        for at in range(4):
            head = padded[:, 128 * at : 128 * at + 128]
            if rotated_too:
                head = turn(head, cos[...], sin[...])
            lanes = pl.ds(pl.multiple_of(lax.rem(i, 2) * 512 + 128 * at, 128), 128)
            q[cols(i // 2, 256), lanes] = head.astype(BF16)

    pl.loop(0, 6)(lambda i: heads(i, True))
    pl.loop(6, 8)(lambda i: heads(i, False))
    outs.put(q, q_out)

    @pl.loop(0, 8)
    def _(j):
        pair = q[cols(j // 4, 256), cols(lax.rem(j, 4), 256)]
        key = q[512:768, cols(j, 128)]
        value = q[768:1024, cols(j, 128)]
        for at in range(2):
            scores = dot_t(pair[:, 128 * at : 128 * at + 128], key) * (1.0 / math.sqrt(HD))
            scores = scores + bias[...]
            exponent = jnp.exp(scores - jnp.max(scores, axis=-1, keepdims=True))
            weights = exponent / jnp.sum(exponent, axis=-1, keepdims=True)
            lanes = pl.ds(pl.multiple_of(j * 256 + 128 * at, 128), 128)
            apad[:, lanes] = dot(weights.astype(BF16), value).astype(BF16)

    @pl.loop(0, 4)
    def _(i):
        a[:, cols(i, 384)] = dot_t(apad[:, cols(i, 512)], spread[...]).astype(BF16)

    @pl.loop(0, 3)
    def _(i):
        m[:, cols(i, 512)] = x[:, cols(i, 512)].astype(F32) + dot(a[...], wo[:, cols(i, 512)])

    own = n2_all.at[ya, c]

    def norm_two(at):
        value = m[at, :]
        own[at, :] = (value * row_norm(value) * gains[1:2, :]).astype(BF16)

    each_rows(64, norm_two)
    near = sems.copy(own, own, sibling)
    near.start()
    far = sems.copy(own, own, across)
    far.start()
    outs.put(m, m_out)
    outs.put(gains, g_out)

    for job in second:
        job.step(5)
    wd_copy = pltpu.make_async_copy(down, wd, local.at[0])
    wd_copy.start()

    def fetch_up(g):
        bits, _ = natural_group(g)
        slot = lax.rem(g, 2)
        return pltpu.make_async_copy(up.at[bits], up_stage.at[slot], group_sem.at[slot])

    def use_up(g):
        bits, n = natural_group(g)
        slot = lax.rem(g, 2)
        rows = pl.ds(pl.multiple_of(n * 48, 16), 48)
        block = jnp.concatenate([up_stage[slot, k].reshape(192, 128) for k in range(4)], axis=1)
        opened = dot(perm[bits[4]], block).astype(BF16)
        for quarter in range(4):
            wgu[rows, 512 * quarter : 512 * quarter + 512] = opened[48 * quarter : 48 * quarter + 48]

    stream_groups(fetch_up, use_up)
    outs.put(wgu, wgu_out)
    near.wait_recv()
    wd_copy.wait()

    def mlp(pair):
        rows = cols(pair, 512)

        @pl.loop(0, 4)
        def _(i):
            left = n2_all[pair].reshape(512, D)
            gate = dot(left, wgu[:, cols(i, 256)])
            upward = dot(left, wgu[:, cols(i + 4, 256)])
            hidden = gate * sigmoid(gate) * upward
            zgu[0, rows, cols(i, 256)] = hidden.astype(BF16)
            zgu[1, rows, cols(i, 256)] = gate.astype(BF16)
            zgu[2, rows, cols(i, 256)] = upward.astype(BF16)

        outs.put(zgu.at[pl.ds(1, 2), rows], gu_out.at[:, rows])

        @pl.loop(0, 4)
        def _(i):
            part = dot(zgu[0, rows, :], wd[..., cols(i, 384)].reshape(1024, 384)).astype(BF16)
            y[pair, :, :, cols(i, 384)] = part.reshape(2, TOK, 384)

        outs.put(y.at[pair], y_out.at[pair])

        @pl.loop(0, 6)
        def _(i):
            n2t[cols(i, 256), rows] = jnp.transpose(n2_all[pair, :, :, cols(i, 256)].reshape(512, 256))

        outs.put(n2t.at[:, rows], n2t_out.at[:, rows])

        @pl.loop(0, 4)
        def _(i):
            zt[cols(i, 256), rows] = jnp.transpose(zgu[0, rows, cols(i, 256)])

        outs.put(zt.at[:, rows], zt_out.at[:, rows])

    mlp(ya)

    @pl.loop(0, 6)
    def _(i):
        turned[0, cols(i, 256), :] = jnp.transpose(n1[:, cols(i, 256)])
        turned[1, cols(i, 256), :] = jnp.transpose(a[:, cols(i, 256)])

    outs.put(turned.at[0], n1t_out)
    outs.put(turned.at[1], at_out)
    dy_far.wait_recv()
    dy_onward = sems.copy(dy_all.at[1 - ya, c], dy_all.at[1 - ya, c], sibling)
    dy_onward.start()
    far.wait_recv()
    onward = sems.copy(n2_all.at[1 - ya, c], n2_all.at[1 - ya, c], sibling)
    onward.start()
    onward.wait_recv()
    mlp(1 - ya)
    near.wait_send()
    far.wait_send()
    onward.wait_send()
    dy_near.wait()
    dy_far.wait_send()
    dy_onward.wait()
    for core in range(2):

        @pl.when(c == core)
        def _():
            for at in range(4):
                for copy in shared[core][at]:
                    copy.wait_send()

    @pl.when(c == 1)
    def _():
        gain_share.wait_send()

    for job in first + second:
        job.end()
    outs.end()


def backward_kernel(
    x, cos, sin, seg_col, seg_row, perm_t, spread, pick, owner, gains,
    down_in, wq_in, wo_in, wgu_in, n2t_in, dy_in, q_in, at_in, n1t_in, m_in, gu_in, zt_in, y_in,
    att_out, up_out, down_out, block_out, grad_out,
    far_att, far_up, far_down, land, quad_got,
    n2t, dy, zt, gu, wo_slots, wgu_slots, g_up, got_up, g_down, got_down0, got_down1, got_down2, got_down3, got_down4,
    stage, down_stage, g_att, got_att, dw, rt, lhs, dm, dn1, p, t, bias, dg, dg_got, up_land, att_land,
    send, recv, local, slot_sem, load_sem, out_sem,
):
    place = Place()
    sems = Sems(send, recv)
    outs = Outs(out_sem)
    quad = quad_of(place)
    sibling, across = quad[0, 1], quad[1, 0]
    greet([place.partner(link) for link in LINKS] + [quad[0, 1], quad[1, 1]])
    dims5 = CUBE[:5]
    home6 = spot(place, CUBE)
    home5 = spot(place, dims5)
    ya, c = place.bit["ya"], place.c
    rank = 2 * ya + c
    loads = {}

    def load(name, src, dst):
        copy = pltpu.make_async_copy(src, dst, load_sem.at[len(loads)])
        copy.start()
        loads[name] = copy

    load("dy", dy_in, dy)
    load("gu", gu_in, gu)
    load("zt", zt_in, zt)
    load("n2t", n2t_in, n2t)
    load("m", m_in, dm)
    load("n1t", n1t_in, lhs.at[0])
    load("at", at_in, lhs.at[1])

    def fetch_wd(i):
        slot = i % 2
        rows = (pl.ds(0, 2),) * 3 + (pl.ds(0, 32), pl.ds(0, D))
        return pltpu.make_async_copy(
            down_in.at[(i // 2, i % 2) + rows], wo_slots.at[slot, pl.ds(0, 256)].reshape(2, 2, 2, 32, D), slot_sem.at[slot]
        )

    y_away = sems.copy(y_in.at[1 - ya, 1 - c], quad_got.at[0], sibling)
    y_away.start()
    y_near = sems.copy(y_in.at[ya, 1 - c], quad_got.at[1], sibling)
    y_near.start()

    up_jobs = [
        Scatter(
            place, sems, g_up, far_up, got_up.at[k], stage, local.at[0], dims5, QUAD_LINKS, by,
            (k, pl.ds(0, 2), pl.ds(0, 2)),
        )
        for k, by in UP_PARTS
    ]
    down_gots = (got_down0, got_down1, got_down2, got_down3, got_down4)
    down_jobs = [
        Scatter(
            place, sems, g_down, far_down, got, down_stage.at[(pl.ds(0, 2),) * 4 + down_cut((0, at[1]))], local.at[1],
            dims5, QUAD_LINKS, by, down_cut(at),
        )
        for (at, by), got in zip(DOWN_PARTS, down_gots)
    ]
    att_jobs = [
        Scatter(place, sems, g_att, far_att, got_att.at[k], stage, local.at[2], CUBE, LINKS, by, (k,))
        for k, by in ATT_PARTS
    ]
    mlp_jobs = up_jobs + down_jobs

    loads["dy"].wait()
    loads["gu"].wait()
    fetch_wd(0).start()
    for i in range(4):
        if i < 3:
            fetch_wd(i + 1).start()
        fetch_wd(i).wait()

        @pl.loop(0, 2)
        def _(pair):
            rows = cols(pair, 512)
            lanes = pl.ds(256 * i, 256)
            dz = dot_t(dy[pair].reshape(512, D), wo_slots[i % 2, 0:256, :])
            gate = gu[0, rows, lanes].astype(F32)
            upward = gu[1, rows, lanes].astype(F32)
            sg = sigmoid(gate)
            gu[0, rows, lanes] = (dz * upward * sg * (1.0 + gate * (1.0 - sg))).astype(BF16)
            gu[1, rows, lanes] = (dz * gate * sg).astype(BF16)

    def fetch_wgu(i, slot):
        return pltpu.make_async_copy(wgu_in.at[cols(i, 256)], wgu_slots.at[slot], slot_sem.at[2 + slot])

    def back_up(pair):
        fetch_wgu(0, 0).start()

        @pl.loop(0, 6)
        def _(i):
            slot = lax.rem(i, 2)

            @pl.when(i < 5)
            def _():
                fetch_wgu(i + 1, lax.rem(i + 1, 2)).start()

            fetch_wgu(i, slot).wait()
            rows = cols(pair, 512)
            part = dot_t(gu[0, rows, :], wgu_slots[slot, :, 0:1024])
            part = part + dot_t(gu[1, rows, :], wgu_slots[slot, :, 1024:2048])
            p[pair, :, :, cols(i, 256)] = part.astype(BF16).reshape(2, TOK, 256)

    def fetch(src, dst):
        copy = pltpu.make_async_copy(src, dst, local.at[3])
        copy.start()
        copy.wait()

    def add_into(total, term):
        def visit(at):
            total[at, :] = (total[at, :].astype(F32) + term[at, :].astype(F32)).astype(BF16)

        each_rows(64, visit)

    back_up(1 - ya)
    away = sems.copy(p.at[1 - ya, 1 - c], quad_got.at[3], sibling)
    away.start()
    back_up(ya)
    near = sems.copy(p.at[ya, 1 - c], quad_got.at[4], sibling)
    near.start()
    away.wait_recv()
    fetch(quad_got.at[3], t.at[1])
    add_into(p.at[1 - ya, c], t.at[1])
    far = sems.copy(p.at[1 - ya, c], quad_got.at[5], across)
    far.start()

    def fold_into(value, at, store):
        for part in range(8):
            zb, za, yb = part // 4, part // 2 % 2, part % 2
            row = (GRAY[2 * zb + za] * 2 + yb) * 48
            stack = jnp.concatenate(
                [value[row : row + 48, 128 * quarter : 128 * quarter + 128] for quarter in range(4)], axis=0
            )
            folded = dot(perm_t[yb], stack).astype(BF16).reshape(2, 2, 48, 128)
            store((at // 2, lax.rem(at, 2), zb, za, yb), folded)

    def natural_x(at):
        return at + lax.rem(at // 2, 2) * (1 - 2 * lax.rem(at, 2))

    loads["n2t"].wait()
    for k in range(4):

        @pl.loop(0, 4)
        def _(at):
            rows = pl.ds(pl.multiple_of(natural_x(at) * 384, 128), 384)
            right = jnp.concatenate(
                [gu[quarter // 2, :, pl.ds((quarter % 2) * 512 + 128 * k, 128)] for quarter in range(4)], axis=1
            )
            value = dot(n2t[rows, :], right).astype(BF16)

            def store(index, folded):
                g_up[index + (k,)] = folded

            fold_into(value, at, store)

        up_jobs[k].copies[0].start()

    loads["zt"].wait()
    for i in range(6):

        @pl.loop(0, 4)
        def _(at):
            right = dy[:, :, :, pl.ds(256 * i, 256)].reshape(1024, 256)
            value = dot(zt[cols(at, 256), :], right).astype(BF16).reshape(2, 2, 2, 32, 256)
            g_down[at // 2, lax.rem(at, 2), :, :, :, :, pl.ds(256 * i, 256)] = value

        if i == 1:
            for job in down_jobs[:4]:
                job.copies[0].start()
    down_jobs[4].copies[0].start()

    y_away.wait_recv()
    fetch(y_in.at[1 - ya, c], t.at[0])
    fetch(quad_got.at[0], t.at[1])
    add_into(t.at[0], t.at[1])
    far.wait_recv()
    y_far = sems.copy(t.at[0], quad_got.at[2], across)
    y_far.start()
    near.wait_recv()
    fetch(quad_got.at[4], t.at[1])
    add_into(p.at[ya, c], t.at[1])
    fetch(quad_got.at[5], t.at[1])
    loads["m"].wait()
    load("q", q_in, gu.at[0])
    dg[...] = jnp.zeros((8, D), F32)

    def back_two(at):
        value = dm[at, :]
        r = row_norm(value)
        xh = value * r
        dn = p.at[ya, c][at, :].astype(F32) + t[1, at, :].astype(F32)
        dg[1:2, :] = dg[1:2, :] + jnp.sum(dn * xh, axis=0, keepdims=True)
        e = dn * gains[1:2, :]
        grad = dy.at[ya, c][at, :].astype(F32) + r * (e - xh * jnp.mean(xh * e, axis=-1, keepdims=True))
        dm[at, :] = grad
        low = grad.astype(BF16)
        for k in range(3):
            for quarter in range(4):
                start = quarter * 384 + k * 128
                rt[6 + k, at, 128 * quarter : 128 * quarter + 128] = low[:, start : start + 128]

    each_rows(32, back_two)

    def fetch_wo(i):
        slot = i % 2
        return pltpu.make_async_copy(wo_in.at[pl.ds(384 * i, 384)], wo_slots.at[slot], slot_sem.at[slot])

    fetch_wo(0).start()
    for i in range(4):
        if i < 3:
            fetch_wo(i + 1).start()
        fetch_wo(i).wait()
        left = jnp.concatenate(
            [rt[6 + k, :, 128 * quarter : 128 * quarter + 128] for quarter in range(4) for k in range(3)], axis=1
        )
        da = dot_t(left, wo_slots[i % 2]).astype(BF16)
        zt[256 * (i // 2) : 256 * (i // 2) + 256, 512 * (i % 2) : 512 * (i % 2) + 512] = dot(
            da, spread[...]
        ).astype(BF16)

    tile_copies = {}
    for u in range(9):
        k = u if u < 5 else u - 5
        for at in range(4):
            rows = pl.ds(384 * at, 384)
            tile_copies[u, at] = sems.copy(dw.at[(4 * u + at) % 4], land.at[k, rows], sibling)
    sent = {0: [], 1: []}

    def give(u):
        core = 1 - ATT_CORE[u]

        @pl.when(c == core)
        def _():
            for at in range(4):
                if len(sent[core]) >= 4:
                    sent[core][-4].wait_send()
                dw[at] = dot(lhs[u // 6, 384 * at : 384 * at + 384, :], rt[u]).astype(BF16)
                tile_copies[u, at].start()
                sent[core].append(tile_copies[u, at])

    def take(u):
        k = u if u < 5 else u - 5

        @pl.when(c == ATT_CORE[u])
        def _():
            for at in range(4):
                tile_copies[u, at].wait_recv()
            copy = pltpu.make_async_copy(land.at[k], n2t.at[:, pl.ds(0, 512)], local.at[3])
            copy.start()
            copy.wait()

            @pl.loop(0, 4)
            def _(at):
                rows = pl.ds(pl.multiple_of(natural_x(at) * 384, 128), 384)
                value = dot(lhs[u // 6, rows, :], rt[u]) + n2t[rows, 0:512].astype(F32)

                def store(index, folded):
                    for spot_ya in range(2):
                        g_att[index + (spot_ya, k)] = folded[spot_ya]

                fold_into(value.astype(BF16), at, store)

            att_jobs[k].copies[0].start()

    loads["at"].wait()
    loads["n1t"].wait()
    for u in (6, 7, 8):
        give(u)
    for job in mlp_jobs:
        job.step(1)

    bias[...] = mask_bias(seg_col[...], seg_row[...])
    loads["q"].wait()
    scale = 1.0 / math.sqrt(HD)

    @pl.loop(0, 8)
    def _(j):
        rows, lanes = cols(j // 4, 256), cols(lax.rem(j, 4), 256)
        pair = gu[0, rows, lanes]
        da = zt[rows, lanes]
        key = gu[0, 512:768, cols(j, 128)]
        value = gu[0, 768:1024, cols(j, 128)]
        dk = jnp.zeros((TOK, 128), F32)
        dv = jnp.zeros((TOK, 128), F32)
        for at in range(2):
            query = pair[:, 128 * at : 128 * at + 128]
            grad = da[:, 128 * at : 128 * at + 128]
            scores = dot_t(query, key) * scale + bias[...]
            exponent = jnp.exp(scores - jnp.max(scores, axis=-1, keepdims=True))
            weights = exponent / jnp.sum(exponent, axis=-1, keepdims=True)
            dv = dv + dot_first(weights.astype(BF16), grad)
            dp = dot_t(grad, value)
            ds = weights * (dp - jnp.sum(weights * dp, axis=-1, keepdims=True))
            ds = ds.astype(BF16)
            dq = dot(ds, key) * scale
            dk = dk + dot_first(ds, query)
            here = pl.ds(pl.multiple_of(lax.rem(j, 4) * 256 + 128 * at, 128), 128)
            gu[1, rows, here] = turn(dq, cos[...], -sin[...]).astype(BF16)
        gu[1, 512:768, cols(j, 128)] = turn(dk * scale, cos[...], -sin[...]).astype(BF16)
        gu[1, 768:1024, cols(j, 128)] = dv.astype(BF16)

    @pl.loop(0, 8)
    def _(i):
        padded = gu[1, cols(i // 2, 256), cols(lax.rem(i, 2), 512)]
        flat = dot_t(padded, spread[...]).astype(BF16)
        for part in range(3):
            rt[lax.rem(i, 2) * 3 + part, :, cols(i // 2, 128)] = flat[:, 128 * part : 128 * part + 128]

    for u in (5, 0, 1, 2, 3, 4):
        give(u)
    for u in (6, 7, 8, 5, 0, 1, 2, 3, 4):
        take(u)
    for job in mlp_jobs:
        job.step(2)

    def fetch_wq(i):
        slot = i % 2
        ref = (n2t, zt)[slot]
        return [
            pltpu.make_async_copy(
                wq_in.at[quarter, pl.ds(256 * i, 256)],
                ref.at[pl.ds(256 * quarter, 256), pl.ds(0, 768)],
                slot_sem.at[4 + 4 * slot + quarter],
            )
            for quarter in range(4)
        ]

    for i in range(6):
        for ahead in (0, 1) if i == 0 else (i + 1,):
            if ahead < 6:
                for copy in fetch_wq(ahead):
                    copy.start()
        for copy in fetch_wq(i):
            copy.wait()
        weight = (n2t, zt)[i % 2]
        total = jnp.zeros((TOK, 256), F32)
        for quarter in range(4):
            left = jnp.concatenate([rt[k, :, 128 * quarter : 128 * quarter + 128] for k in range(6)], axis=1)
            total = total + dot_t(left, weight[256 * quarter : 256 * quarter + 256, 0:768])
        dn1[:, 256 * i : 256 * i + 256] = total

    def back_one(at):
        value = x[at, :].astype(F32)
        r = row_norm(value)
        xh = value * r
        dn = dn1[at, :]
        dg[0:1, :] = dg[0:1, :] + jnp.sum(dn * xh, axis=0, keepdims=True)
        e = dn * gains[0:1, :]
        dn1[at, :] = dm[at, :] + r * (e - xh * jnp.mean(xh * e, axis=-1, keepdims=True))

    each_rows(32, back_one)
    outs.put(dn1, grad_out)
    dg_copy = sems.copy(dg, dg_got, sibling)

    @pl.when(c == 0)
    def _():
        dg_copy.start()
        dg_copy.wait_send()

    @pl.when(c == 1)
    def _():
        g_att[(slice(None),) * 6 + (4,)] = jnp.zeros(TWO7 + (48, 128), BF16)
        dg_copy.wait_recv()
        lines = lax.broadcasted_iota(jnp.int32, (128, 16, 128), 1)
        tiles = jnp.zeros((128, 16, 128), F32)
        for number in range(2):
            vector = dg[number : number + 1, :] + dg_got[number : number + 1, :]
            spread_out = (owner[...].astype(F32) * vector).astype(BF16)
            line = dot_t(spread_out, pick[...])
            tiles = jnp.where(lines == number, line.reshape(128, 1, 128), tiles)
        g_att[(slice(None),) * 6 + (4, slice(None), slice(0, 16))] = tiles.astype(BF16).reshape(
            TWO7 + (16, 128)
        )
        att_jobs[4].copies[0].start()

    for number in range(1, 7):
        for job in att_jobs:
            job.step(number)
        if number + 2 < 6:
            for job in mlp_jobs:
                job.step(number + 2)
    last = []
    for (dya, dc), device in quad.items():
        to = 2 * (1 - ya if dya else ya) + (1 - c if dc else c)
        src = g_up.at[home5 + (pl.ds(0, 4), 1 - ya if dya else ya, 1 - c if dc else c)]
        copy = sems.copy(src, up_land.at[rank], device)
        copy.start()
        last.append(copy)
    att_last = sems.copy(g_att.at[home6 + (pl.ds(0, 5), 1 - c)], att_land, sibling)
    att_last.start()
    up_out[rank] = g_up[home5 + (slice(None), ya, c)].astype(F32)
    down_out[...] = g_down[home5].astype(F32)
    att_out[pl.ds(5 * c, 5)] = g_att[home6 + (slice(None), c)].astype(F32)

    outs.end()
    y_far.wait_send()
    y_near.wait_recv()
    y_far.wait_recv()
    fetch(m_in, dm)
    for src in (y_in.at[ya, c], quad_got.at[1], quad_got.at[2]):
        fetch(src, t.at[1])

        def add_y(at):
            dm[at, :] = dm[at, :] + t[1, at, :].astype(F32)

        each_rows(64, add_y)

    def store_block(at):
        block_out[at, :] = dm[at, :].astype(BF16)

    each_rows(64, store_block)
    for copy in last:
        copy.wait()
    att_last.wait()
    for dya, dc in quad:
        to = 2 * (1 - ya if dya else ya) + (1 - c if dc else c)
        up_out[to] = up_land[to].astype(F32)
    att_out[pl.ds(5 - 5 * c, 5)] = att_land[...].astype(F32)
    for copy in (y_away, y_near, away, near, far):
        copy.wait_send()
    for core in range(2):

        @pl.when(c == core)
        def _():
            for copy in sent[core][-4:]:
                copy.wait_send()

    for job in att_jobs + mlp_jobs:
        job.end()


ANY = pl.BlockSpec(memory_space=pl.ANY)
VMEM = pl.BlockSpec(memory_space=pltpu.VMEM)
TWO4 = (2,) * 4
TWO5 = (2,) * 5
TWO6 = (2,) * 6
TWO7 = (2,) * 7


def shape(dims, kind=BF16):
    return jax.ShapeDtypeStruct(dims, kind)


def vmem(dims, kind=BF16):
    return pltpu.VMEM(dims, kind)


def params(number, mib):
    return pltpu.CompilerParams(
        collective_id=number, has_side_effects=True, vmem_limit_bytes=mib * MIB
    )


def dma(count):
    return pltpu.SemaphoreType.DMA((count,))


def forward(*operands):
    return pl.pallas_call(
        forward_kernel,
        name="forward",
        out_shape=(
            shape(TWO6 + (5, 2, 48, 128)),
            shape(TWO5 + (4, 4, 48, 128)),
            shape(TWO5 + (32, D)),
            shape((4, D, 768)),
            shape((D, D)),
            shape((D, 2048)),
            shape((D, 1024)),
            shape((2, 2, TOK, D)),
            shape((1024, 1024)),
            shape((D, TOK)),
            shape((D, TOK)),
            shape((TOK, D), F32),
            shape((8, D), F32),
            shape((2, 1024, 1024)),
            shape((1024, 1024)),
            shape((2, 2, TOK, D)),
        ),
        in_specs=[ANY] * 3 + [VMEM, ANY] + [VMEM] * 8,
        out_specs=[ANY] * 16,
        scratch_shapes=[
            vmem((4, D, 768)),
            vmem((D, D)),
            vmem((D, 2048)),
            vmem(TWO5 + (32, D)),
            vmem((2, 2, 5, 2, 48, 128)),
            vmem((2, 4, 4, 48, 128)),
            vmem(TWO7 + (16, 128)),
            vmem((8, D), F32),
            vmem((TOK, D)),
            vmem((1024, 1024)),
            vmem((TOK, 2048)),
            vmem((TOK, D)),
            vmem((TOK, D), F32),
            vmem((2, 2, TOK, D)),
            vmem((3, 1024, 1024)),
            vmem((TOK, TOK), F32),
            vmem((2, D, TOK)),
            vmem((D, 1024)),
            vmem((1024, 1024)),
            vmem((2, 2, TOK, D)),
            dma(110),
            dma(110),
            dma(4),
            dma(2),
            dma(20),
        ],
        compiler_params=params(0, 62),
    )(*operands)


def backward(*operands):
    return pl.pallas_call(
        backward_kernel,
        name="backward",
        out_shape=(
            shape((10, 48, 128), F32),
            shape((4, 4, 48, 128), F32),
            shape((32, D), F32),
            shape((TOK, D)),
            shape((TOK, D), F32),
            shape(TWO6 + (5, 2, 48, 128)),
            shape(TWO5 + (4, 2, 2, 48, 128)),
            shape(TWO5 + (32, D)),
            shape((5, D, 512)),
            shape((6, TOK, D)),
        ),
        in_specs=[VMEM] * 10 + [ANY] * 13,
        out_specs=[VMEM] * 4 + [ANY] * 6,
        scratch_shapes=[
            vmem((D, 1024)),
            vmem((2, 2, TOK, D)),
            vmem((1024, 1024)),
            vmem((2, 1024, 1024)),
            vmem((2, 384, D)),
            vmem((2, 256, 2048)),
            vmem(TWO5 + (4, 2, 2, 48, 128)),
            vmem((4,) + TWO6 + (48, 128)),
            vmem(TWO5 + (32, D)),
            *[vmem(TWO4 + (32, columns[1])) for columns, _ in DOWN_PARTS],
            vmem(TWO6 + (48, 128)),
            vmem(TWO4 + (32, 1024)),
            vmem(TWO6 + (5, 2, 48, 128)),
            vmem((5,) + TWO6 + (48, 128)),
            vmem((4, 384, 512)),
            vmem((9, TOK, 512)),
            vmem((2, D, TOK)),
            vmem((TOK, D), F32),
            vmem((TOK, D), F32),
            vmem((2, 2, TOK, D)),
            vmem((2, TOK, D)),
            vmem((TOK, TOK), F32),
            vmem((8, D), F32),
            vmem((8, D), F32),
            vmem((4, 4, 48, 128)),
            vmem((5, 48, 128)),
            dma(140),
            dma(140),
            dma(4),
            dma(12),
            dma(8),
            dma(1),
        ],
        compiler_params=params(1, 63),
    )(*operands)


def tables():
    perm = np.zeros((2, 192, 192), np.float32)
    for yb in range(2):
        for spot_ya in range(2):
            for core in range(2):
                at = 2 * spot_ya + core
                to = 2 * (1 - spot_ya if yb else spot_ya) + core
                for quarter in range(4):
                    for row in range(12):
                        perm[yb, quarter * 48 + to * 12 + row, at * 48 + quarter * 12 + row] = 1
    spread = np.zeros((384, 512), np.float32)
    for head in range(4):
        for lane in range(96):
            spread[head * 96 + lane, head * 128 + lane + (16 if lane >= 48 else 0)] = 1
    pick = np.zeros((128, D), np.float32)
    pick[np.arange(D) % 12, np.arange(D)] = 1
    owner = np.zeros((128, D), np.float32)
    order = np.array(GRAY)
    for gx in range(4):
        for gz in range(4):
            for gy in range(4):
                for core in range(2):
                    at = ((gx * 4 + gz) * 4 + gy) * 2 + core
                    device = ((order[gx] * 4 + order[gz]) * 4 + order[gy]) * 2 + core
                    owner[at, device * 12 : device * 12 + 12] = 1
    return [jnp.asarray(table, BF16) for table in (perm, spread, pick, owner)]


def padded_tables(cos_table, sin_table):
    gap = jnp.zeros((TOK, 16), F32)
    cos = jnp.concatenate([cos_table, gap, cos_table, gap], axis=1)
    sin = jnp.concatenate([-sin_table, gap, sin_table, gap], axis=1)
    return cos, sin


def gray(array, axes):
    for axis in axes:
        pieces = jnp.split(array, 4, axis=axis)
        array = jnp.concatenate([pieces[at] for at in GRAY], axis=axis)
    return array


def fold(weight, lead=()):
    columns = weight.shape[-1] // 4
    parts = [weight[..., at * columns : (at + 1) * columns] for at in range(4)]
    return jnp.concatenate(parts, axis=-2)


def unfold(block):
    parts = [block[..., at * 12 : (at + 1) * 12, :] for at in range(4)]
    return jnp.concatenate(parts, axis=-1)


def rank_columns(up):
    split = gray(up.reshape(12, 2, 4, 4, 4, 2, 32), (2, 3, 4)).reshape(12, 2, 4, 4, 2, 2, 2, 32)
    return split.transpose(5, 6, 0, 1, 2, 3, 4, 7).reshape(4, 12, 2048)


def natural_columns(pieces):
    split = pieces.reshape(2, 2, 12, 2, 4, 4, 2, 32).transpose(2, 3, 4, 5, 6, 0, 1, 7)
    return gray(split.reshape(12, 2, 4, 4, 4, 2, 32), (2, 3, 4)).reshape(12, 8192)


def tiled(block):
    count = block.shape[-1] // 128
    return jnp.stack([block[..., 128 * at : 128 * at + 128] for at in range(count)], axis=-3)


def untiled(tiles):
    return jnp.concatenate([tiles[..., at, :, :] for at in range(tiles.shape[-3])], axis=-1)


def layout(segment_row):
    length = segment_row.shape[0]
    places = jnp.arange(length, dtype=jnp.int32)
    same_doc = segment_row[:, None] == segment_row[None, :]
    starts = jnp.min(jnp.where(same_doc, places[None, :], length), axis=1)
    offsets = (places - starts).astype(jnp.float32)
    allowed = jnp.logical_and(same_doc, places[None, :] <= places[:, None])
    exponents = jnp.arange(0, HD, 2, dtype=jnp.float32) / HD
    angles = offsets[:, None] * (THETA ** (-exponents))[None, :]
    return (allowed, jnp.cos(angles), jnp.sin(angles))


def adamw_step(weight, moment_one, moment_two, gradient, rate, decay):
    first_new = BETA_ONE * moment_one + (1.0 - BETA_ONE) * gradient
    second_new = BETA_TWO * moment_two + (1.0 - BETA_TWO) * gradient * gradient
    unbiased_one = first_new / (1.0 - BETA_ONE**STEP)
    unbiased_two = second_new / (1.0 - BETA_TWO**STEP)
    weight_new = weight - rate * (
        unbiased_one / (jnp.sqrt(unbiased_two) + ADAM_EPSILON) + decay * weight
    )
    return (weight_new, first_new, second_new)


def body(
    tokens_in,
    cotangent,
    segment_ids,
    proj_qkv,
    proj_out,
    proj_up,
    proj_down,
    norm_gains,
    first_qkv,
    first_out,
    first_up,
    first_down,
    first_gains,
    second_qkv,
    second_out,
    second_up,
    second_down,
    second_gains,
):
    masters = (proj_qkv, proj_out, proj_up, proj_down, norm_gains)
    low_qkv, low_out, low_up, low_down, low_gains = (part.astype(BF16) for part in masters)
    gain_tile = jnp.pad(low_gains.T, ((0, 46), (0, 116)))
    att_tiles = jnp.concatenate(
        [tiled(fold(low_qkv)), tiled(fold(low_out)), gain_tile[None]], axis=0
    )
    up_tiles = tiled(fold(rank_columns(low_up)))
    _, cos_table, sin_table = layout(segment_ids)
    cos, sin = padded_tables(cos_table, sin_table)
    perm, spread, pick, owner = tables()
    seg_col, seg_row = segment_ids.reshape(TOK, 1), segment_ids.reshape(1, TOK)
    (
        _, _, down_all, wq, wo, wgu, n2t, dy_all, heads, a_t, n1_t, middle, gains, gate_up, z_t, y_part,
    ) = forward(
        att_tiles, up_tiles, low_down, tokens_in, cotangent, seg_col, seg_row, cos, sin, perm, spread, pick, owner
    )
    att_sum, up_sum, down_sum, block_output, input_grad, *_ = backward(
        tokens_in, cos, sin, seg_col, seg_row, perm.transpose(0, 2, 1), spread, pick, owner, gains,
        down_all, wq, wo, wgu, n2t, dy_all, heads, a_t, n1_t, middle, gate_up, z_t, y_part,
    )
    shard_grads = (
        unfold(untiled(att_sum[:6])),
        unfold(untiled(att_sum[6:9])),
        natural_columns(unfold(untiled(up_sum))),
        down_sum,
        att_sum[9, :2, :12].T,
    )
    firsts = (first_qkv, first_out, first_up, first_down, first_gains)
    seconds = (second_qkv, second_out, second_up, second_down, second_gains)
    updated = [
        adamw_step(
            masters[number],
            firsts[number],
            seconds[number],
            shard_grads[number],
            RATES[number],
            DECAYS[number],
        )
        for number in range(5)
    ]
    return (
        block_output,
        input_grad,
        *(update[0] for update in updated),
        *(update[1] for update in updated),
        *(update[2] for update in updated),
    )


def solution(mesh):
    rows = P("fsdp", None)
    return jax.shard_map(
        body,
        mesh=mesh,
        in_specs=(rows, rows, P("fsdp")) + (rows,) * 15,
        out_specs=(rows,) * 17,
        check_vma=False,
    )
```

```python
import functools
import math

import jax
import jax.numpy as jnp
import numpy as np
from jax import lax
from jax.experimental import pallas as pl
from jax.experimental.pallas import tpu as pltpu
from jax.sharding import PartitionSpec as P

H = 16
KVH = 8
HD = 96
FF = 4096
STEP = 10
D = 1536
TOK = 256


EPSILON = 1e-05
THETA = 100000.0
BETA_ONE = 0.9
BETA_TWO = 0.95
ADAM_EPSILON = 1e-08
RATES = (0.08, 0.3, 0.08, 0.05, 1.0)
DECAYS = (0.1, 0.1, 0.1, 0.1, 0.0)
MASKED = -1e30

MESH = pl.DeviceIdType.MESH
BF16 = jnp.bfloat16
F32 = jnp.float32
MIB = 1024 * 1024
LAG = 3

CUBE = ("xb", "xa", "zb", "za", "yb", "ya")
LINKS = ("xa", "xb", "za", "zb", "ya", "yb")
QUAD_LINKS = ("xa", "xb", "za", "zb", "yb")
GRAY = (0, 1, 3, 2)
FOUR = ((0, 1, 2, 3), (2, 3, 0, 1))


class Place:
    def __init__(self):
        me = lax.axis_index("fsdp")
        self.me = me
        self.c = lax.rem(me, 2)
        self.y = lax.rem(me // 2, 4)
        self.z = lax.rem(me // 8, 4)
        self.x = me // 32
        self.bit = {"c": self.c}
        for name in "xyz":
            at = getattr(self, name)
            self.bit[name + "b"] = at // 2
            self.bit[name + "a"] = lax.rem(at + at // 2, 2)

    def partner(self, *dims):
        at = {"x": self.x, "y": self.y, "z": self.z, "c": self.c}
        for dim in dims:
            name = dim[0]
            if dim == "c":
                at["c"] = 1 - at["c"]
            elif dim[1] == "a":
                at[name] = at[name] + 1 - 2 * lax.rem(at[name], 2)
            else:
                at[name] = 3 - at[name]
        return ((at["x"] * 4 + at["z"]) * 4 + at["y"]) * 2 + at["c"]


def greet(devices):
    barrier = pltpu.get_barrier_semaphore()
    for device in devices:
        pl.semaphore_signal(barrier, inc=1, device_id=(device,), device_id_type=MESH)
    pl.semaphore_wait(barrier, len(devices))


class Sems:
    def __init__(self, send, recv):
        self.send, self.recv, self.used = send, recv, 0

    def copy(self, src, dst, device):
        at = self.used
        self.used += 1
        return pltpu.make_async_remote_copy(
            src_ref=src,
            dst_ref=dst,
            send_sem=self.send.at[at],
            recv_sem=self.recv.at[at],
            device_id=(device,),
            device_id_type=MESH,
        )


def spot(place, dims, done=(), flip=None):
    return tuple(
        pl.ds(0, 2) if dim in done else (1 - place.bit[dim] if dim == flip else place.bit[dim])
        for dim in dims
    )


def rotated(links, by):
    return links[by:] + links[:by]


UP_PARTS = ((0, 5), (5, 5), (10, 5), (15, 5), (20, 4))
DOWN_PARTS = ((0, 4), (4, 4), (8, 5), (13, 4), (17, 7))
TILES = ((0, 2, 0, 0, 0), (2, 2, 0, 2, 0), (4, 1, 0, 4, 0), (5, 1, 1, 3, 0), (6, 2, 1, 0, 1), (8, 1, 1, 2, 1))


class Gather:
    def __init__(self, place, sems, ref, dims, links, rotation, cut):
        self.place, self.sems, self.ref, self.dims, self.cut = place, sems, ref, dims, cut
        self.order, self.copies = rotated(links, rotation), []

    def step(self, number):
        if number > 0:
            self.copies[number - 1].wait_recv()
        if number < len(self.order):
            view = self.ref.at[spot(self.place, self.dims, self.order[:number]) + self.cut]
            copy = self.sems.copy(view, view, self.place.partner(self.order[number]))
            copy.start()
            self.copies.append(copy)

    def end(self):
        for copy in self.copies:
            copy.wait_send()


def each_block(place, dims, free, whole, visit):
    looped = tuple(dim for dim in free if dim not in whole)
    count = 2 ** len(looped)

    def at(i):
        index = []
        weight = count
        for dim in dims:
            if dim in whole:
                index.append(slice(None))
            elif dim in looped:
                weight //= 2
                index.append(lax.rem(i // weight, 2))
            else:
                index.append(place.bit[dim])
        return tuple(index)

    if count == 1:
        visit(at(0))
    else:
        pl.loop(0, count)(lambda i: visit(at(i)))


class Scatter:
    def __init__(self, place, sems, ref, far, got, dims, links, rotation, cuts, cut, counts):
        self.place, self.sems, self.ref, self.far, self.got = place, sems, ref, far, got
        self.dims, self.cut, self.counts = dims, cut, counts
        self.order = tuple(reversed(rotated(links, rotation)))
        self.rest = tuple(dim for dim in dims if dim != self.order[0])
        link, free = self.order[0], self.order[1:]
        there = spot(place, dims, free, flip=link)
        here = spot(place, dims, free)
        self.firsts = [sems.copy(ref.at[there + at], far.at[here + at], place.partner(link)) for at in cuts]
        self.size = math.prod(counts) * 2 ** len(free)
        self.copies = [None]

    def prepare(self, number):
        link = self.order[number]
        free = self.order[number + 1 :]
        src = self.ref.at[spot(self.place, self.dims, free, flip=link) + self.cut]
        dst = self.got.at[spot(self.place, self.rest, free)]
        self.copies.append(self.sems.copy(src, dst, self.place.partner(link)))

    def fetch(self, stage, sem):
        for copy in self.firsts:
            copy.wait_recv()
        link, free = self.order[0], self.order[1:]
        here = self.far.at[spot(self.place, self.dims, free, flip=link) + self.cut]
        self.stage = stage.reshape(*(2,) * len(free), *self.counts, 16, 128)
        self.staged = pltpu.make_async_copy(here, self.stage, sem)
        self.staged.start()

    def add(self, number):
        link = self.order[number]
        free = tuple(dim for dim in self.dims if dim in self.order[number + 1 :])
        whole = free[-2:]

        def visit(index):
            bits = dict(zip(self.dims, index))
            own = index + self.cut
            if number == 0:
                other = self.stage[tuple(bits[dim] for dim in self.rest)]
            else:
                other = self.got[tuple(1 - bits[dim] if dim == link else bits[dim] for dim in self.rest)]
            self.ref[own] = (self.ref[own].astype(F32) + other.astype(F32)).astype(BF16)

        each_block(self.place, self.dims, free, whole, visit)

    def step(self, number):
        if number == 1:
            self.staged.wait()
        elif number > 1:
            self.copies[number - 1].wait_recv()
        if number > 0:
            self.add(number - 1)
        if number < len(self.order):
            self.prepare(number)
            self.copies[number].start()

    def end(self):
        for copy in self.firsts + self.copies[1:]:
            copy.wait_send()


def first_adds(jobs, stage, sems):
    at = 0
    while at < len(jobs):
        batch, units = [], 0
        while at < len(jobs) and len(batch) < 9:
            if units + jobs[at].size > 640:
                break
            jobs[at].fetch(stage.at[pl.ds(units, jobs[at].size)], sems.at[len(batch)])
            batch.append(jobs[at])
            units += jobs[at].size
            at += 1
        for job in batch:
            job.step(1)


def natural_group(g):
    xb, xa = lax.rem(g // 16, 2), lax.rem(g // 8, 2)
    zb, za = lax.rem(g // 4, 2), lax.rem(g // 2, 2)
    yb = lax.rem(g, 2)
    x = 2 * xb + lax.rem(xa + xb, 2)
    z = 2 * zb + lax.rem(za + zb, 2)
    return (xb, xa, zb, za, yb), (x * 4 + z) * 2 + yb


def dot(left, right):
    return lax.dot_general(left, right, (((1,), (0,)), ((), ())), preferred_element_type=F32)


def dot_t(left, right):
    return lax.dot_general(left, right, (((1,), (1,)), ((), ())), preferred_element_type=F32)


def cols(i, width):
    return pl.ds(pl.multiple_of(i * width, width), width)


def head_pad(value, spread):
    high = value.astype(BF16)
    low = (value - high.astype(F32)).astype(BF16)
    return dot(high, spread) + dot(low, spread)


def turn(value, cos, sin):
    return value * cos + pltpu.roll(value, 64, 1) * sin


def mask_bias(seg_col, seg_row):
    rows = lax.broadcasted_iota(jnp.int32, (TOK, TOK), 0)
    columns = lax.broadcasted_iota(jnp.int32, (TOK, TOK), 1)
    allowed = jnp.logical_and(seg_col == seg_row, columns <= rows)
    return jnp.where(allowed, 0.0, MASKED).astype(F32)


def row_norm(value):
    return lax.rsqrt(jnp.mean(value * value, axis=-1, keepdims=True) + EPSILON)


def each_rows(step, visit, rows=TOK):
    @pl.loop(0, rows // step)
    def _(i):
        visit(pl.ds(pl.multiple_of(i * step, step), step))


def open_quarter(block, yb, quarter):
    pieces = [block[48 * at + 12 * quarter : 48 * at + 12 * quarter + 12] for at in FOUR[yb]]
    return jnp.concatenate(pieces, axis=0)


def sigmoid(value):
    return 1.0 / (1.0 + jnp.exp(-value))


def dot_first(left, right):
    return lax.dot_general(left, right, (((0,), (0,)), ((), ())), preferred_element_type=F32)


class Outs:
    def __init__(self, sems):
        self.sems, self.copies, self.ended = sems, [], 0

    def put(self, src, dst):
        copy = pltpu.make_async_copy(src, dst, self.sems.at[len(self.copies)])
        copy.start()
        self.copies.append(copy)

    def end(self):
        for copy in self.copies[self.ended :]:
            copy.wait()
        self.ended = len(self.copies)


def quad_of(place):
    return {(0, 1): place.partner("c"), (1, 0): place.partner("ya"), (1, 1): place.partner("ya", "c")}


def forward_kernel(
    att_in, up_in, down_in, x, dy, seg_col, seg_row, cos, sin, spread, pick, owner,
    down_out, wq_out, wo_out, wgu_out, n2t_out, dy_all, q_out, at_out, n1t_out, m_out, g_out, gu_out, zt_out,
    y_out,
    att, up, down, wq, wo, wgu, gains, n1, q, apad, a, m, n2_all, z, gu, bias, turned, n2t, zt, y,
    send, recv, local, out_sem,
):
    place = Place()
    sems = Sems(send, recv)
    outs = Outs(out_sem)
    quad = quad_of(place)
    sibling, across = quad[0, 1], quad[1, 0]
    greet([place.partner(link) for link in LINKS] + [quad[0, 1], quad[1, 1]])
    dims5 = CUBE[:5]
    home6 = spot(place, CUBE)
    home5 = spot(place, dims5)
    ya, c = place.bit["ya"], place.c
    rank = 2 * ya + c
    mine = pl.ds(3 * c, 3)
    six = pl.ds(pl.multiple_of(6 * rank, 2), 6)
    swap = sems.copy(att_in.at[1 - c], att.at[home6 + (mine,)], sibling)
    swap.start()
    starts = [
        pltpu.make_async_copy(att_in.at[c], att.at[home6 + (mine,)], local.at[0]),
        pltpu.make_async_copy(down_in, down.at[home5], local.at[1]),
        pltpu.make_async_copy(up_in.at[rank], up.at[home5 + (pl.ds(0, 2), six)], local.at[2]),
    ]
    for copy in starts:
        copy.start()
    scatter = []
    for (dya, dc), device in quad.items():
        to = 2 * (1 - ya if dya else ya) + (1 - c if dc else c)
        copy = sems.copy(up_in.at[to], up.at[home5 + (pl.ds(0, 2), six)], device)
        copy.start()
        scatter.append(copy)
    for copy in starts:
        copy.wait()
    swap.wait()
    first = [Gather(place, sems, att, CUBE, LINKS, by, (by,)) for by in range(6)]
    ups = [
        Gather(place, sems, up, dims5, QUAD_LINKS, by, (pl.ds(0, 2), pl.ds(*at)))
        for by, at in enumerate(UP_PARTS)
    ]
    downs = [Gather(place, sems, down, dims5, QUAD_LINKS, by, (pl.ds(*at),)) for by, at in enumerate(DOWN_PARTS)]
    second = ups + downs
    for number in range(7):
        for job in first:
            job.step(number)
        if number == 0:
            bias[...] = mask_bias(seg_col[...], seg_row[...])
            for copy in scatter:
                copy.wait()
        if number >= LAG:
            for job in second:
                job.step(number - LAG)
    dy_near = sems.copy(dy, dy_all.at[ya, c], sibling)
    dy_near.start()
    dy_far = sems.copy(dy, dy_all.at[ya, c], across)
    dy_far.start()

    wide, narrow = pl.ds(0, 640), pl.ds(640, 128)
    shared = {0: [], 1: []}
    for at in range(4):
        rows = pl.ds(GRAY[at] * 384, 384)
        for core, refs in ((0, [wq.at[:, rows, wide]]), (1, [wq.at[:, rows, narrow], wo.at[rows]])):
            shared[core].append([sems.copy(ref, ref, sibling) for ref in refs])
    gain_share = sems.copy(gains, gains, sibling)

    @pl.when(c == 1)
    def _():
        tiles = jnp.stack([att[..., 3 * core, 4, :, :].reshape(64, 16, 128) for core in range(2)], axis=1)
        tiles = tiles.reshape(128, 16, 128).astype(F32)
        lines = lax.broadcasted_iota(jnp.int32, (128, 16, 128), 1)
        for number in range(2):
            line = jnp.sum(jnp.where(lines == number, tiles, 0.0), axis=1).astype(BF16)
            vector = jnp.sum(dot(line, pick[...]) * owner[...].astype(F32), axis=0, keepdims=True)
            gains[number : number + 1, :] = vector
        gains[2:8, :] = jnp.zeros((6, D), F32)
        gain_share.start()

    for at in range(4):

        @pl.loop(0, 8)
        def _(part):
            bits, n = natural_group(at * 8 + part)
            rows = pl.ds(pl.multiple_of(n * 48, 16), 48)
            block = jnp.concatenate([att[bits][:, :, k].reshape(192, 128) for k in range(5)], axis=1)
            for yb in range(2):

                @pl.when(jnp.logical_and(bits[4] == yb, c == 0))
                def _():
                    for quarter in range(4):
                        wq[quarter, rows, 0:640] = open_quarter(block, yb, quarter)

                @pl.when(jnp.logical_and(bits[4] == yb, c == 1))
                def _():
                    for quarter in range(4):
                        piece = open_quarter(block[:, :512], yb, quarter)
                        wq[quarter, rows, 640:768] = piece[:, 384:]
                        wo[rows, 384 * quarter : 384 * quarter + 384] = piece[:, :384]

        for core in range(2):

            @pl.when(c == core)
            def _():
                for copy in shared[core][at]:
                    copy.start()


    @pl.when(c == 0)
    def _():
        gain_share.wait_recv()

    def norm_one(at):
        value = x[at, :].astype(F32)
        n1[at, :] = (value * row_norm(value) * gains[0:1, :]).astype(BF16)

    each_rows(64, norm_one)
    for core in range(2):

        @pl.when(c == core)
        def _():
            for at in range(4):
                for copy in shared[1 - core][at]:
                    copy.wait_recv()

    outs.put(wq, wq_out)
    outs.put(wo, wo_out)

    def heads(i, rotated_too):
        value = dot(n1[...], wq[i // 2, :, cols(lax.rem(i, 2), 384)])
        padded = head_pad(value, spread[...])
        for at in range(4):
            head = padded[:, 128 * at : 128 * at + 128]
            if rotated_too:
                head = turn(head, cos[...], sin[...])
            lanes = pl.ds(pl.multiple_of(lax.rem(i, 2) * 512 + 128 * at, 128), 128)
            q[cols(i // 2, 256), lanes] = head.astype(BF16)

    pl.loop(0, 6)(lambda i: heads(i, True))
    pl.loop(6, 8)(lambda i: heads(i, False))
    for job in ups:
        job.step(4)
    outs.put(q, q_out)

    @pl.loop(0, 8)
    def _(j):
        pair = q[cols(j // 4, 256), cols(lax.rem(j, 4), 256)]
        key = q[512:768, cols(j, 128)]
        value = q[768:1024, cols(j, 128)]
        for at in range(2):
            scores = dot_t(pair[:, 128 * at : 128 * at + 128], key) * (1.0 / math.sqrt(HD))
            scores = scores + bias[...]
            exponent = jnp.exp(scores - jnp.max(scores, axis=-1, keepdims=True))
            weights = exponent / jnp.sum(exponent, axis=-1, keepdims=True)
            lanes = pl.ds(pl.multiple_of(j * 256 + 128 * at, 128), 128)
            apad[:, lanes] = dot(weights.astype(BF16), value).astype(BF16)

    for job in downs:
        job.step(4)
    @pl.loop(0, 4)
    def _(i):
        a[:, cols(i, 384)] = dot_t(apad[:, cols(i, 512)], spread[...]).astype(BF16)

    @pl.loop(0, 3)
    def _(i):
        m[:, cols(i, 512)] = x[:, cols(i, 512)].astype(F32) + dot(a[...], wo[:, cols(i, 512)])

    own = n2_all.at[ya, c]

    def norm_two(at):
        value = m[at, :]
        own[at, :] = (value * row_norm(value) * gains[1:2, :]).astype(BF16)

    each_rows(64, norm_two)
    near = sems.copy(own, own, sibling)
    near.start()
    far = sems.copy(own, own, across)
    far.start()
    outs.put(m, m_out)
    outs.put(gains, g_out)

    for job in ups:
        job.step(5)

    @pl.loop(0, 32)
    def _(g):
        bits, n = natural_group(g)
        rows = pl.ds(pl.multiple_of(n * 48, 16), 48)
        block = jnp.concatenate(
            [up[bits + (k // 2,)].reshape(12, 2, 16, 128)[:, k % 2].reshape(192, 128) for k in range(4)], axis=1
        )
        for yb in range(2):

            @pl.when(bits[4] == yb)
            def _():
                for quarter in range(4):
                    wgu[rows, 512 * quarter : 512 * quarter + 512] = open_quarter(block, yb, quarter)

    outs.put(wgu, wgu_out)
    for job in downs:
        job.step(5)
    outs.put(down, down_out)
    near.wait_recv()

    def mlp(pair):
        rows = cols(pair, 512)

        @pl.loop(0, 4)
        def _(i):
            left = n2_all[pair].reshape(512, D)
            gate = dot(left, wgu[:, cols(i, 256)])
            upward = dot(left, wgu[:, cols(i + 4, 256)])
            hidden = gate * sigmoid(gate) * upward
            z[:, cols(i, 256)] = hidden.astype(BF16)
            gu[0, :, cols(i, 256)] = gate.astype(BF16)
            gu[1, :, cols(i, 256)] = upward.astype(BF16)

        outs.put(gu, gu_out.at[:, rows])

        @pl.loop(0, 6)
        def _(i):
            right = jnp.concatenate(
                [down[..., pl.ds(4 * i + 2 * at, 2), :, :].reshape(1024, 128) for at in range(2)], axis=1
            )
            y[:, :, cols(i, 256)] = dot(z[...], right).astype(BF16).reshape(2, TOK, 256)

        outs.put(y, y_out.at[pair])

        @pl.loop(0, 6)
        def _(i):
            n2t[cols(i, 256), rows] = jnp.transpose(n2_all[pair, :, :, cols(i, 256)].reshape(512, 256))

        outs.put(n2t.at[:, rows], n2t_out.at[:, rows])

        @pl.loop(0, 4)
        def _(i):
            zt[cols(i, 256), rows] = jnp.transpose(z[:, cols(i, 256)])

        outs.put(zt.at[:, rows], zt_out.at[:, rows])

    mlp(ya)

    @pl.loop(0, 6)
    def _(i):
        turned[0, cols(i, 256), :] = jnp.transpose(n1[:, cols(i, 256)])
        turned[1, cols(i, 256), :] = jnp.transpose(a[:, cols(i, 256)])

    outs.put(turned.at[0], n1t_out)
    outs.put(turned.at[1], at_out)
    dy_far.wait_recv()
    dy_onward = sems.copy(dy_all.at[1 - ya, c], dy_all.at[1 - ya, c], sibling)
    dy_onward.start()
    far.wait_recv()
    onward = sems.copy(n2_all.at[1 - ya, c], n2_all.at[1 - ya, c], sibling)
    onward.start()
    onward.wait_recv()
    outs.end()
    mlp(1 - ya)
    near.wait_send()
    far.wait_send()
    onward.wait_send()
    dy_near.wait()
    dy_far.wait_send()
    dy_onward.wait()
    for core in range(2):

        @pl.when(c == core)
        def _():
            for at in range(4):
                for copy in shared[core][at]:
                    copy.wait_send()

    @pl.when(c == 1)
    def _():
        gain_share.wait_send()

    for job in first + second:
        job.end()
    outs.end()


def backward_kernel(
    x, cos, sin, seg_col, seg_row, spread, pick, owner, gains, cotangent,
    down_in, wq_in, wo_in, wgu_in, n2t_in, dy_in, q_in, at_in, n1t_in, m_in, gu_in, zt_in, y_in,
    att_out, up_out, down_out, block_out, grad_out,
    far_att, far_up, far_down, land, quad_got,
    n2t, dy, zt, gu, wo_slots, wgu_slots, g_up, got_up, g_down, got_down, stage, g_att, got_att,
    dw, rt, lhs, dm, dn1, p, t, bias, dg, dg_got, up_land, att_land,
    send, recv, local, slot_sem, load_sem, out_sem, stage_sem,
):
    place = Place()
    sems = Sems(send, recv)
    outs = Outs(out_sem)
    quad = quad_of(place)
    sibling, across = quad[0, 1], quad[1, 0]
    greet([place.partner(link) for link in LINKS] + [quad[0, 1], quad[1, 1]])
    dims5 = CUBE[:5]
    home6 = spot(place, CUBE)
    home5 = spot(place, dims5)
    ya, c = place.bit["ya"], place.c
    rank = 2 * ya + c
    loads = {}

    def load(name, src, dst):
        copy = pltpu.make_async_copy(src, dst, load_sem.at[len(loads)])
        copy.start()
        loads[name] = copy

    load("dy", cotangent, dy.at[ya, c])
    load("dy1", dy_in.at[ya, 1 - c], dy.at[ya, 1 - c])
    load("dy2", dy_in.at[1 - ya], dy.at[1 - ya])
    load("gu", gu_in, gu)
    load("zt", zt_in, zt)
    load("n2t", n2t_in, n2t)
    load("m", m_in, dm)
    load("n1t", n1t_in, lhs.at[0])
    load("at", at_in, lhs.at[1])

    wd_slots = [stage.at[pl.ds(192 * slot, 192)].reshape(2, 2, 2, 24, 16, 128) for slot in range(2)]

    def fetch_wd(i):
        slot = i % 2
        whole = (pl.ds(0, 2),) * 3 + (pl.ds(0, 24), pl.ds(0, 16), pl.ds(0, 128))
        return pltpu.make_async_copy(down_in.at[(i // 2, i % 2) + whole], wd_slots[slot], slot_sem.at[slot])

    fetch_wd(0).start()
    fetch_wd(1).start()

    y_away = sems.copy(y_in.at[1 - ya, 1 - c], quad_got.at[0], sibling)
    y_away.start()
    y_near = sems.copy(y_in.at[ya, 1 - c], quad_got.at[1], sibling)
    y_near.start()

    up_jobs = [
        Scatter(
            place, sems, g_up, far_up, got_up.at[by, :, :, :, :, :, pl.ds(0, at[1])], dims5, QUAD_LINKS, by,
            [(pair, pl.ds(*at)) for pair in range(2)], (pl.ds(0, 2), pl.ds(*at)), (2, at[1]),
        )
        for by, at in enumerate(UP_PARTS)
    ]
    down_jobs = [
        Scatter(
            place, sems, g_down, far_down, got_down.at[by, :, :, :, :, pl.ds(0, at[1])], dims5, QUAD_LINKS, by,
            [(pl.ds(*at),)], (pl.ds(*at),), (at[1],),
        )
        for by, at in enumerate(DOWN_PARTS)
    ]
    att_jobs = [
        Scatter(
            place, sems, g_att, far_att, got_att.at[by], CUBE, LINKS, by,
            [(by, pl.ds(0, 2)), (by, pl.ds(2, 2)), (by, pl.ds(4, 1))], (by, pl.ds(0, 5)), (5,),
        )
        for by in range(6)
    ]
    mlp_jobs = up_jobs + down_jobs

    def fetch_wo(i):
        slot = i % 2
        return pltpu.make_async_copy(wo_in.at[pl.ds(384 * i, 384)], wo_slots.at[slot], slot_sem.at[4 + slot])

    def fetch_wgu(i, slot):
        return pltpu.make_async_copy(wgu_in.at[cols(i, 256)], wgu_slots.at[slot], slot_sem.at[2 + slot])

    fetch_wgu(0, 0).start()
    fetch_wgu(1, 1).start()
    fetch_wo(0).start()
    fetch_wo(1).start()
    for name in ("dy", "dy1", "dy2"):
        loads[name].wait()
    loads["gu"].wait()
    for i in range(4):
        fetch_wd(i).wait()

        @pl.loop(0, 2)
        def _(pair):
            rows = cols(pair, 512)
            lanes = pl.ds(256 * i, 256)
            right = jnp.concatenate(
                [wd_slots[i % 2][:, :, :, 2 * at : 2 * at + 2].reshape(256, 128) for at in range(12)], axis=1
            )
            dz = dot_t(dy[pair].reshape(512, D), right)
            gate = gu[0, rows, lanes].astype(F32)
            upward = gu[1, rows, lanes].astype(F32)
            sg = sigmoid(gate)
            gu[0, rows, lanes] = (dz * upward * sg * (1.0 + gate * (1.0 - sg))).astype(BF16)
            gu[1, rows, lanes] = (dz * gate * sg).astype(BF16)

        if i < 2:
            fetch_wd(i + 2).start()

    def back_up():
        @pl.loop(0, 6)
        def _(i):
            slot = lax.rem(i, 2)
            fetch_wgu(i, slot).wait()
            for pair in range(2):
                rows = pl.ds(512 * pair, 512)
                part = dot_t(gu[0, rows, :], wgu_slots[slot, :, 0:1024])
                part = part + dot_t(gu[1, rows, :], wgu_slots[slot, :, 1024:2048])
                p[pair, :, :, cols(i, 256)] = part.astype(BF16).reshape(2, TOK, 256)

            @pl.when(i < 4)
            def _():
                fetch_wgu(i + 2, slot).start()

    def fetch(src, dst):
        copy = pltpu.make_async_copy(src, dst, local.at[3])
        copy.start()
        copy.wait()

    def add_into(total, term):
        def visit(at):
            total[at, :] = (total[at, :].astype(F32) + term[at, :].astype(F32)).astype(BF16)

        each_rows(64, visit)

    back_up()
    away = sems.copy(p.at[1 - ya, 1 - c], quad_got.at[3], sibling)
    away.start()
    near = sems.copy(p.at[ya, 1 - c], quad_got.at[4], sibling)
    near.start()
    away.wait_recv()
    fetch(quad_got.at[3], t.at[1])
    add_into(p.at[1 - ya, c], t.at[1])
    far = sems.copy(p.at[1 - ya, c], quad_got.at[5], across)
    far.start()

    def fold_into(value, width, at, store):
        zb = lax.rem(at, 2)
        for part in range(4):
            z, yb = part // 2, part % 2
            row = part * 48
            pieces = [
                value[row + 12 * to : row + 12 * to + 12, width * quarter : width * quarter + width]
                for to in FOUR[yb]
                for quarter in range(4)
            ]
            folded = jnp.concatenate(pieces, axis=0).reshape(2, 6, 16, width)
            store((at // 4, lax.rem(at // 2, 2), zb, z + zb * (1 - 2 * z), yb), folded)

    def natural_rows(at):
        x = at // 2
        x = x + lax.rem(x // 2, 2) * (1 - 2 * lax.rem(x, 2))
        return pl.ds(pl.multiple_of(x * 384 + lax.rem(at, 2) * 192, 64), 192)

    loads["n2t"].wait()
    for pair in range(2):

        @pl.loop(0, 8)
        def _(at):
            rows = natural_rows(at)
            right = jnp.concatenate(
                [gu[quarter // 2, :, pl.ds((quarter % 2) * 512 + 256 * pair, 256)] for quarter in range(4)], axis=1
            )
            value = dot(n2t[rows, :], right).astype(BF16)

            def store(index, folded):
                folded = folded.reshape(12, 16, 256)
                halves = jnp.stack([folded[:, :, :128], folded[:, :, 128:]], axis=1)
                g_up[index + (pair,)] = halves.reshape(24, 16, 128)

            fold_into(value, 256, at, store)

        for job in up_jobs:
            job.firsts[pair].start()

    loads["zt"].wait()
    for i in range(6):

        @pl.loop(0, 4)
        def _(at):
            right = dy[:, :, :, pl.ds(256 * i, 256)].reshape(1024, 256)
            value = dot(zt[cols(at, 256), :], right).astype(BF16)
            for part in range(2):
                piece = value[:, 128 * part : 128 * part + 128].reshape(2, 2, 2, 2, 16, 128)
                g_down[at // 2, lax.rem(at, 2), :, :, :, pl.ds(4 * i + 2 * part, 2)] = piece

        for job, (start, count) in zip(down_jobs, DOWN_PARTS):
            if 4 * i < start + count <= 4 * i + 4:
                job.firsts[0].start()

    y_away.wait_recv()
    fetch(y_in.at[1 - ya, c], t.at[0])
    fetch(quad_got.at[0], t.at[1])
    add_into(t.at[0], t.at[1])
    far.wait_recv()
    y_far = sems.copy(t.at[0], quad_got.at[2], across)
    y_far.start()
    near.wait_recv()
    fetch(quad_got.at[4], t.at[1])
    add_into(p.at[ya, c], t.at[1])
    fetch(quad_got.at[5], t.at[1])
    loads["m"].wait()
    load("q", q_in, gu.at[0])
    dg[...] = jnp.zeros((8, D), F32)

    def back_two(at):
        value = dm[at, :]
        r = row_norm(value)
        xh = value * r
        dn = p.at[ya, c][at, :].astype(F32) + t[1, at, :].astype(F32)
        dg[1:2, :] = dg[1:2, :] + jnp.sum(dn * xh, axis=0, keepdims=True)
        e = dn * gains[1:2, :]
        grad = dy.at[ya, c][at, :].astype(F32) + r * (e - xh * jnp.mean(xh * e, axis=-1, keepdims=True))
        dm[at, :] = grad
        low = grad.astype(BF16)
        for k in range(3):
            for quarter in range(4):
                start = quarter * 384 + k * 128
                rt[6 + k, at, 128 * quarter : 128 * quarter + 128] = low[:, start : start + 128]

    each_rows(32, back_two)
    load("x", x, dy.at[ya, c])

    for i in range(4):
        fetch_wo(i).wait()
        left = jnp.concatenate(
            [rt[6 + k, :, 128 * quarter : 128 * quarter + 128] for quarter in range(4) for k in range(3)], axis=1
        )
        da = dot_t(left, wo_slots[i % 2]).astype(BF16)
        zt[256 * (i // 2) : 256 * (i // 2) + 256, 512 * (i % 2) : 512 * (i % 2) + 512] = dot(
            da, spread[...]
        ).astype(BF16)
        if i < 2:
            fetch_wo(i + 2).start()

    tile_copies = {}
    for number, (u, count, core, k, out) in enumerate(TILES):
        for at in range(4):
            lanes = pl.ds(0, 512 * count)
            tile_copies[number, at] = sems.copy(
                dw.at[at % 2, :, lanes], land.at[number % 3, pl.ds(384 * at, 384), lanes], sibling
            )
    sent = {0: [], 1: []}

    def tile_right(u, count):
        return jnp.concatenate(
            [rt[u + at, :, 128 * quarter : 128 * quarter + 128] for quarter in range(4) for at in range(count)], axis=1
        )

    def give(number):
        u, count, owner_core, k, out = TILES[number]
        core = 1 - owner_core

        @pl.when(c == core)
        def _():
            right = tile_right(u, count)
            for at in range(4):
                if len(sent[core]) >= 2:
                    sent[core][-2].wait_send()
                left = lhs[out, 384 * at : 384 * at + 384, :]
                dw[at % 2, :, 0 : 512 * count] = dot(left, right).astype(BF16)
                tile_copies[number, at].start()
                sent[core].append(tile_copies[number, at])

    def land_copy(number):
        lanes = pl.ds(0, 512 * TILES[number][1])
        return pltpu.make_async_copy(land.at[number % 3, :, lanes], n2t.at[:, lanes], local.at[3])

    def take(number):
        u, count, core, k, out = TILES[number]

        @pl.when(c == core)
        def _():
            for at in range(4):
                tile_copies[number, at].wait_recv()
            copy = land_copy(number)
            copy.start()
            copy.wait()

            @pl.loop(0, 8)
            def _(at):
                rows = natural_rows(at)
                value = dot(lhs[out, rows, :], tile_right(u, count)) + n2t[rows, 0 : 512 * count].astype(F32)

                def store(index, folded):
                    for spot_ya in range(2):
                        for part in range(count):
                            piece = folded[spot_ya, :, :, 128 * part : 128 * part + 128]
                            g_att[index + (spot_ya, slice(None), k + part)] = piece

                fold_into(value.astype(BF16), 128 * count, at, store)

            if k + count in (2, 4, 5):
                for job in att_jobs:
                    job.firsts[(k + count) // 2 - 1 if k + count < 5 else 2].start()

    loads["at"].wait()
    loads["n1t"].wait()
    give(4)
    give(5)
    bias[...] = mask_bias(seg_col[...], seg_row[...])
    loads["q"].wait()
    scale = 1.0 / math.sqrt(HD)

    @pl.loop(0, 8)
    def _(j):
        rows, lanes = cols(j // 4, 256), cols(lax.rem(j, 4), 256)
        pair = gu[0, rows, lanes]
        da = zt[rows, lanes]
        key = gu[0, 512:768, cols(j, 128)]
        value = gu[0, 768:1024, cols(j, 128)]
        dk = jnp.zeros((TOK, 128), F32)
        dv = jnp.zeros((TOK, 128), F32)
        for at in range(2):
            query = pair[:, 128 * at : 128 * at + 128]
            grad = da[:, 128 * at : 128 * at + 128]
            scores = dot_t(query, key) * scale + bias[...]
            exponent = jnp.exp(scores - jnp.max(scores, axis=-1, keepdims=True))
            weights = exponent / jnp.sum(exponent, axis=-1, keepdims=True)
            dv = dv + dot_first(weights.astype(BF16), grad)
            dp = dot_t(grad, value)
            ds = weights * (dp - jnp.sum(weights * dp, axis=-1, keepdims=True))
            ds = ds.astype(BF16)
            dq = dot(ds, key) * scale
            dk = dk + dot_first(ds, query)
            here = pl.ds(pl.multiple_of(lax.rem(j, 4) * 256 + 128 * at, 128), 128)
            gu[1, rows, here] = turn(dq, cos[...], -sin[...]).astype(BF16)
        gu[1, 512:768, cols(j, 128)] = turn(dk * scale, cos[...], -sin[...]).astype(BF16)
        gu[1, 768:1024, cols(j, 128)] = dv.astype(BF16)

    @pl.loop(0, 8)
    def _(i):
        padded = gu[1, cols(i // 2, 256), cols(lax.rem(i, 2), 512)]
        flat = dot_t(padded, spread[...]).astype(BF16)
        for part in range(3):
            rt[lax.rem(i, 2) * 3 + part, :, cols(i // 2, 128)] = flat[:, 128 * part : 128 * part + 128]

    for number in (3, 0, 1, 2):
        give(number)
    first_adds(mlp_jobs, stage, stage_sem)
    for number in (0, 1, 2, 4, 5, 3):
        take(number)
    for job in mlp_jobs:
        job.step(2)
    def fetch_wq(i):
        slot = i % 2
        ref = (n2t, zt)[slot]
        return [
            pltpu.make_async_copy(
                wq_in.at[quarter, pl.ds(256 * i, 256)],
                ref.at[pl.ds(256 * quarter, 256), pl.ds(0, 768)],
                slot_sem.at[4 + 4 * slot + quarter],
            )
            for quarter in range(4)
        ]

    for i in range(6):
        for ahead in (0, 1) if i == 0 else (i + 1,):
            if ahead < 6:
                for copy in fetch_wq(ahead):
                    copy.start()
        for copy in fetch_wq(i):
            copy.wait()
        weight = (n2t, zt)[i % 2]
        total = jnp.zeros((TOK, 256), F32)
        for quarter in range(4):
            left = jnp.concatenate([rt[k, :, 128 * quarter : 128 * quarter + 128] for k in range(6)], axis=1)
            total = total + dot_t(left, weight[256 * quarter : 256 * quarter + 256, 0:768])
        dn1[:, 256 * i : 256 * i + 256] = total

    def back_one(at):
        value = dy[ya, c, at, :].astype(F32)
        r = row_norm(value)
        xh = value * r
        dn = dn1[at, :]
        dg[0:1, :] = dg[0:1, :] + jnp.sum(dn * xh, axis=0, keepdims=True)
        e = dn * gains[0:1, :]
        dn1[at, :] = dm[at, :] + r * (e - xh * jnp.mean(xh * e, axis=-1, keepdims=True))

    loads["x"].wait()
    each_rows(32, back_one)
    outs.put(dn1, grad_out)
    dg_copy = sems.copy(dg, dg_got, sibling)

    @pl.when(c == 0)
    def _():
        dg_copy.start()
        dg_copy.wait_send()

    @pl.when(c == 1)
    def _():
        g_att[(slice(None),) * 6 + (slice(None), 4)] = jnp.zeros(TWO6 + (6, 16, 128), BF16)
        dg_copy.wait_recv()
        lines = lax.broadcasted_iota(jnp.int32, (128, 16, 128), 1)
        tiles = jnp.zeros((128, 16, 128), F32)
        for number in range(2):
            vector = dg[number : number + 1, :] + dg_got[number : number + 1, :]
            spread_out = (owner[...].astype(F32) * vector).astype(BF16)
            line = dot_t(spread_out, pick[...])
            tiles = jnp.where(lines == number, line.reshape(128, 1, 128), tiles)
        tiles = tiles.astype(BF16).reshape(TWO7 + (16, 128))
        for core in range(2):
            g_att[(slice(None),) * 6 + (3 * core, 4)] = tiles[:, :, :, :, :, :, core]
        for job in att_jobs:
            job.firsts[2].start()

    for job in mlp_jobs:
        job.step(3)
    first_adds(att_jobs, stage, stage_sem)
    for number in range(2, 7):
        for job in att_jobs:
            job.step(number)
        if number < 4:
            for job in mlp_jobs:
                job.step(number + 2)
    last = []
    for (dya, dc), device in quad.items():
        to = 2 * (1 - ya if dya else ya) + (1 - c if dc else c)
        src = g_up.at[home5 + (pl.ds(0, 2), pl.ds(pl.multiple_of(6 * to, 2), 6))]
        copy = sems.copy(src, up_land.at[rank], device)
        copy.start()
        last.append(copy)
    att_last = sems.copy(g_att.at[home6 + (pl.ds(3 - 3 * c, 3),)], att_land, sibling)
    att_last.start()
    up_out[rank] = g_up[home5 + (slice(None), pl.ds(pl.multiple_of(6 * rank, 2), 6))].astype(F32)
    down_out[...] = g_down[home5].astype(F32)
    att_out[c] = g_att[home6 + (pl.ds(3 * c, 3),)].astype(F32)

    outs.end()
    y_far.wait_send()
    y_near.wait_recv()
    y_far.wait_recv()
    fetch(m_in, dm)
    for src in (y_in.at[ya, c], quad_got.at[1], quad_got.at[2]):
        fetch(src, t.at[1])

        def add_y(at):
            dm[at, :] = dm[at, :] + t[1, at, :].astype(F32)

        each_rows(64, add_y)

    def store_block(at):
        t[0, at, :] = dm[at, :].astype(BF16)

    each_rows(64, store_block)
    fetch(t.at[0], block_out)
    for copy in last:
        copy.wait()
    att_last.wait()
    for dya, dc in quad:
        to = 2 * (1 - ya if dya else ya) + (1 - c if dc else c)
        up_out[to] = up_land[to].astype(F32)
    att_out[1 - c] = att_land[...].astype(F32)
    for copy in (y_away, y_near, away, near, far):
        copy.wait_send()
    for core in range(2):

        @pl.when(c == core)
        def _():
            for copy in sent[core][-2:]:
                copy.wait_send()

    for job in att_jobs + mlp_jobs:
        job.end()


ANY = pl.BlockSpec(memory_space=pl.ANY)
VMEM = pl.BlockSpec(memory_space=pltpu.VMEM)
TWO4 = (2,) * 4
TWO5 = (2,) * 5
TWO6 = (2,) * 6
TWO7 = (2,) * 7


def shape(dims, kind=BF16):
    return jax.ShapeDtypeStruct(dims, kind)


def vmem(dims, kind=BF16):
    return pltpu.VMEM(dims, kind)


def params(number, mib):
    return pltpu.CompilerParams(
        collective_id=number, has_side_effects=True, vmem_limit_bytes=mib * MIB
    )


def dma(count):
    return pltpu.SemaphoreType.DMA((count,))


def forward(*operands):
    return pl.pallas_call(
        forward_kernel,
        name="forward",
        out_shape=(
            shape(TWO5 + (24, 16, 128)),
            shape((4, D, 768)),
            shape((D, D)),
            shape((D, 2048)),
            shape((D, 1024)),
            shape((2, 2, TOK, D)),
            shape((1024, 1024)),
            shape((D, TOK)),
            shape((D, TOK)),
            shape((TOK, D), F32),
            shape((8, D), F32),
            shape((2, 1024, 1024)),
            shape((1024, 1024)),
            shape((2, 2, TOK, D)),
        ),
        in_specs=[ANY] * 3 + [VMEM, ANY] + [VMEM] * 7,
        out_specs=[ANY] * 14,
        scratch_shapes=[
            vmem(TWO6 + (6, 5, 16, 128)),
            vmem(TWO5 + (2, 24, 16, 128)),
            vmem(TWO5 + (24, 16, 128)),
            vmem((4, D, 768)),
            vmem((D, D)),
            vmem((D, 2048)),
            vmem((8, D), F32),
            vmem((TOK, D)),
            vmem((1024, 1024)),
            vmem((TOK, 2048)),
            vmem((TOK, D)),
            vmem((TOK, D), F32),
            vmem((2, 2, TOK, D)),
            vmem((512, 1024)),
            vmem((2, 512, 1024)),
            vmem((TOK, TOK), F32),
            vmem((2, D, TOK)),
            vmem((D, 1024)),
            vmem((1024, 1024)),
            vmem((2, TOK, D)),
            dma(140),
            dma(140),
            dma(4),
            dma(20),
        ],
        compiler_params=params(0, 63),
    )(*operands)


def backward(*operands):
    return pl.pallas_call(
        backward_kernel,
        name="backward",
        out_shape=(
            shape((2, 3, 5, 16, 128), F32),
            shape((4, 2, 6, 16, 128), F32),
            shape((24, 16, 128), F32),
            shape((TOK, D)),
            shape((TOK, D), F32),
            shape(TWO6 + (6, 5, 16, 128)),
            shape(TWO5 + (2, 24, 16, 128)),
            shape(TWO5 + (24, 16, 128)),
            shape((3, D, 1024)),
            shape((6, TOK, D)),
        ),
        in_specs=[ANY] + [VMEM] * 8 + [ANY] * 14,
        out_specs=[VMEM] * 3 + [ANY] * 7,
        scratch_shapes=[
            vmem((D, 1024)),
            vmem((2, 2, TOK, D)),
            vmem((1024, 1024)),
            vmem((2, 1024, 1024)),
            vmem((2, 384, D)),
            vmem((2, 256, 2048)),
            vmem(TWO5 + (2, 24, 16, 128)),
            vmem((5,) + TWO4 + (2, 5, 16, 128)),
            vmem(TWO5 + (24, 16, 128)),
            vmem((5,) + TWO4 + (7, 16, 128)),
            vmem((640, 16, 128)),
            vmem(TWO6 + (6, 5, 16, 128)),
            vmem((6,) + TWO5 + (5, 16, 128)),
            vmem((2, 384, 1024)),
            vmem((9, TOK, 512)),
            vmem((2, D, TOK)),
            vmem((TOK, D), F32),
            vmem((TOK, D), F32),
            vmem((2, 2, TOK, D)),
            vmem((2, TOK, D)),
            vmem((TOK, TOK), F32),
            vmem((8, D), F32),
            vmem((8, D), F32),
            vmem((4, 2, 6, 16, 128)),
            vmem((3, 5, 16, 128)),
            dma(200),
            dma(200),
            dma(4),
            dma(12),
            dma(12),
            dma(1),
            dma(9),
        ],
        compiler_params=params(1, 63),
    )(*operands)


def tables():
    spread = np.zeros((384, 512), np.float32)
    for head in range(4):
        for lane in range(96):
            spread[head * 96 + lane, head * 128 + lane + (16 if lane >= 48 else 0)] = 1
    pick = np.zeros((128, D), np.float32)
    pick[np.arange(D) % 12, np.arange(D)] = 1
    owner = np.zeros((128, D), np.float32)
    order = np.array(GRAY)
    for gx in range(4):
        for gz in range(4):
            for gy in range(4):
                for core in range(2):
                    at = ((gx * 4 + gz) * 4 + gy) * 2 + core
                    device = ((order[gx] * 4 + order[gz]) * 4 + order[gy]) * 2 + core
                    owner[at, device * 12 : device * 12 + 12] = 1
    return [jnp.asarray(table, BF16) for table in (spread, pick, owner)]


def padded_tables(cos_table, sin_table):
    gap = jnp.zeros((TOK, 16), F32)
    cos = jnp.concatenate([cos_table, gap, cos_table, gap], axis=1)
    sin = jnp.concatenate([-sin_table, gap, sin_table, gap], axis=1)
    return cos, sin


def gray(array, axes):
    for axis in axes:
        pieces = jnp.split(array, 4, axis=axis)
        array = jnp.concatenate([pieces[at] for at in GRAY], axis=axis)
    return array


def fold(weight, lead=()):
    columns = weight.shape[-1] // 4
    parts = [weight[..., at * columns : (at + 1) * columns] for at in range(4)]
    return jnp.concatenate(parts, axis=-2)


def unfold(block):
    parts = [block[..., at * 12 : (at + 1) * 12, :] for at in range(4)]
    return jnp.concatenate(parts, axis=-1)


def rank_columns(up):
    split = gray(up.reshape(12, 2, 4, 4, 4, 2, 32), (2, 3, 4)).reshape(12, 2, 4, 4, 2, 2, 2, 32)
    return split.transpose(5, 6, 0, 1, 2, 3, 4, 7).reshape(4, 12, 2048)


def natural_columns(pieces):
    split = pieces.reshape(2, 2, 12, 2, 4, 4, 2, 32).transpose(2, 3, 4, 5, 6, 0, 1, 7)
    return gray(split.reshape(12, 2, 4, 4, 4, 2, 32), (2, 3, 4)).reshape(12, 8192)


def tiled(block):
    count = block.shape[-1] // 128
    return jnp.stack([block[..., 128 * at : 128 * at + 128] for at in range(count)], axis=-3)


def untiled(tiles):
    return jnp.concatenate([tiles[..., at, :, :] for at in range(tiles.shape[-3])], axis=-1)


def layout(segment_row):
    length = segment_row.shape[0]
    places = jnp.arange(length, dtype=jnp.int32)
    same_doc = segment_row[:, None] == segment_row[None, :]
    starts = jnp.min(jnp.where(same_doc, places[None, :], length), axis=1)
    offsets = (places - starts).astype(jnp.float32)
    allowed = jnp.logical_and(same_doc, places[None, :] <= places[:, None])
    exponents = jnp.arange(0, HD, 2, dtype=jnp.float32) / HD
    angles = offsets[:, None] * (THETA ** (-exponents))[None, :]
    return (allowed, jnp.cos(angles), jnp.sin(angles))


def adamw_step(weight, moment_one, moment_two, gradient, rate, decay):
    first_new = BETA_ONE * moment_one + (1.0 - BETA_ONE) * gradient
    second_new = BETA_TWO * moment_two + (1.0 - BETA_TWO) * gradient * gradient
    unbiased_one = first_new / (1.0 - BETA_ONE**STEP)
    unbiased_two = second_new / (1.0 - BETA_TWO**STEP)
    weight_new = weight - rate * (
        unbiased_one / (jnp.sqrt(unbiased_two) + ADAM_EPSILON) + decay * weight
    )
    return (weight_new, first_new, second_new)


def body(
    tokens_in,
    cotangent,
    segment_ids,
    proj_qkv,
    proj_out,
    proj_up,
    proj_down,
    norm_gains,
    first_qkv,
    first_out,
    first_up,
    first_down,
    first_gains,
    second_qkv,
    second_out,
    second_up,
    second_down,
    second_gains,
):
    masters = (proj_qkv, proj_out, proj_up, proj_down, norm_gains)
    low_qkv, low_out, low_up, low_down, low_gains = (part.astype(BF16) for part in masters)
    qkv_tiles = tiled(fold(low_qkv))
    gain_tile = jnp.pad(low_gains.T, ((0, 46), (0, 116)))
    att_tiles = jnp.concatenate([qkv_tiles[:5], tiled(fold(low_out)), qkv_tiles[5:], gain_tile[None]], axis=0)
    att_units = att_tiles.reshape(2, 5, 3, 16, 128).transpose(0, 2, 1, 3, 4)
    up_tiles = tiled(fold(rank_columns(low_up))).reshape(4, 2, 2, 3, 16, 128)
    up_units = up_tiles.transpose(0, 1, 3, 2, 4, 5).reshape(4, 2, 6, 16, 128)
    down_units = low_down.reshape(2, 16, 12, 128).transpose(2, 0, 1, 3).reshape(24, 16, 128)
    _, cos_table, sin_table = layout(segment_ids)
    cos, sin = padded_tables(cos_table, sin_table)
    spread, pick, owner = tables()
    seg_col, seg_row = segment_ids.reshape(TOK, 1), segment_ids.reshape(1, TOK)
    (
        down_all, wq, wo, wgu, n2t, dy_all, heads, a_t, n1_t, middle, gains, gate_up, z_t, y_part,
    ) = forward(
        att_units, up_units, down_units, tokens_in, cotangent, seg_col, seg_row, cos, sin, spread, pick, owner
    )
    att_sum, up_sum, down_sum, block_output, input_grad, *_ = backward(
        tokens_in, cos, sin, seg_col, seg_row, spread, pick, owner, gains, cotangent,
        down_all, wq, wo, wgu, n2t, dy_all, heads, a_t, n1_t, middle, gate_up, z_t, y_part,
    )
    att_sum = att_sum.transpose(0, 2, 1, 3, 4).reshape(10, 48, 128)
    up_sum = up_sum.reshape(4, 2, 3, 2, 16, 128).transpose(0, 1, 3, 2, 4, 5).reshape(4, 4, 48, 128)
    down_sum = down_sum.reshape(12, 2, 16, 128).transpose(1, 2, 0, 3).reshape(32, 1536)
    shard_grads = (
        unfold(untiled(jnp.concatenate([att_sum[:5], att_sum[8:9]], axis=0))),
        unfold(untiled(att_sum[5:8])),
        natural_columns(unfold(untiled(up_sum))),
        down_sum,
        att_sum[9, :2, :12].T,
    )
    firsts = (first_qkv, first_out, first_up, first_down, first_gains)
    seconds = (second_qkv, second_out, second_up, second_down, second_gains)
    updated = [
        adamw_step(
            masters[number],
            firsts[number],
            seconds[number],
            shard_grads[number],
            RATES[number],
            DECAYS[number],
        )
        for number in range(5)
    ]
    return (
        block_output,
        input_grad,
        *(update[0] for update in updated),
        *(update[1] for update in updated),
        *(update[2] for update in updated),
    )


def solution(mesh):
    rows = P("fsdp", None)
    return jax.shard_map(
        body,
        mesh=mesh,
        in_specs=(rows, rows, P("fsdp")) + (rows,) * 15,
        out_specs=(rows,) * 17,
        check_vma=False,
    )
```

```python
import functools
import math

import jax
import jax.numpy as jnp
import numpy as np
from jax import lax
from jax.experimental import pallas as pl
from jax.experimental.pallas import tpu as pltpu
from jax.sharding import PartitionSpec as P

H = 16
KVH = 8
HD = 96
FF = 4096
STEP = 10
D = 1536
TOK = 256


EPSILON = 1e-05
THETA = 100000.0
BETA_ONE = 0.9
BETA_TWO = 0.95
ADAM_EPSILON = 1e-08
RATES = (0.08, 0.3, 0.08, 0.05, 1.0)
DECAYS = (0.1, 0.1, 0.1, 0.1, 0.0)
MASKED = -1e30

MESH = pl.DeviceIdType.MESH
BF16 = jnp.bfloat16
F32 = jnp.float32
MIB = 1024 * 1024
LAG = 3

CUBE = ("xb", "xa", "zb", "za", "yb", "ya")
LINKS = ("xa", "xb", "za", "zb", "ya", "yb")
QUAD_LINKS = ("xa", "xb", "za", "zb", "yb")
GRAY = (0, 1, 3, 2)
FOUR = ((0, 1, 2, 3), (2, 3, 0, 1))


class Place:
    def __init__(self):
        me = lax.axis_index("fsdp")
        self.me = me
        self.c = lax.rem(me, 2)
        self.y = lax.rem(me // 2, 4)
        self.z = lax.rem(me // 8, 4)
        self.x = me // 32
        self.bit = {"c": self.c}
        for name in "xyz":
            at = getattr(self, name)
            self.bit[name + "b"] = at // 2
            self.bit[name + "a"] = lax.rem(at + at // 2, 2)

    def partner(self, *dims):
        at = {"x": self.x, "y": self.y, "z": self.z, "c": self.c}
        for dim in dims:
            name = dim[0]
            if dim == "c":
                at["c"] = 1 - at["c"]
            elif dim[1] == "a":
                at[name] = at[name] + 1 - 2 * lax.rem(at[name], 2)
            else:
                at[name] = 3 - at[name]
        return ((at["x"] * 4 + at["z"]) * 4 + at["y"]) * 2 + at["c"]


def greet(devices):
    barrier = pltpu.get_barrier_semaphore()
    for device in devices:
        pl.semaphore_signal(barrier, inc=1, device_id=(device,), device_id_type=MESH)
    pl.semaphore_wait(barrier, len(devices))


class Sems:
    def __init__(self, send, recv):
        self.send, self.recv, self.used = send, recv, 0

    def copy(self, src, dst, device):
        at = self.used
        self.used += 1
        assert at < self.send.shape[0]
        return pltpu.make_async_remote_copy(
            src_ref=src,
            dst_ref=dst,
            send_sem=self.send.at[at],
            recv_sem=self.recv.at[at],
            device_id=(device,),
            device_id_type=MESH,
        )


def spot(place, dims, done=(), flip=None):
    return tuple(
        pl.ds(0, 2) if dim in done else (1 - place.bit[dim] if dim == flip else place.bit[dim])
        for dim in dims
    )


def rotated(links, by):
    return links[by:] + links[:by]


UP_PARTS = ((0, 5), (5, 5), (10, 5), (15, 5), (20, 4))
DOWN_PARTS = ((0, 4), (4, 4), (8, 5), (13, 4), (17, 7))
TILES = ((0, 2, 0, 0, 0), (2, 2, 0, 2, 0), (4, 1, 0, 4, 0), (5, 1, 1, 3, 0), (6, 2, 1, 0, 1), (8, 1, 1, 2, 1))


class Gather:
    def __init__(self, place, sems, ref, dims, links, rotation, cut):
        self.place, self.sems, self.ref, self.dims, self.cut = place, sems, ref, dims, cut
        self.order, self.copies = rotated(links, rotation), []

    def step(self, number):
        if number > 0:
            self.copies[number - 1].wait_recv()
        if number < len(self.order):
            view = self.ref.at[spot(self.place, self.dims, self.order[:number]) + self.cut]
            copy = self.sems.copy(view, view, self.place.partner(self.order[number]))
            copy.start()
            self.copies.append(copy)

    def end(self):
        for copy in self.copies:
            copy.wait_send()


def each_block(place, dims, free, whole, visit):
    looped = tuple(dim for dim in free if dim not in whole)
    count = 2 ** len(looped)

    def at(i):
        index = []
        weight = count
        for dim in dims:
            if dim in whole:
                index.append(slice(None))
            elif dim in looped:
                weight //= 2
                index.append(lax.rem(i // weight, 2))
            else:
                index.append(place.bit[dim])
        return tuple(index)

    if count == 1:
        visit(at(0))
    else:
        pl.loop(0, count)(lambda i: visit(at(i)))


class Scatter:
    def __init__(self, place, sems, ref, far, got, dims, links, rotation, cuts, cut, counts):
        self.place, self.sems, self.ref, self.far, self.got = place, sems, ref, far, got
        self.dims, self.cut, self.counts = dims, cut, counts
        self.order = tuple(reversed(rotated(links, rotation)))
        self.rest = tuple(dim for dim in dims if dim != self.order[0])
        link, free = self.order[0], self.order[1:]
        there = spot(place, dims, free, flip=link)
        here = spot(place, dims, free)
        self.firsts = [sems.copy(ref.at[there + at], far.at[here + at], place.partner(link)) for at in cuts]
        self.size = math.prod(counts) * 2 ** len(free)
        self.copies = [None]

    def prepare(self, number):
        link = self.order[number]
        free = self.order[number + 1 :]
        src = self.ref.at[spot(self.place, self.dims, free, flip=link) + self.cut]
        dst = self.got.at[spot(self.place, self.rest, free)]
        self.copies.append(self.sems.copy(src, dst, self.place.partner(link)))

    def fetch(self, stage, sem):
        for copy in self.firsts:
            copy.wait_recv()
        link, free = self.order[0], self.order[1:]
        here = self.far.at[spot(self.place, self.dims, free, flip=link) + self.cut]
        self.stage = stage.reshape(*(2,) * len(free), *self.counts, 16, 128)
        self.staged = pltpu.make_async_copy(here, self.stage, sem)
        self.staged.start()

    def add(self, number):
        link = self.order[number]
        free = tuple(dim for dim in self.dims if dim in self.order[number + 1 :])
        whole = free[-2:]

        def visit(index):
            bits = dict(zip(self.dims, index))
            own = index + self.cut
            if number == 0:
                other = self.stage[tuple(bits[dim] for dim in self.rest)]
            else:
                other = self.got[tuple(1 - bits[dim] if dim == link else bits[dim] for dim in self.rest)]
            self.ref[own] = (self.ref[own].astype(F32) + other.astype(F32)).astype(BF16)

        each_block(self.place, self.dims, free, whole, visit)

    def step(self, number):
        if number == 1:
            self.staged.wait()
        elif number > 1:
            self.copies[number - 1].wait_recv()
        if number > 0:
            self.add(number - 1)
        if number < len(self.order):
            self.prepare(number)
            self.copies[number].start()

    def end(self):
        for copy in self.firsts + self.copies[1:]:
            copy.wait_send()


def first_adds(jobs, stage, sems):
    at = 0
    while at < len(jobs):
        batch, units = [], 0
        while at < len(jobs) and len(batch) < 9:
            if units + jobs[at].size > 640:
                break
            jobs[at].fetch(stage.at[pl.ds(units, jobs[at].size)], sems.at[len(batch)])
            batch.append(jobs[at])
            units += jobs[at].size
            at += 1
        for job in batch:
            job.step(1)


def natural_group(g):
    xb, xa = lax.rem(g // 16, 2), lax.rem(g // 8, 2)
    zb, za = lax.rem(g // 4, 2), lax.rem(g // 2, 2)
    yb = lax.rem(g, 2)
    x = 2 * xb + lax.rem(xa + xb, 2)
    z = 2 * zb + lax.rem(za + zb, 2)
    return (xb, xa, zb, za, yb), (x * 4 + z) * 2 + yb


def dot(left, right):
    return lax.dot_general(left, right, (((1,), (0,)), ((), ())), preferred_element_type=F32)


def dot_t(left, right):
    return lax.dot_general(left, right, (((1,), (1,)), ((), ())), preferred_element_type=F32)


def cols(i, width):
    return pl.ds(pl.multiple_of(i * width, width), width)


def head_pad(value, spread):
    high = value.astype(BF16)
    low = (value - high.astype(F32)).astype(BF16)
    return dot(high, spread) + dot(low, spread)


def turn(value, cos, sin):
    return value * cos + pltpu.roll(value, 64, 1) * sin


def mask_bias(seg_col, seg_row):
    rows = lax.broadcasted_iota(jnp.int32, (TOK, TOK), 0)
    columns = lax.broadcasted_iota(jnp.int32, (TOK, TOK), 1)
    allowed = jnp.logical_and(seg_col == seg_row, columns <= rows)
    return jnp.where(allowed, 0.0, MASKED).astype(F32)


def row_norm(value):
    return lax.rsqrt(jnp.mean(value * value, axis=-1, keepdims=True) + EPSILON)


def each_rows(step, visit, rows=TOK):
    @pl.loop(0, rows // step)
    def _(i):
        visit(pl.ds(pl.multiple_of(i * step, step), step))


def open_quarter(block, yb, quarter):
    pieces = [block[48 * at + 12 * quarter : 48 * at + 12 * quarter + 12] for at in FOUR[yb]]
    return jnp.concatenate(pieces, axis=0)


def sigmoid(value):
    return 1.0 / (1.0 + jnp.exp(-value))


def dot_first(left, right):
    return lax.dot_general(left, right, (((0,), (0,)), ((), ())), preferred_element_type=F32)


class Outs:
    def __init__(self, sems):
        self.sems, self.copies, self.ended = sems, [], 0

    def put(self, src, dst):
        assert len(self.copies) < self.sems.shape[0]
        copy = pltpu.make_async_copy(src, dst, self.sems.at[len(self.copies)])
        copy.start()
        self.copies.append(copy)

    def end(self):
        for copy in self.copies[self.ended :]:
            copy.wait()
        self.ended = len(self.copies)


def quad_of(place):
    return {(0, 1): place.partner("c"), (1, 0): place.partner("ya"), (1, 1): place.partner("ya", "c")}


def forward_kernel(
    att_in, up_in, down_in, x, dy, bias, cos, sin, spread, pick, owner,
    down_out, wq_out, wo_out, wgu_out, n2t_out, dy_all, q_out, at_out, n1t_out, m_out, g_out, gu_out, zt_out,
    y_out,
    att, up, down, wq, wo, wgu, gains, n1, q, apad, a, m, n2_all, z, gu, turned, n2t, zt, y,
    send, recv, local, out_sem,
):
    place = Place()
    sems = Sems(send, recv)
    outs = Outs(out_sem)
    quad = quad_of(place)
    sibling, across = quad[0, 1], quad[1, 0]
    greet([place.partner(link) for link in LINKS] + [quad[0, 1], quad[1, 1]])
    dims5 = CUBE[:5]
    home6 = spot(place, CUBE)
    home5 = spot(place, dims5)
    ya, c = place.bit["ya"], place.c
    rank = 2 * ya + c
    mine = pl.ds(3 * c, 3)
    six = pl.ds(pl.multiple_of(6 * rank, 2), 6)
    swap = sems.copy(att_in.at[1 - c], att.at[home6 + (mine,)], sibling)
    swap.start()
    starts = [
        pltpu.make_async_copy(att_in.at[c], att.at[home6 + (mine,)], local.at[0]),
        pltpu.make_async_copy(down_in, down.at[home5], local.at[1]),
        pltpu.make_async_copy(up_in.at[rank], up.at[home5 + (pl.ds(0, 2), six)], local.at[2]),
    ]
    for copy in starts:
        copy.start()
    scatter = []
    for (dya, dc), device in quad.items():
        to = 2 * (1 - ya if dya else ya) + (1 - c if dc else c)
        copy = sems.copy(up_in.at[to], up.at[home5 + (pl.ds(0, 2), six)], device)
        copy.start()
        scatter.append(copy)
    for copy in starts:
        copy.wait()
    swap.wait()
    first = [Gather(place, sems, att, CUBE, LINKS, by, (by,)) for by in range(6)]
    ups = [
        Gather(place, sems, up, dims5, QUAD_LINKS, by, (pl.ds(0, 2), pl.ds(*at)))
        for by, at in enumerate(UP_PARTS)
    ]
    downs = [Gather(place, sems, down, dims5, QUAD_LINKS, by, (pl.ds(*at),)) for by, at in enumerate(DOWN_PARTS)]
    second = ups + downs
    for number in range(7):
        for job in first:
            job.step(number)
        if number == 0:
            for copy in scatter:
                copy.wait()
        if number >= LAG:
            for job in second:
                job.step(number - LAG)
    dy_near = sems.copy(dy, dy_all.at[ya, c], sibling)
    dy_near.start()
    dy_far = sems.copy(dy, dy_all.at[ya, c], across)
    dy_far.start()

    wide, narrow = pl.ds(0, 640), pl.ds(640, 128)
    shared = {0: [], 1: []}
    for at in range(4):
        rows = pl.ds(GRAY[at] * 384, 384)
        for core, refs in ((0, [wq.at[:, rows, wide]]), (1, [wq.at[:, rows, narrow], wo.at[rows]])):
            shared[core].append([sems.copy(ref, ref, sibling) for ref in refs])
    gain_share = sems.copy(gains, gains, sibling)

    @pl.when(c == 1)
    def _():
        tiles = jnp.stack([att[..., 3 * core, 4, :, :].reshape(64, 16, 128) for core in range(2)], axis=1)
        tiles = tiles.reshape(128, 16, 128).astype(F32)
        lines = lax.broadcasted_iota(jnp.int32, (128, 16, 128), 1)
        for number in range(2):
            line = jnp.sum(jnp.where(lines == number, tiles, 0.0), axis=1).astype(BF16)
            vector = jnp.sum(dot(line, pick[...]) * owner[...].astype(F32), axis=0, keepdims=True)
            gains[number : number + 1, :] = vector
        gains[2:8, :] = jnp.zeros((6, D), F32)
        gain_share.start()

    for at in range(4):

        @pl.loop(0, 8)
        def _(part):
            bits, n = natural_group(at * 8 + part)
            rows = pl.ds(pl.multiple_of(n * 48, 16), 48)
            block = jnp.concatenate([att[bits][:, :, k].reshape(192, 128) for k in range(5)], axis=1)
            for yb in range(2):

                @pl.when(jnp.logical_and(bits[4] == yb, c == 0))
                def _():
                    for quarter in range(4):
                        wq[quarter, rows, 0:640] = open_quarter(block, yb, quarter)

                @pl.when(jnp.logical_and(bits[4] == yb, c == 1))
                def _():
                    for quarter in range(4):
                        piece = open_quarter(block[:, :512], yb, quarter)
                        wq[quarter, rows, 640:768] = piece[:, 384:]
                        wo[rows, 384 * quarter : 384 * quarter + 384] = piece[:, :384]

        for core in range(2):

            @pl.when(c == core)
            def _():
                for copy in shared[core][at]:
                    copy.start()


    @pl.when(c == 0)
    def _():
        gain_share.wait_recv()

    def norm_one(at):
        value = x[at, :].astype(F32)
        n1[at, :] = (value * row_norm(value) * gains[0:1, :]).astype(BF16)

    each_rows(64, norm_one)
    for core in range(2):

        @pl.when(c == core)
        def _():
            for at in range(4):
                for copy in shared[1 - core][at]:
                    copy.wait_recv()

    outs.put(wq, wq_out)
    outs.put(wo, wo_out)

    def heads(i, rotated_too):
        value = dot(n1[...], wq[i // 2, :, cols(lax.rem(i, 2), 384)])
        padded = head_pad(value, spread[...])
        for at in range(4):
            head = padded[:, 128 * at : 128 * at + 128]
            if rotated_too:
                head = turn(head, cos[...], sin[...])
            lanes = pl.ds(pl.multiple_of(lax.rem(i, 2) * 512 + 128 * at, 128), 128)
            q[cols(i // 2, 256), lanes] = head.astype(BF16)

    pl.loop(0, 6)(lambda i: heads(i, True))
    pl.loop(6, 8)(lambda i: heads(i, False))
    for job in ups:
        job.step(4)
    outs.put(q, q_out)

    own = n2_all.at[ya, c]
    near, far = [], []
    for half in range(2):
        start, seen = 128 * half, 128 * half + 128
        rows = pl.ds(start, 128)

        @pl.loop(0, 8)
        def _(j):
            pair = q[pl.ds(pl.multiple_of(j // 4 * 256 + start, 128), 128), cols(lax.rem(j, 4), 256)]
            both = jnp.concatenate([pair[:, :128], pair[:, 128:]], axis=0)
            key = q[512 : 512 + seen, cols(j, 128)]
            value = q[768 : 768 + seen, cols(j, 128)]
            mask = bias[rows, 0:seen]
            scores = dot_t(both, key) * (1.0 / math.sqrt(HD)) + jnp.concatenate([mask, mask], axis=0)
            exponent = jnp.exp(scores - jnp.max(scores, axis=-1, keepdims=True))
            weights = exponent / jnp.sum(exponent, axis=-1, keepdims=True)
            result = dot(weights.astype(BF16), value).astype(BF16)
            for at in range(2):
                lanes = pl.ds(pl.multiple_of(j * 256 + 128 * at, 128), 128)
                apad[rows, lanes] = result[128 * at : 128 * at + 128]

        if half == 1:
            for job in downs:
                job.step(4)

        @pl.loop(0, 4)
        def _(i):
            a[rows, cols(i, 384)] = dot_t(apad[rows, cols(i, 512)], spread[...]).astype(BF16)

        @pl.loop(0, 3)
        def _(i):
            m[rows, cols(i, 512)] = x[rows, cols(i, 512)].astype(F32) + dot(a[rows, :], wo[:, cols(i, 512)])

        def norm_two(i):
            at = pl.ds(pl.multiple_of(start + i * 64, 64), 64)
            value = m[at, :]
            own[at, :] = (value * row_norm(value) * gains[1:2, :]).astype(BF16)

        pl.loop(0, 2)(norm_two)
        near.append(sems.copy(own.at[rows], own.at[rows], sibling))
        near[half].start()
        far.append(sems.copy(own.at[rows], own.at[rows], across))
        far[half].start()
    outs.put(m, m_out)
    outs.put(gains, g_out)

    for job in ups:
        job.step(5)

    @pl.loop(0, 32)
    def _(g):
        bits, n = natural_group(g)
        rows = pl.ds(pl.multiple_of(n * 48, 16), 48)
        block = jnp.concatenate(
            [up[bits + (k // 2,)].reshape(12, 2, 16, 128)[:, k % 2].reshape(192, 128) for k in range(4)], axis=1
        )
        for yb in range(2):

            @pl.when(bits[4] == yb)
            def _():
                for quarter in range(4):
                    wgu[rows, 512 * quarter : 512 * quarter + 512] = open_quarter(block, yb, quarter)

    outs.put(wgu, wgu_out)
    for job in downs:
        job.step(5)
    outs.put(down, down_out)
    for copy in near:
        copy.wait_recv()

    def mlp(pair):
        rows = cols(pair, 512)

        @pl.loop(0, 4)
        def _(i):
            left = n2_all[pair].reshape(512, D)
            gate = dot(left, wgu[:, cols(i, 256)])
            upward = dot(left, wgu[:, cols(i + 4, 256)])
            hidden = gate * sigmoid(gate) * upward
            z[:, cols(i, 256)] = hidden.astype(BF16)
            gu[0, :, cols(i, 256)] = gate.astype(BF16)
            gu[1, :, cols(i, 256)] = upward.astype(BF16)

        outs.put(gu, gu_out.at[:, rows])

        @pl.loop(0, 6)
        def _(i):
            right = jnp.concatenate(
                [down[..., pl.ds(4 * i + 2 * at, 2), :, :].reshape(1024, 128) for at in range(2)], axis=1
            )
            y[:, :, cols(i, 256)] = dot(z[...], right).astype(BF16).reshape(2, TOK, 256)

        outs.put(y, y_out.at[pair])

        @pl.loop(0, 6)
        def _(i):
            n2t[cols(i, 256), rows] = jnp.transpose(n2_all[pair, :, :, cols(i, 256)].reshape(512, 256))

        outs.put(n2t.at[:, rows], n2t_out.at[:, rows])

        @pl.loop(0, 4)
        def _(i):
            zt[cols(i, 256), rows] = jnp.transpose(z[:, cols(i, 256)])

        outs.put(zt.at[:, rows], zt_out.at[:, rows])

    def pass_on(half):
        far[half].wait_recv()
        there = n2_all.at[1 - ya, c, pl.ds(128 * half, 128)]
        copy = sems.copy(there, there, sibling)
        copy.start()
        return copy

    mlp(ya)
    onward = [pass_on(0)]

    @pl.loop(0, 6)
    def _(i):
        turned[0, cols(i, 256), :] = jnp.transpose(n1[:, cols(i, 256)])
        turned[1, cols(i, 256), :] = jnp.transpose(a[:, cols(i, 256)])

    outs.put(turned.at[0], n1t_out)
    outs.put(turned.at[1], at_out)
    dy_far.wait_recv()
    dy_onward = sems.copy(dy_all.at[1 - ya, c], dy_all.at[1 - ya, c], sibling)
    dy_onward.start()
    onward.append(pass_on(1))
    for copy in onward:
        copy.wait_recv()
    outs.end()
    mlp(1 - ya)
    for copy in near + far + onward:
        copy.wait_send()
    dy_near.wait()
    dy_far.wait_send()
    dy_onward.wait()
    for core in range(2):

        @pl.when(c == core)
        def _():
            for at in range(4):
                for copy in shared[core][at]:
                    copy.wait_send()

    @pl.when(c == 1)
    def _():
        gain_share.wait_send()

    for job in first + second:
        job.end()
    outs.end()


def backward_kernel(
    x, cos, sin, bias, spread, pick, owner, gains, cotangent,
    down_in, wq_in, wo_in, wgu_in, n2t_in, dy_in, q_in, at_in, n1t_in, m_in, gu_in, zt_in, y_in,
    att_out, up_out, down_out, block_out, grad_out,
    far_att, far_up, far_down, land, quad_got,
    n2t, dy, zt, gu, wo_slots, wgu_slots, g_up, got_up, g_down, got_down, stage, g_att, got_att,
    dw, rt, lhs, dm, dn1, p, t, dg, dg_got, up_land, att_land,
    send, recv, local, slot_sem, load_sem, out_sem, stage_sem,
):
    place = Place()
    sems = Sems(send, recv)
    outs = Outs(out_sem)
    quad = quad_of(place)
    sibling, across = quad[0, 1], quad[1, 0]
    greet([place.partner(link) for link in LINKS] + [quad[0, 1], quad[1, 1]])
    dims5 = CUBE[:5]
    home6 = spot(place, CUBE)
    home5 = spot(place, dims5)
    ya, c = place.bit["ya"], place.c
    rank = 2 * ya + c
    loads = {}

    def load(name, src, dst):
        assert len(loads) < load_sem.shape[0]
        copy = pltpu.make_async_copy(src, dst, load_sem.at[len(loads)])
        copy.start()
        loads[name] = copy

    load("zt", zt_in, zt)
    load("dy", cotangent, dy.at[ya, c])
    load("dy1", dy_in.at[ya, 1 - c], dy.at[ya, 1 - c])
    load("dy2", dy_in.at[1 - ya], dy.at[1 - ya])
    load("gu", gu_in, gu)

    wd_slots = [stage.at[pl.ds(192 * slot, 192)].reshape(2, 2, 2, 24, 16, 128) for slot in range(2)]

    def fetch_wd(i):
        slot = i % 2
        whole = (pl.ds(0, 2),) * 3 + (pl.ds(0, 24), pl.ds(0, 16), pl.ds(0, 128))
        return pltpu.make_async_copy(down_in.at[(i // 2, i % 2) + whole], wd_slots[slot], slot_sem.at[slot])

    fetch_wd(0).start()
    fetch_wd(1).start()

    y_away = sems.copy(y_in.at[1 - ya, 1 - c], quad_got.at[0], sibling)
    y_away.start()
    y_near = sems.copy(y_in.at[ya, 1 - c], quad_got.at[1], sibling)
    y_near.start()

    up_jobs = [
        Scatter(
            place, sems, g_up, far_up, got_up.at[by, :, :, :, :, :, pl.ds(0, at[1])], dims5, QUAD_LINKS, by,
            [(pair, pl.ds(*at)) for pair in range(2)], (pl.ds(0, 2), pl.ds(*at)), (2, at[1]),
        )
        for by, at in enumerate(UP_PARTS)
    ]
    down_jobs = [
        Scatter(
            place, sems, g_down, far_down, got_down.at[by, :, :, :, :, pl.ds(0, at[1])], dims5, QUAD_LINKS, by,
            [(pl.ds(*at),)], (pl.ds(*at),), (at[1],),
        )
        for by, at in enumerate(DOWN_PARTS)
    ]
    att_jobs = [
        Scatter(
            place, sems, g_att, far_att, got_att.at[by], CUBE, LINKS, by,
            [(by, pl.ds(0, 2)), (by, pl.ds(2, 2)), (by, pl.ds(4, 1))], (by, pl.ds(0, 5)), (5,),
        )
        for by in range(6)
    ]
    mlp_jobs = up_jobs + down_jobs

    for name in ("zt", "dy", "dy1", "dy2"):
        loads[name].wait()
    for i in range(6):

        @pl.loop(0, 4)
        def _(at):
            right = dy[:, :, :, pl.ds(256 * i, 256)].reshape(1024, 256)
            value = dot(zt[cols(at, 256), :], right).astype(BF16)
            for part in range(2):
                piece = value[:, 128 * part : 128 * part + 128].reshape(2, 2, 2, 2, 16, 128)
                g_down[at // 2, lax.rem(at, 2), :, :, :, pl.ds(4 * i + 2 * part, 2)] = piece

        for job, (start, count) in zip(down_jobs, DOWN_PARTS):
            if 4 * i < start + count <= 4 * i + 4:
                job.firsts[0].start()

    def fetch_wo(i):
        slot = i % 2
        return pltpu.make_async_copy(wo_in.at[pl.ds(384 * i, 384)], wo_slots.at[slot], slot_sem.at[4 + slot])

    def fetch_wgu(i, slot):
        return pltpu.make_async_copy(wgu_in.at[cols(i, 256)], wgu_slots.at[slot], slot_sem.at[2 + slot])

    fetch_wgu(0, 0).start()
    fetch_wgu(1, 1).start()
    fetch_wo(0).start()
    fetch_wo(1).start()
    loads["gu"].wait()
    load("n2t", n2t_in, n2t)
    load("m", m_in, dm)
    load("n1t", n1t_in, lhs.at[0])
    load("at", at_in, lhs.at[1])
    for i in range(4):
        fetch_wd(i).wait()

        @pl.loop(0, 2)
        def _(pair):
            rows = cols(pair, 512)
            lanes = pl.ds(256 * i, 256)
            right = jnp.concatenate(
                [wd_slots[i % 2][:, :, :, 2 * at : 2 * at + 2].reshape(256, 128) for at in range(12)], axis=1
            )
            dz = dot_t(dy[pair].reshape(512, D), right)
            gate = gu[0, rows, lanes].astype(F32)
            upward = gu[1, rows, lanes].astype(F32)
            sg = sigmoid(gate)
            gu[0, rows, lanes] = (dz * upward * sg * (1.0 + gate * (1.0 - sg))).astype(BF16)
            gu[1, rows, lanes] = (dz * gate * sg).astype(BF16)

        if i < 2:
            fetch_wd(i + 2).start()

    aways, fars = [], []

    def mix(i):
        lanes = pl.ds(256 * i, 256)
        aways[i].wait_recv()

        def visit(at):
            total = p[1 - ya, c, at, lanes].astype(F32) + t[1, at, lanes].astype(F32)
            p[1 - ya, c, at, lanes] = total.astype(BF16)

        each_rows(128, visit)
        fars.append(sems.copy(p.at[1 - ya, c, :, lanes], quad_got.at[5, :, lanes], across))
        fars[i].start()

    for i in range(6):
        slot = i % 2
        lanes = pl.ds(256 * i, 256)
        fetch_wgu(i, slot).wait()

        @pl.loop(0, 2)
        def _(pair):
            rows = cols(pair, 512)
            part = dot_t(gu[0, rows, :], wgu_slots[slot, :, 0:1024])
            part = part + dot_t(gu[1, rows, :], wgu_slots[slot, :, 1024:2048])
            p[pair, :, :, lanes] = part.astype(BF16).reshape(2, TOK, 256)

        if i < 4:
            fetch_wgu(i + 2, slot).start()
        aways.append(sems.copy(p.at[1 - ya, 1 - c, :, lanes], t.at[1, :, lanes], sibling))
        aways[i].start()
        if i > 0:
            mix(i - 1)
    near = sems.copy(p.at[ya, 1 - c], t.at[0], sibling)
    near.start()
    mix(5)

    def fetch(src, dst):
        copy = pltpu.make_async_copy(src, dst, local.at[3])
        copy.start()
        copy.wait()

    def add_into(total, term):
        def visit(at):
            total[at, :] = (total[at, :].astype(F32) + term[at, :].astype(F32)).astype(BF16)

        each_rows(64, visit)

    def fold_into(value, width, at, store):
        zb = lax.rem(at, 2)
        for part in range(4):
            z, yb = part // 2, part % 2
            row = part * 48
            pieces = [
                value[row + 12 * to : row + 12 * to + 12, width * quarter : width * quarter + width]
                for to in FOUR[yb]
                for quarter in range(4)
            ]
            folded = jnp.concatenate(pieces, axis=0).reshape(2, 6, 16, width)
            store((at // 4, lax.rem(at // 2, 2), zb, z + zb * (1 - 2 * z), yb), folded)

    def natural_rows(at):
        x = at // 2
        x = x + lax.rem(x // 2, 2) * (1 - 2 * lax.rem(x, 2))
        return pl.ds(pl.multiple_of(x * 384 + lax.rem(at, 2) * 192, 64), 192)

    loads["n2t"].wait()
    for pair in range(2):

        @pl.loop(0, 8)
        def _(at):
            rows = natural_rows(at)
            right = jnp.concatenate(
                [gu[quarter // 2, :, pl.ds((quarter % 2) * 512 + 256 * pair, 256)] for quarter in range(4)], axis=1
            )
            value = dot(n2t[rows, :], right).astype(BF16)

            def store(index, folded):
                folded = folded.reshape(12, 16, 256)
                halves = jnp.stack([folded[:, :, :128], folded[:, :, 128:]], axis=1)
                g_up[index + (pair,)] = halves.reshape(24, 16, 128)

            fold_into(value, 256, at, store)

        for job in up_jobs:
            job.firsts[pair].start()

    near.wait_recv()
    for copy in fars:
        copy.wait_recv()
    fetch(quad_got.at[5], t.at[1])
    loads["m"].wait()
    load("q", q_in, gu.at[0])
    dg[...] = jnp.zeros((8, D), F32)

    def back_two(at):
        value = dm[at, :]
        r = row_norm(value)
        xh = value * r
        dn = p[ya, c, at, :].astype(F32) + t[0, at, :].astype(F32) + t[1, at, :].astype(F32)
        dg[1:2, :] = dg[1:2, :] + jnp.sum(dn * xh, axis=0, keepdims=True)
        e = dn * gains[1:2, :]
        grad = dy[ya, c, at, :].astype(F32) + r * (e - xh * jnp.mean(xh * e, axis=-1, keepdims=True))
        dm[at, :] = grad
        low = grad.astype(BF16)
        for k in range(3):
            for quarter in range(4):
                start = quarter * 384 + k * 128
                rt[6 + k, at, 128 * quarter : 128 * quarter + 128] = low[:, start : start + 128]

    each_rows(32, back_two)
    load("x", x, dy.at[ya, c])

    y_away.wait_recv()
    load("y0", y_in.at[1 - ya, c], t.at[0])
    load("y1", quad_got.at[0], t.at[1])

    for i in range(4):
        fetch_wo(i).wait()
        left = jnp.concatenate(
            [rt[6 + k, :, 128 * quarter : 128 * quarter + 128] for quarter in range(4) for k in range(3)], axis=1
        )
        da = dot_t(left, wo_slots[i % 2]).astype(BF16)
        zt[256 * (i // 2) : 256 * (i // 2) + 256, 512 * (i % 2) : 512 * (i % 2) + 512] = dot(
            da, spread[...]
        ).astype(BF16)
        if i < 2:
            fetch_wo(i + 2).start()

    tile_copies = {}
    for number, (u, count, core, k, out) in enumerate(TILES):
        for at in range(4):
            lanes = pl.ds(0, 512 * count)
            tile_copies[number, at] = sems.copy(
                dw.at[at % 2, :, lanes], land.at[number % 3, pl.ds(384 * at, 384), lanes], sibling
            )
    sent = {0: [], 1: []}

    def tile_right(u, count):
        return jnp.concatenate(
            [rt[u + at, :, 128 * quarter : 128 * quarter + 128] for quarter in range(4) for at in range(count)], axis=1
        )

    def give(number):
        u, count, owner_core, k, out = TILES[number]
        core = 1 - owner_core

        @pl.when(c == core)
        def _():
            right = tile_right(u, count)
            for at in range(4):
                if len(sent[core]) >= 2:
                    sent[core][-2].wait_send()
                left = lhs[out, 384 * at : 384 * at + 384, :]
                dw[at % 2, :, 0 : 512 * count] = dot(left, right).astype(BF16)
                tile_copies[number, at].start()
                sent[core].append(tile_copies[number, at])

    def land_copy(number):
        lanes = pl.ds(0, 512 * TILES[number][1])
        return pltpu.make_async_copy(land.at[number % 3, :, lanes], n2t.at[:, lanes], local.at[3])

    def take(number):
        u, count, core, k, out = TILES[number]

        @pl.when(c == core)
        def _():
            for at in range(4):
                tile_copies[number, at].wait_recv()
            copy = land_copy(number)
            copy.start()
            copy.wait()

            @pl.loop(0, 8)
            def _(at):
                rows = natural_rows(at)
                value = dot(lhs[out, rows, :], tile_right(u, count)) + n2t[rows, 0 : 512 * count].astype(F32)

                def store(index, folded):
                    for spot_ya in range(2):
                        for part in range(count):
                            piece = folded[spot_ya, :, :, 128 * part : 128 * part + 128]
                            g_att[index + (spot_ya, slice(None), k + part)] = piece

                fold_into(value.astype(BF16), 128 * count, at, store)

            if k + count in (2, 4, 5):
                for job in att_jobs:
                    job.firsts[(k + count) // 2 - 1 if k + count < 5 else 2].start()

    loads["at"].wait()
    loads["n1t"].wait()
    give(4)
    give(5)
    loads["y0"].wait()
    loads["y1"].wait()
    add_into(t.at[0], t.at[1])
    y_far = sems.copy(t.at[0], quad_got.at[2], across)
    y_far.start()
    first_adds(mlp_jobs, stage, stage_sem)
    loads["q"].wait()
    scale = 1.0 / math.sqrt(HD)

    @pl.loop(0, 8)
    def _(j):
        rows, lanes = cols(j // 4, 256), cols(lax.rem(j, 4), 256)
        pair = gu[0, rows, lanes]
        da = zt[rows, lanes]
        key = gu[0, 512:768, cols(j, 128)]
        value = gu[0, 768:1024, cols(j, 128)]
        dk = jnp.zeros((TOK, 128), F32)
        dv = jnp.zeros((TOK, 128), F32)
        for at in range(2):
            query = pair[:, 128 * at : 128 * at + 128]
            grad = da[:, 128 * at : 128 * at + 128]
            scores = dot_t(query, key) * scale + bias[...]
            exponent = jnp.exp(scores - jnp.max(scores, axis=-1, keepdims=True))
            weights = exponent / jnp.sum(exponent, axis=-1, keepdims=True)
            dv = dv + dot_first(weights.astype(BF16), grad)
            dp = dot_t(grad, value)
            ds = weights * (dp - jnp.sum(weights * dp, axis=-1, keepdims=True))
            ds = ds.astype(BF16)
            dq = dot(ds, key) * scale
            dk = dk + dot_first(ds, query)
            here = pl.ds(pl.multiple_of(lax.rem(j, 4) * 256 + 128 * at, 128), 128)
            gu[1, rows, here] = turn(dq, cos[...], -sin[...]).astype(BF16)
        gu[1, 512:768, cols(j, 128)] = turn(dk * scale, cos[...], -sin[...]).astype(BF16)
        gu[1, 768:1024, cols(j, 128)] = dv.astype(BF16)

    for job in mlp_jobs:
        job.step(2)
    @pl.loop(0, 8)
    def _(i):
        padded = gu[1, cols(i // 2, 256), cols(lax.rem(i, 2), 512)]
        flat = dot_t(padded, spread[...]).astype(BF16)
        for part in range(3):
            rt[lax.rem(i, 2) * 3 + part, :, cols(i // 2, 128)] = flat[:, 128 * part : 128 * part + 128]

    for number in (3, 0, 1, 2):
        give(number)
    for job in mlp_jobs:
        job.step(3)
    for number in (0, 1, 2, 4, 5, 3):
        take(number)
    for job in mlp_jobs:
        job.step(4)
    def fetch_wq(i):
        slot = i % 2
        ref = (n2t, zt)[slot]
        return [
            pltpu.make_async_copy(
                wq_in.at[quarter, pl.ds(256 * i, 256)],
                ref.at[pl.ds(256 * quarter, 256), pl.ds(0, 768)],
                slot_sem.at[4 + 4 * slot + quarter],
            )
            for quarter in range(4)
        ]

    for i in range(6):
        for ahead in (0, 1) if i == 0 else (i + 1,):
            if ahead < 6:
                for copy in fetch_wq(ahead):
                    copy.start()
        for copy in fetch_wq(i):
            copy.wait()
        weight = (n2t, zt)[i % 2]
        total = jnp.zeros((TOK, 256), F32)
        for quarter in range(4):
            left = jnp.concatenate([rt[k, :, 128 * quarter : 128 * quarter + 128] for k in range(6)], axis=1)
            total = total + dot_t(left, weight[256 * quarter : 256 * quarter + 256, 0:768])
        dn1[:, 256 * i : 256 * i + 256] = total

    def back_one(at):
        value = dy[ya, c, at, :].astype(F32)
        r = row_norm(value)
        xh = value * r
        dn = dn1[at, :]
        dg[0:1, :] = dg[0:1, :] + jnp.sum(dn * xh, axis=0, keepdims=True)
        e = dn * gains[0:1, :]
        dn1[at, :] = dm[at, :] + r * (e - xh * jnp.mean(xh * e, axis=-1, keepdims=True))

    loads["x"].wait()
    each_rows(32, back_one)
    outs.put(dn1, grad_out)
    dg_copy = sems.copy(dg, dg_got, sibling)

    @pl.when(c == 0)
    def _():
        dg_copy.start()
        dg_copy.wait_send()

    @pl.when(c == 1)
    def _():
        g_att[(slice(None),) * 6 + (slice(None), 4)] = jnp.zeros(TWO6 + (6, 16, 128), BF16)
        dg_copy.wait_recv()
        lines = lax.broadcasted_iota(jnp.int32, (128, 16, 128), 1)
        tiles = jnp.zeros((128, 16, 128), F32)
        for number in range(2):
            vector = dg[number : number + 1, :] + dg_got[number : number + 1, :]
            spread_out = (owner[...].astype(F32) * vector).astype(BF16)
            line = dot_t(spread_out, pick[...])
            tiles = jnp.where(lines == number, line.reshape(128, 1, 128), tiles)
        tiles = tiles.astype(BF16).reshape(TWO7 + (16, 128))
        for core in range(2):
            g_att[(slice(None),) * 6 + (3 * core, 4)] = tiles[:, :, :, :, :, :, core]
        for job in att_jobs:
            job.firsts[2].start()

    for job in mlp_jobs:
        job.step(5)
    last = []
    for (dya, dc), device in quad.items():
        to = 2 * (1 - ya if dya else ya) + (1 - c if dc else c)
        src = g_up.at[home5 + (pl.ds(0, 2), pl.ds(pl.multiple_of(6 * to, 2), 6))]
        copy = sems.copy(src, up_land.at[rank], device)
        copy.start()
        last.append(copy)
    up_out[rank] = g_up[home5 + (slice(None), pl.ds(pl.multiple_of(6 * rank, 2), 6))].astype(F32)
    down_out[...] = g_down[home5].astype(F32)
    first_adds(att_jobs, stage, stage_sem)

    outs.end()
    for copy in aways + fars + [near]:
        copy.wait_send()
    y_far.wait_send()
    y_near.wait_recv()
    y_far.wait_recv()
    load("m2", m_in, dm)
    load("y2", y_in.at[ya, c], t.at[0])
    load("y3", quad_got.at[1], t.at[1])
    load("y4", quad_got.at[2], p.at[0, 0])
    for name in ("m2", "y2", "y3", "y4"):
        loads[name].wait()

    def add_y(at):
        total = dm[at, :] + t[0, at, :].astype(F32) + t[1, at, :].astype(F32) + p[0, 0, at, :].astype(F32)
        t[0, at, :] = total.astype(BF16)

    each_rows(64, add_y)
    outs.put(t.at[0], block_out)
    for number in range(2, 7):
        for job in att_jobs:
            job.step(number)
    att_last = sems.copy(g_att.at[home6 + (pl.ds(3 - 3 * c, 3),)], att_land, sibling)
    att_last.start()
    att_out[c] = g_att[home6 + (pl.ds(3 * c, 3),)].astype(F32)
    for copy in last:
        copy.wait()
    att_last.wait()
    for dya, dc in quad:
        to = 2 * (1 - ya if dya else ya) + (1 - c if dc else c)
        up_out[to] = up_land[to].astype(F32)
    att_out[1 - c] = att_land[...].astype(F32)
    for copy in (y_away, y_near):
        copy.wait_send()
    outs.end()
    for core in range(2):

        @pl.when(c == core)
        def _():
            for copy in sent[core][-2:]:
                copy.wait_send()

    for job in att_jobs + mlp_jobs:
        job.end()


ANY = pl.BlockSpec(memory_space=pl.ANY)
VMEM = pl.BlockSpec(memory_space=pltpu.VMEM)
TWO4 = (2,) * 4
TWO5 = (2,) * 5
TWO6 = (2,) * 6
TWO7 = (2,) * 7


def shape(dims, kind=BF16):
    return jax.ShapeDtypeStruct(dims, kind)


def vmem(dims, kind=BF16):
    return pltpu.VMEM(dims, kind)


def params(number, mib):
    return pltpu.CompilerParams(
        collective_id=number, has_side_effects=True, vmem_limit_bytes=mib * MIB
    )


def dma(count):
    return pltpu.SemaphoreType.DMA((count,))


def forward(*operands):
    return pl.pallas_call(
        forward_kernel,
        name="forward",
        out_shape=(
            shape(TWO5 + (24, 16, 128)),
            shape((4, D, 768)),
            shape((D, D)),
            shape((D, 2048)),
            shape((D, 1024)),
            shape((2, 2, TOK, D)),
            shape((1024, 1024)),
            shape((D, TOK)),
            shape((D, TOK)),
            shape((TOK, D), F32),
            shape((8, D), F32),
            shape((2, 1024, 1024)),
            shape((1024, 1024)),
            shape((2, 2, TOK, D)),
        ),
        in_specs=[ANY] * 3 + [VMEM, ANY] + [VMEM] * 6,
        out_specs=[ANY] * 14,
        scratch_shapes=[
            vmem(TWO6 + (6, 5, 16, 128)),
            vmem(TWO5 + (2, 24, 16, 128)),
            vmem(TWO5 + (24, 16, 128)),
            vmem((4, D, 768)),
            vmem((D, D)),
            vmem((D, 2048)),
            vmem((8, D), F32),
            vmem((TOK, D)),
            vmem((1024, 1024)),
            vmem((TOK, 2048)),
            vmem((TOK, D)),
            vmem((TOK, D), F32),
            vmem((2, 2, TOK, D)),
            vmem((512, 1024)),
            vmem((2, 512, 1024)),
            vmem((2, D, TOK)),
            vmem((D, 1024)),
            vmem((1024, 1024)),
            vmem((2, TOK, D)),
            dma(140),
            dma(140),
            dma(4),
            dma(20),
        ],
        compiler_params=params(0, 63),
    )(*operands)


def backward(*operands):
    return pl.pallas_call(
        backward_kernel,
        name="backward",
        out_shape=(
            shape((2, 3, 5, 16, 128), F32),
            shape((4, 2, 6, 16, 128), F32),
            shape((24, 16, 128), F32),
            shape((TOK, D)),
            shape((TOK, D), F32),
            shape(TWO6 + (6, 5, 16, 128)),
            shape(TWO5 + (2, 24, 16, 128)),
            shape(TWO5 + (24, 16, 128)),
            shape((3, D, 1024)),
            shape((6, TOK, D)),
        ),
        in_specs=[ANY] + [VMEM] * 7 + [ANY] * 14,
        out_specs=[VMEM] * 3 + [ANY] * 7,
        scratch_shapes=[
            vmem((D, 1024)),
            vmem((2, 2, TOK, D)),
            vmem((1024, 1024)),
            vmem((2, 1024, 1024)),
            vmem((2, 384, D)),
            vmem((2, 256, 2048)),
            vmem(TWO5 + (2, 24, 16, 128)),
            vmem((5,) + TWO4 + (2, 5, 16, 128)),
            vmem(TWO5 + (24, 16, 128)),
            vmem((5,) + TWO4 + (7, 16, 128)),
            vmem((640, 16, 128)),
            vmem(TWO6 + (6, 5, 16, 128)),
            vmem((6,) + TWO5 + (5, 16, 128)),
            vmem((2, 384, 1024)),
            vmem((9, TOK, 512)),
            vmem((2, D, TOK)),
            vmem((TOK, D), F32),
            vmem((TOK, D), F32),
            vmem((2, 2, TOK, D)),
            vmem((2, TOK, D)),
            vmem((8, D), F32),
            vmem((8, D), F32),
            vmem((4, 2, 6, 16, 128)),
            vmem((3, 5, 16, 128)),
            dma(200),
            dma(200),
            dma(4),
            dma(12),
            dma(20),
            dma(2),
            dma(9),
        ],
        compiler_params=params(1, 63),
    )(*operands)


def tables():
    spread = np.zeros((384, 512), np.float32)
    for head in range(4):
        for lane in range(96):
            spread[head * 96 + lane, head * 128 + lane + (16 if lane >= 48 else 0)] = 1
    pick = np.zeros((128, D), np.float32)
    pick[np.arange(D) % 12, np.arange(D)] = 1
    owner = np.zeros((128, D), np.float32)
    order = np.array(GRAY)
    for gx in range(4):
        for gz in range(4):
            for gy in range(4):
                for core in range(2):
                    at = ((gx * 4 + gz) * 4 + gy) * 2 + core
                    device = ((order[gx] * 4 + order[gz]) * 4 + order[gy]) * 2 + core
                    owner[at, device * 12 : device * 12 + 12] = 1
    return [jnp.asarray(table, BF16) for table in (spread, pick, owner)]


def adamw_step(weight, moment_one, moment_two, gradient, rate, decay):
    first_new = BETA_ONE * moment_one + (1.0 - BETA_ONE) * gradient
    second_new = BETA_TWO * moment_two + (1.0 - BETA_TWO) * gradient * gradient
    unbiased_one = first_new / (1.0 - BETA_ONE**STEP)
    unbiased_two = second_new / (1.0 - BETA_TWO**STEP)
    weight_new = weight - rate * (
        unbiased_one / (jnp.sqrt(unbiased_two) + ADAM_EPSILON) + decay * weight
    )
    return (weight_new, first_new, second_new)


def hidden_chunks():
    chunks = []
    for x in range(4):
        for z in range(4):
            for yb in range(2):
                gx, gz = GRAY[x], GRAY[z]
                xb, xa, zb, za = gx // 2, gx % 2, gz // 2, gz % 2
                pieces = []
                for low in range(2):
                    for core in range(2):
                        ya = 1 - low if yb else low
                        pieces.append((2 * ya + core, xb, 2 * xa + zb, 32 * (2 * za + yb)))
                chunks.append((128 * ((x * 4 + z) * 2 + yb), pieces))
    return chunks


ATT_SPOTS = ((0, 0), (0, 1), (0, 2), (0, 3), (0, 4), (1, 3), (1, 0), (1, 1), (1, 2))


def prepare_kernel(qkv, out, upw, downw, gains, seg_col, seg_row, freq, pick, att, up, down, cos, sin, bias):
    for number, (part, k) in enumerate(ATT_SPOTS):
        ref, width, start = (qkv, 768, 128 * number) if number < 6 else (out, 384, 128 * number - 768)
        pieces = [ref[:, width * at + start : width * at + start + 128] for at in range(4)]
        att[part, :, k] = jnp.concatenate(pieces, axis=0).astype(BF16).reshape(3, 16, 128)
    lines = dot_first(gains[...].astype(BF16), pick[0:12, 0:128])
    lines = jnp.concatenate([lines, jnp.zeros((14, 128), F32)], axis=0).astype(BF16)
    att[1, 0, 4] = lines
    att[1, 1:3, 4] = jnp.zeros((2, 16, 128), BF16)
    sources = {}
    for start, pieces in hidden_chunks():
        for at, (rank, high, tile, lane) in enumerate(pieces):
            sources[rank, high, tile, lane] = start + 32 * at
    for rank in range(4):
        for tile in range(4):
            quarters = []
            for quarter in range(4):
                base = 4096 * (quarter // 2)
                lanes = [base + sources[rank, quarter % 2, tile, 32 * at] for at in range(4)]
                quarters.append(jnp.concatenate([upw[:, lane : lane + 32] for lane in lanes], axis=1))
            block = jnp.concatenate(quarters, axis=0).astype(BF16).reshape(3, 16, 128)
            for third in range(3):
                up[rank, tile // 2, 2 * third + tile % 2] = block[third]
    for at in range(12):
        down[2 * at : 2 * at + 2] = downw[:, 128 * at : 128 * at + 128].astype(BF16).reshape(2, 16, 128)
    places = lax.broadcasted_iota(jnp.int32, (TOK, TOK), 1)
    same = seg_col[...] == seg_row[...]
    first = jnp.min(jnp.where(same, places, TOK).astype(F32), axis=1, keepdims=True)
    rows = lax.broadcasted_iota(jnp.int32, (TOK, 128), 0).astype(F32)
    angles = (rows - first) * freq[...]
    cos[...] = jnp.cos(angles)
    lanes = lax.broadcasted_iota(jnp.int32, (TOK, 128), 1)
    sine = jnp.sin(angles)
    sin[...] = jnp.where(lanes < 64, -sine, sine)
    bias[...] = mask_bias(seg_col[...], seg_row[...])


def prepare(qkv, out, up, down, gains, segment_ids, pick):
    steps = THETA ** (-jnp.arange(0, HD, 2, dtype=F32) / HD)
    gap = jnp.zeros((16,), F32)
    freq = jnp.concatenate([steps, gap, steps, gap]).reshape(1, 128)
    return pl.pallas_call(
        prepare_kernel,
        name="prepare",
        out_shape=(
            shape((2, 3, 5, 16, 128)),
            shape((4, 2, 6, 16, 128)),
            shape((24, 16, 128)),
            shape((TOK, 128), F32),
            shape((TOK, 128), F32),
            shape((TOK, TOK), F32),
        ),
        in_specs=[VMEM] * 9,
        out_specs=[VMEM] * 6,
        compiler_params=pltpu.CompilerParams(vmem_limit_bytes=62 * MIB),
    )(qkv, out, up, down, gains, segment_ids.reshape(TOK, 1), segment_ids.reshape(1, TOK), freq, pick)


def finish_kernel(att, up, down, *refs):
    old, new = (refs[0:5], refs[5:10], refs[10:15]), (refs[15:20], refs[20:25], refs[25:30])

    def step(number, at, gradient):
        values = [group[number][at] for group in old]
        for group, value in zip(new, adamw_step(*values, gradient, RATES[number], DECAYS[number])):
            group[number][at] = value

    everything = slice(None)
    for number, (part, k) in enumerate(ATT_SPOTS):
        which, width, start = (0, 768, 128 * number) if number < 6 else (1, 384, 128 * number - 768)
        block = att[part, :, k].reshape(48, 128)
        for at in range(4):
            lane = width * at + start
            step(which, (everything, slice(lane, lane + 128)), block[12 * at : 12 * at + 12])
    blocks = {}
    for rank in range(4):
        for tile in range(4):
            units = [up[rank, tile // 2, 2 * third + tile % 2] for third in range(3)]
            block = jnp.concatenate(units, axis=0)
            for quarter in range(4):
                blocks[rank, quarter, tile] = block[12 * quarter : 12 * quarter + 12]
    for start, pieces in hidden_chunks():
        for half in range(2):
            parts = [
                blocks[rank, 2 * half + high, tile][:, lane : lane + 32] for rank, high, tile, lane in pieces
            ]
            lane = 4096 * half + start
            step(2, (everything, slice(lane, lane + 128)), jnp.concatenate(parts, axis=1))
    for at in range(12):
        step(3, (everything, slice(128 * at, 128 * at + 128)), down[2 * at : 2 * at + 2].reshape(32, 128))
    step(4, (everything, everything), jnp.transpose(att[1, 0, 4][0:8])[0:12, 0:2])


def finish(sums, masters, firsts, seconds):
    kinds = [shape(master.shape, F32) for master in masters]
    return pl.pallas_call(
        finish_kernel,
        name="finish",
        out_shape=kinds * 3,
        in_specs=[VMEM] * 18,
        out_specs=[VMEM] * 15,
        compiler_params=pltpu.CompilerParams(vmem_limit_bytes=62 * MIB),
    )(*sums, *masters, *firsts, *seconds)


def body(
    tokens_in,
    cotangent,
    segment_ids,
    proj_qkv,
    proj_out,
    proj_up,
    proj_down,
    norm_gains,
    first_qkv,
    first_out,
    first_up,
    first_down,
    first_gains,
    second_qkv,
    second_out,
    second_up,
    second_down,
    second_gains,
):
    spread, pick, owner = tables()
    att_units, up_units, down_units, cos, sin, bias = prepare(
        proj_qkv, proj_out, proj_up, proj_down, norm_gains, segment_ids, pick
    )
    (
        down_all, wq, wo, wgu, n2t, dy_all, heads, a_t, n1_t, middle, gains, gate_up, z_t, y_part,
    ) = forward(
        att_units, up_units, down_units, tokens_in, cotangent, bias, cos, sin, spread, pick, owner
    )
    att_sum, up_sum, down_sum, block_output, input_grad, *_ = backward(
        tokens_in, cos, sin, bias, spread, pick, owner, gains, cotangent,
        down_all, wq, wo, wgu, n2t, dy_all, heads, a_t, n1_t, middle, gate_up, z_t, y_part,
    )
    updated = finish(
        (att_sum, up_sum, down_sum),
        (proj_qkv, proj_out, proj_up, proj_down, norm_gains),
        (first_qkv, first_out, first_up, first_down, first_gains),
        (second_qkv, second_out, second_up, second_down, second_gains),
    )
    return (block_output, input_grad, *updated)


def solution(mesh):
    rows = P("fsdp", None)
    return jax.shard_map(
        body,
        mesh=mesh,
        in_specs=(rows, rows, P("fsdp")) + (rows,) * 15,
        out_specs=(rows,) * 17,
        check_vma=False,
    )
```

```python
import functools
import math

import jax
import jax.numpy as jnp
import numpy as np
from jax import lax
from jax.experimental import pallas as pl
from jax.experimental.pallas import tpu as pltpu
from jax.sharding import PartitionSpec as P

H = 16
KVH = 8
HD = 96
FF = 4096
STEP = 10
D = 1536
TOK = 256


EPSILON = 1e-05
THETA = 100000.0
BETA_ONE = 0.9
BETA_TWO = 0.95
ADAM_EPSILON = 1e-08
RATES = (0.08, 0.3, 0.08, 0.05, 1.0)
DECAYS = (0.1, 0.1, 0.1, 0.1, 0.0)
MASKED = -1e30

MESH = pl.DeviceIdType.MESH
BF16 = jnp.bfloat16
F32 = jnp.float32
MIB = 1024 * 1024
LAG = 3

CUBE = ("xb", "xa", "zb", "za", "yb", "ya")
LINKS = ("xa", "xb", "za", "zb", "ya", "yb")
QUAD_LINKS = ("xa", "xb", "za", "zb", "yb")
GRAY = (0, 1, 3, 2)
FOUR = ((0, 1, 2, 3), (2, 3, 0, 1))


class Place:
    def __init__(self):
        me = lax.axis_index("fsdp")
        self.me = me
        self.c = lax.rem(me, 2)
        self.y = lax.rem(me // 2, 4)
        self.z = lax.rem(me // 8, 4)
        self.x = me // 32
        self.bit = {"c": self.c}
        for name in "xyz":
            at = getattr(self, name)
            self.bit[name + "b"] = at // 2
            self.bit[name + "a"] = lax.rem(at + at // 2, 2)

    def partner(self, *dims):
        at = {"x": self.x, "y": self.y, "z": self.z, "c": self.c}
        for dim in dims:
            name = dim[0]
            if dim == "c":
                at["c"] = 1 - at["c"]
            elif dim[1] == "a":
                at[name] = at[name] + 1 - 2 * lax.rem(at[name], 2)
            else:
                at[name] = 3 - at[name]
        return ((at["x"] * 4 + at["z"]) * 4 + at["y"]) * 2 + at["c"]


def greet(devices):
    barrier = pltpu.get_barrier_semaphore()
    for device in devices:
        pl.semaphore_signal(barrier, inc=1, device_id=(device,), device_id_type=MESH)
    pl.semaphore_wait(barrier, len(devices))


class Sems:
    def __init__(self, send, recv):
        self.send, self.recv, self.used = send, recv, 0

    def copy(self, src, dst, device):
        at = self.used
        self.used += 1
        assert at < self.send.shape[0]
        return pltpu.make_async_remote_copy(
            src_ref=src,
            dst_ref=dst,
            send_sem=self.send.at[at],
            recv_sem=self.recv.at[at],
            device_id=(device,),
            device_id_type=MESH,
        )


def spot(place, dims, done=(), flip=None):
    return tuple(
        pl.ds(0, 2) if dim in done else (1 - place.bit[dim] if dim == flip else place.bit[dim])
        for dim in dims
    )


def rotated(links, by):
    return links[by:] + links[:by]


UP_PARTS = ((0, 5), (5, 5), (10, 5), (15, 5), (20, 4))
DOWN_PARTS = ((0, 4), (4, 4), (8, 5), (13, 4), (17, 7))
TILES = ((0, 2, 0, 0, 0), (2, 2, 0, 2, 0), (4, 1, 0, 4, 0), (5, 1, 1, 3, 0), (6, 2, 1, 0, 1), (8, 1, 1, 2, 1))


class Gather:
    def __init__(self, place, sems, ref, dims, links, rotation, cut):
        self.place, self.sems, self.ref, self.dims, self.cut = place, sems, ref, dims, cut
        self.order, self.copies = rotated(links, rotation), []

    def step(self, number):
        if number > 0:
            self.copies[number - 1].wait_recv()
        if number < len(self.order):
            view = self.ref.at[spot(self.place, self.dims, self.order[:number]) + self.cut]
            copy = self.sems.copy(view, view, self.place.partner(self.order[number]))
            copy.start()
            self.copies.append(copy)

    def end(self):
        for copy in self.copies:
            copy.wait_send()


def each_block(place, dims, free, whole, visit):
    looped = tuple(dim for dim in free if dim not in whole)
    count = 2 ** len(looped)

    def at(i):
        index = []
        weight = count
        for dim in dims:
            if dim in whole:
                index.append(slice(None))
            elif dim in looped:
                weight //= 2
                index.append(lax.rem(i // weight, 2))
            else:
                index.append(place.bit[dim])
        return tuple(index)

    if count == 1:
        visit(at(0))
    else:
        pl.loop(0, count)(lambda i: visit(at(i)))


class Scatter:
    def __init__(self, place, sems, ref, far, got, dims, links, rotation, cuts, cut, counts):
        self.place, self.sems, self.ref, self.far, self.got = place, sems, ref, far, got
        self.dims, self.cut, self.counts = dims, cut, counts
        self.order = tuple(reversed(rotated(links, rotation)))
        self.rest = tuple(dim for dim in dims if dim != self.order[0])
        link, free = self.order[0], self.order[1:]
        there = spot(place, dims, free, flip=link)
        here = spot(place, dims, free)
        self.firsts = [sems.copy(ref.at[there + at], far.at[here + at], place.partner(link)) for at in cuts]
        self.size = math.prod(counts) * 2 ** len(free)
        self.copies = [None]

    def prepare(self, number):
        link = self.order[number]
        free = self.order[number + 1 :]
        src = self.ref.at[spot(self.place, self.dims, free, flip=link) + self.cut]
        dst = self.got.at[spot(self.place, self.rest, free)]
        self.copies.append(self.sems.copy(src, dst, self.place.partner(link)))

    def fetch(self, stage, sem):
        for copy in self.firsts:
            copy.wait_recv()
        link, free = self.order[0], self.order[1:]
        here = self.far.at[spot(self.place, self.dims, free, flip=link) + self.cut]
        self.stage = stage.reshape(*(2,) * len(free), *self.counts, 16, 128)
        self.staged = pltpu.make_async_copy(here, self.stage, sem)
        self.staged.start()

    def add(self, number):
        link = self.order[number]
        free = tuple(dim for dim in self.dims if dim in self.order[number + 1 :])
        whole = free[-2:]

        def visit(index):
            bits = dict(zip(self.dims, index))
            own = index + self.cut
            if number == 0:
                other = self.stage[tuple(bits[dim] for dim in self.rest)]
            else:
                other = self.got[tuple(1 - bits[dim] if dim == link else bits[dim] for dim in self.rest)]
            self.ref[own] = (self.ref[own].astype(F32) + other.astype(F32)).astype(BF16)

        each_block(self.place, self.dims, free, whole, visit)

    def step(self, number):
        if number == 1:
            self.staged.wait()
        elif number > 1:
            self.copies[number - 1].wait_recv()
        if number > 0:
            self.add(number - 1)
        if number < len(self.order):
            self.prepare(number)
            self.copies[number].start()

    def end(self):
        for copy in self.firsts + self.copies[1:]:
            copy.wait_send()


def first_adds(jobs, stage, sems):
    at = 0
    while at < len(jobs):
        batch, units = [], 0
        while at < len(jobs) and len(batch) < 9:
            if units + jobs[at].size > 640:
                break
            jobs[at].fetch(stage.at[pl.ds(units, jobs[at].size)], sems.at[len(batch)])
            batch.append(jobs[at])
            units += jobs[at].size
            at += 1
        for job in batch:
            job.step(1)


def natural_group(g):
    xb, xa = lax.rem(g // 16, 2), lax.rem(g // 8, 2)
    zb, za = lax.rem(g // 4, 2), lax.rem(g // 2, 2)
    yb = lax.rem(g, 2)
    x = 2 * xb + lax.rem(xa + xb, 2)
    z = 2 * zb + lax.rem(za + zb, 2)
    return (xb, xa, zb, za, yb), (x * 4 + z) * 2 + yb


def dot(left, right):
    return lax.dot_general(left, right, (((1,), (0,)), ((), ())), preferred_element_type=F32)


def dot_t(left, right):
    return lax.dot_general(left, right, (((1,), (1,)), ((), ())), preferred_element_type=F32)


def cols(i, width):
    return pl.ds(pl.multiple_of(i * width, width), width)


def head_pad(value, spread):
    high = value.astype(BF16)
    low = (value - high.astype(F32)).astype(BF16)
    return dot(high, spread) + dot(low, spread)


def turn(value, cos, sin):
    return value * cos + pltpu.roll(value, 64, 1) * sin


def mask_bias(seg_col, seg_row):
    rows = lax.broadcasted_iota(jnp.int32, (TOK, TOK), 0)
    columns = lax.broadcasted_iota(jnp.int32, (TOK, TOK), 1)
    allowed = jnp.logical_and(seg_col == seg_row, columns <= rows)
    return jnp.where(allowed, 0.0, MASKED).astype(F32)


def row_norm(value):
    return lax.rsqrt(jnp.mean(value * value, axis=-1, keepdims=True) + EPSILON)


def each_rows(step, visit, rows=TOK):
    @pl.loop(0, rows // step)
    def _(i):
        visit(pl.ds(pl.multiple_of(i * step, step), step))


def open_quarter(block, yb, quarter):
    pieces = [block[48 * at + 12 * quarter : 48 * at + 12 * quarter + 12] for at in FOUR[yb]]
    return jnp.concatenate(pieces, axis=0)


def sigmoid(value):
    return 1.0 / (1.0 + jnp.exp(-value))


def dot_first(left, right):
    return lax.dot_general(left, right, (((0,), (0,)), ((), ())), preferred_element_type=F32)


class Outs:
    def __init__(self, sems):
        self.sems, self.copies, self.ended = sems, [], 0

    def put(self, src, dst):
        assert len(self.copies) < self.sems.shape[0]
        copy = pltpu.make_async_copy(src, dst, self.sems.at[len(self.copies)])
        copy.start()
        self.copies.append(copy)

    def end(self):
        for copy in self.copies[self.ended :]:
            copy.wait()
        self.ended = len(self.copies)


def quad_of(place):
    return {(0, 1): place.partner("c"), (1, 0): place.partner("ya"), (1, 1): place.partner("ya", "c")}


def forward_kernel(
    att_in, up_in, down_in, x, dy, bias, cos, sin, spread, pick, owner,
    down_out, wq_out, wo_out, wgu_out, n2t_out, dy_all, q_out, at_out, n1t_out, m_out, g_out, gu_out, zt_out,
    y_out,
    att, up, down, wq, wo, wgu, gains, n1, q, apad, a, m, n2_all, z, gu, turned, n2t, zt, y,
    send, recv, local, out_sem,
):
    place = Place()
    sems = Sems(send, recv)
    outs = Outs(out_sem)
    quad = quad_of(place)
    sibling, across = quad[0, 1], quad[1, 0]
    greet([place.partner(link) for link in LINKS] + [quad[0, 1], quad[1, 1]])
    dims5 = CUBE[:5]
    home6 = spot(place, CUBE)
    home5 = spot(place, dims5)
    ya, c = place.bit["ya"], place.c
    rank = 2 * ya + c
    mine = pl.ds(3 * c, 3)
    six = pl.ds(pl.multiple_of(6 * rank, 2), 6)
    swap = sems.copy(att_in.at[1 - c], att.at[home6 + (mine,)], sibling)
    swap.start()
    starts = [
        pltpu.make_async_copy(att_in.at[c], att.at[home6 + (mine,)], local.at[0]),
        pltpu.make_async_copy(down_in, down.at[home5], local.at[1]),
        pltpu.make_async_copy(up_in.at[rank], up.at[home5 + (pl.ds(0, 2), six)], local.at[2]),
    ]
    for copy in starts:
        copy.start()
    scatter = []
    for (dya, dc), device in quad.items():
        to = 2 * (1 - ya if dya else ya) + (1 - c if dc else c)
        copy = sems.copy(up_in.at[to], up.at[home5 + (pl.ds(0, 2), six)], device)
        copy.start()
        scatter.append(copy)
    for copy in starts:
        copy.wait()
    swap.wait()
    first = [Gather(place, sems, att, CUBE, LINKS, by, (by,)) for by in range(6)]
    ups = [
        Gather(place, sems, up, dims5, QUAD_LINKS, by, (pl.ds(0, 2), pl.ds(*at)))
        for by, at in enumerate(UP_PARTS)
    ]
    downs = [Gather(place, sems, down, dims5, QUAD_LINKS, by, (pl.ds(*at),)) for by, at in enumerate(DOWN_PARTS)]
    second = ups + downs
    for number in range(7):
        for job in first:
            job.step(number)
        if number == 0:
            for copy in scatter:
                copy.wait()
        if number >= LAG:
            for job in second:
                job.step(number - LAG)
    dy_near = sems.copy(dy, dy_all.at[ya, c], sibling)
    dy_near.start()
    dy_far = sems.copy(dy, dy_all.at[ya, c], across)
    dy_far.start()

    wide, narrow = pl.ds(0, 640), pl.ds(640, 128)
    shared = {0: [], 1: []}
    for at in range(4):
        rows = pl.ds(GRAY[at] * 384, 384)
        for core, refs in ((0, [wq.at[:, rows, wide]]), (1, [wq.at[:, rows, narrow], wo.at[rows]])):
            shared[core].append([sems.copy(ref, ref, sibling) for ref in refs])
    gain_share = sems.copy(gains, gains, sibling)

    @pl.when(c == 1)
    def _():
        tiles = jnp.stack([att[..., 3 * core, 4, :, :].reshape(64, 16, 128) for core in range(2)], axis=1)
        tiles = tiles.reshape(128, 16, 128).astype(F32)
        lines = lax.broadcasted_iota(jnp.int32, (128, 16, 128), 1)
        for number in range(2):
            line = jnp.sum(jnp.where(lines == number, tiles, 0.0), axis=1).astype(BF16)
            vector = jnp.sum(dot(line, pick[...]) * owner[...].astype(F32), axis=0, keepdims=True)
            gains[number : number + 1, :] = vector
        gains[2:8, :] = jnp.zeros((6, D), F32)
        gain_share.start()

    for at in range(4):

        @pl.loop(0, 8)
        def _(part):
            bits, n = natural_group(at * 8 + part)
            rows = pl.ds(pl.multiple_of(n * 48, 16), 48)
            block = jnp.concatenate([att[bits][:, :, k].reshape(192, 128) for k in range(5)], axis=1)
            for yb in range(2):

                @pl.when(jnp.logical_and(bits[4] == yb, c == 0))
                def _():
                    for quarter in range(4):
                        wq[quarter, rows, 0:640] = open_quarter(block, yb, quarter)

                @pl.when(jnp.logical_and(bits[4] == yb, c == 1))
                def _():
                    for quarter in range(4):
                        piece = open_quarter(block[:, :512], yb, quarter)
                        wq[quarter, rows, 640:768] = piece[:, 384:]
                        wo[rows, 384 * quarter : 384 * quarter + 384] = piece[:, :384]

        for core in range(2):

            @pl.when(c == core)
            def _():
                for copy in shared[core][at]:
                    copy.start()


    @pl.when(c == 0)
    def _():
        gain_share.wait_recv()

    def norm_one(at):
        value = x[at, :].astype(F32)
        n1[at, :] = (value * row_norm(value) * gains[0:1, :]).astype(BF16)

    each_rows(64, norm_one)
    for core in range(2):

        @pl.when(c == core)
        def _():
            for at in range(4):
                for copy in shared[1 - core][at]:
                    copy.wait_recv()

    outs.put(wq, wq_out)
    outs.put(wo, wo_out)

    def heads(i, rotated_too):
        value = dot(n1[...], wq[i // 2, :, cols(lax.rem(i, 2), 384)])
        padded = head_pad(value, spread[...])
        for at in range(4):
            head = padded[:, 128 * at : 128 * at + 128]
            if rotated_too:
                head = turn(head, cos[...], sin[...])
            lanes = pl.ds(pl.multiple_of(lax.rem(i, 2) * 512 + 128 * at, 128), 128)
            q[cols(i // 2, 256), lanes] = head.astype(BF16)

    pl.loop(0, 6)(lambda i: heads(i, True))
    pl.loop(6, 8)(lambda i: heads(i, False))
    for job in ups:
        job.step(4)
    outs.put(q, q_out)

    own = n2_all.at[ya, c]
    near, far = [], []
    for half in range(2):
        start, seen = 128 * half, 128 * half + 128
        rows = pl.ds(start, 128)

        @pl.loop(0, 8)
        def _(j):
            pair = q[pl.ds(pl.multiple_of(j // 4 * 256 + start, 128), 128), cols(lax.rem(j, 4), 256)]
            both = jnp.concatenate([pair[:, :128], pair[:, 128:]], axis=0)
            key = q[512 : 512 + seen, cols(j, 128)]
            value = q[768 : 768 + seen, cols(j, 128)]
            mask = bias[rows, 0:seen]
            scores = dot_t(both, key) * (1.0 / math.sqrt(HD)) + jnp.concatenate([mask, mask], axis=0)
            exponent = jnp.exp(scores - jnp.max(scores, axis=-1, keepdims=True))
            weights = exponent / jnp.sum(exponent, axis=-1, keepdims=True)
            result = dot(weights.astype(BF16), value).astype(BF16)
            for at in range(2):
                lanes = pl.ds(pl.multiple_of(j * 256 + 128 * at, 128), 128)
                apad[rows, lanes] = result[128 * at : 128 * at + 128]

        if half == 1:
            for job in downs:
                job.step(4)

        @pl.loop(0, 4)
        def _(i):
            a[rows, cols(i, 384)] = dot_t(apad[rows, cols(i, 512)], spread[...]).astype(BF16)

        @pl.loop(0, 3)
        def _(i):
            m[rows, cols(i, 512)] = x[rows, cols(i, 512)].astype(F32) + dot(a[rows, :], wo[:, cols(i, 512)])

        def norm_two(i):
            at = pl.ds(pl.multiple_of(start + i * 64, 64), 64)
            value = m[at, :]
            own[at, :] = (value * row_norm(value) * gains[1:2, :]).astype(BF16)

        pl.loop(0, 2)(norm_two)
        near.append(sems.copy(own.at[rows], own.at[rows], sibling))
        near[half].start()
        far.append(sems.copy(own.at[rows], own.at[rows], across))
        far[half].start()
    outs.put(m, m_out)
    outs.put(gains, g_out)

    @pl.loop(0, 6)
    def _(i):
        turned[0, cols(i, 256), :] = jnp.transpose(n1[:, cols(i, 256)])
        turned[1, cols(i, 256), :] = jnp.transpose(a[:, cols(i, 256)])

    outs.put(turned.at[0], n1t_out)
    outs.put(turned.at[1], at_out)

    for job in ups:
        job.step(5)

    @pl.loop(0, 32)
    def _(g):
        bits, n = natural_group(g)
        rows = pl.ds(pl.multiple_of(n * 48, 16), 48)
        block = jnp.concatenate(
            [up[bits + (k // 2,)].reshape(12, 2, 16, 128)[:, k % 2].reshape(192, 128) for k in range(4)], axis=1
        )
        for yb in range(2):

            @pl.when(bits[4] == yb)
            def _():
                for quarter in range(4):
                    wgu[rows, 512 * quarter : 512 * quarter + 512] = open_quarter(block, yb, quarter)

    outs.put(wgu, wgu_out)
    for job in downs:
        job.step(5)
    outs.put(down, down_out)
    for copy in near:
        copy.wait_recv()

    def mlp(pair):
        rows = cols(pair, 512)

        @pl.loop(0, 4)
        def _(i):
            left = n2_all[pair].reshape(512, D)
            gate = dot(left, wgu[:, cols(i, 256)])
            upward = dot(left, wgu[:, cols(i + 4, 256)])
            hidden = gate * sigmoid(gate) * upward
            z[:, cols(i, 256)] = hidden.astype(BF16)
            gu[0, :, cols(i, 256)] = gate.astype(BF16)
            gu[1, :, cols(i, 256)] = upward.astype(BF16)

        outs.put(gu, gu_out.at[:, rows])

        @pl.loop(0, 6)
        def _(i):
            right = jnp.concatenate(
                [down[..., pl.ds(4 * i + 2 * at, 2), :, :].reshape(1024, 128) for at in range(2)], axis=1
            )
            y[:, :, cols(i, 256)] = dot(z[...], right).astype(BF16).reshape(2, TOK, 256)

        outs.put(y, y_out.at[pair])

        @pl.loop(0, 6)
        def _(i):
            n2t[cols(i, 256), rows] = jnp.transpose(n2_all[pair, :, :, cols(i, 256)].reshape(512, 256))

        outs.put(n2t.at[:, rows], n2t_out.at[:, rows])

        @pl.loop(0, 4)
        def _(i):
            zt[cols(i, 256), rows] = jnp.transpose(z[:, cols(i, 256)])

        outs.put(zt.at[:, rows], zt_out.at[:, rows])

    def pass_on(half):
        far[half].wait_recv()
        there = n2_all.at[1 - ya, c, pl.ds(128 * half, 128)]
        copy = sems.copy(there, there, sibling)
        copy.start()
        return copy

    mlp(ya)
    onward = [pass_on(0)]

    dy_far.wait_recv()
    dy_onward = sems.copy(dy_all.at[1 - ya, c], dy_all.at[1 - ya, c], sibling)
    dy_onward.start()
    onward.append(pass_on(1))
    for copy in onward:
        copy.wait_recv()
    outs.end()
    mlp(1 - ya)
    for copy in near + far + onward:
        copy.wait_send()
    dy_near.wait()
    dy_far.wait_send()
    dy_onward.wait()
    for core in range(2):

        @pl.when(c == core)
        def _():
            for at in range(4):
                for copy in shared[core][at]:
                    copy.wait_send()

    @pl.when(c == 1)
    def _():
        gain_share.wait_send()

    for job in first + second:
        job.end()
    outs.end()


def backward_kernel(
    x, cos, sin, bias, spread, pick, owner, gains, cotangent,
    down_in, wq_in, wo_in, wgu_in, n2t_in, dy_in, q_in, at_in, n1t_in, m_in, gu_in, zt_in, y_in,
    att_out, up_out, down_out, block_out, grad_out,
    far_att, far_up, far_down, land, quad_got,
    n2t, dy, zt, gu, wo_slots, wgu_slots, g_up, got_up, g_down, got_down, stage, g_att, got_att,
    dw, rt, lhs, dm, dn1, p, t, dg, dg_got, up_land, att_land,
    send, recv, local, slot_sem, load_sem, out_sem, stage_sem,
):
    place = Place()
    sems = Sems(send, recv)
    outs = Outs(out_sem)
    quad = quad_of(place)
    sibling, across = quad[0, 1], quad[1, 0]
    greet([place.partner(link) for link in LINKS] + [quad[0, 1], quad[1, 1]])
    dims5 = CUBE[:5]
    home6 = spot(place, CUBE)
    home5 = spot(place, dims5)
    ya, c = place.bit["ya"], place.c
    rank = 2 * ya + c
    loads = {}

    def load(name, src, dst):
        assert len(loads) < load_sem.shape[0]
        copy = pltpu.make_async_copy(src, dst, load_sem.at[len(loads)])
        copy.start()
        loads[name] = copy

    load("zt", zt_in, zt)
    load("dy", cotangent, dy.at[ya, c])
    load("dy1", dy_in.at[ya, 1 - c], dy.at[ya, 1 - c])
    load("dy2", dy_in.at[1 - ya], dy.at[1 - ya])
    load("gu", gu_in, gu)

    wd_slots = [stage.at[pl.ds(192 * slot, 192)].reshape(2, 2, 2, 24, 16, 128) for slot in range(2)]

    def fetch_wd(i):
        slot = i % 2
        whole = (pl.ds(0, 2),) * 3 + (pl.ds(0, 24), pl.ds(0, 16), pl.ds(0, 128))
        return pltpu.make_async_copy(down_in.at[(i // 2, i % 2) + whole], wd_slots[slot], slot_sem.at[slot])

    fetch_wd(0).start()
    fetch_wd(1).start()

    y_away = sems.copy(y_in.at[1 - ya, 1 - c], quad_got.at[0], sibling)
    y_away.start()
    y_near = sems.copy(y_in.at[ya, 1 - c], quad_got.at[1], sibling)
    y_near.start()

    up_jobs = [
        Scatter(
            place, sems, g_up, far_up, got_up.at[by, :, :, :, :, :, pl.ds(0, at[1])], dims5, QUAD_LINKS, by,
            [(pair, pl.ds(*at)) for pair in range(2)], (pl.ds(0, 2), pl.ds(*at)), (2, at[1]),
        )
        for by, at in enumerate(UP_PARTS)
    ]
    down_jobs = [
        Scatter(
            place, sems, g_down, far_down, got_down.at[by, :, :, :, :, pl.ds(0, at[1])], dims5, QUAD_LINKS, by,
            [(pl.ds(*at),)], (pl.ds(*at),), (at[1],),
        )
        for by, at in enumerate(DOWN_PARTS)
    ]
    att_jobs = [
        Scatter(
            place, sems, g_att, far_att, got_att.at[by], CUBE, LINKS, by,
            [(by, pl.ds(0, 2)), (by, pl.ds(2, 2)), (by, pl.ds(4, 1))], (by, pl.ds(0, 5)), (5,),
        )
        for by in range(6)
    ]
    mlp_jobs = up_jobs + down_jobs

    for name in ("zt", "dy", "dy1", "dy2"):
        loads[name].wait()
    for i in range(6):

        @pl.loop(0, 4)
        def _(at):
            right = dy[:, :, :, pl.ds(256 * i, 256)].reshape(1024, 256)
            value = dot(zt[cols(at, 256), :], right).astype(BF16)
            for part in range(2):
                piece = value[:, 128 * part : 128 * part + 128].reshape(2, 2, 2, 2, 16, 128)
                g_down[at // 2, lax.rem(at, 2), :, :, :, pl.ds(4 * i + 2 * part, 2)] = piece

        for job, (start, count) in zip(down_jobs, DOWN_PARTS):
            if 4 * i < start + count <= 4 * i + 4:
                job.firsts[0].start()

    def fetch_wo(i):
        slot = i % 2
        return pltpu.make_async_copy(wo_in.at[pl.ds(384 * i, 384)], wo_slots.at[slot], slot_sem.at[4 + slot])

    def fetch_wgu(i, slot):
        return pltpu.make_async_copy(wgu_in.at[cols(i, 256)], wgu_slots.at[slot], slot_sem.at[2 + slot])

    fetch_wgu(0, 0).start()
    fetch_wgu(1, 1).start()
    fetch_wo(0).start()
    fetch_wo(1).start()
    loads["gu"].wait()
    load("n2t", n2t_in, n2t)
    load("m", m_in, dm)
    load("n1t", n1t_in, lhs.at[0])
    load("at", at_in, lhs.at[1])
    for i in range(4):
        fetch_wd(i).wait()

        @pl.loop(0, 2)
        def _(pair):
            rows = cols(pair, 512)
            lanes = pl.ds(256 * i, 256)
            right = jnp.concatenate(
                [wd_slots[i % 2][:, :, :, 2 * at : 2 * at + 2].reshape(256, 128) for at in range(12)], axis=1
            )
            dz = dot_t(dy[pair].reshape(512, D), right)
            gate = gu[0, rows, lanes].astype(F32)
            upward = gu[1, rows, lanes].astype(F32)
            sg = sigmoid(gate)
            gu[0, rows, lanes] = (dz * upward * sg * (1.0 + gate * (1.0 - sg))).astype(BF16)
            gu[1, rows, lanes] = (dz * gate * sg).astype(BF16)

        if i < 2:
            fetch_wd(i + 2).start()

    aways, fars = [], []

    def mix(i):
        lanes = pl.ds(256 * i, 256)
        aways[i].wait_recv()

        def visit(at):
            total = p[1 - ya, c, at, lanes].astype(F32) + t[1, at, lanes].astype(F32)
            p[1 - ya, c, at, lanes] = total.astype(BF16)

        each_rows(128, visit)
        fars.append(sems.copy(p.at[1 - ya, c, :, lanes], quad_got.at[5, :, lanes], across))
        fars[i].start()

    for i in range(6):
        slot = i % 2
        lanes = pl.ds(256 * i, 256)
        fetch_wgu(i, slot).wait()

        @pl.loop(0, 2)
        def _(pair):
            rows = cols(pair, 512)
            part = dot_t(gu[0, rows, :], wgu_slots[slot, :, 0:1024])
            part = part + dot_t(gu[1, rows, :], wgu_slots[slot, :, 1024:2048])
            p[pair, :, :, lanes] = part.astype(BF16).reshape(2, TOK, 256)

        if i < 4:
            fetch_wgu(i + 2, slot).start()
        aways.append(sems.copy(p.at[1 - ya, 1 - c, :, lanes], t.at[1, :, lanes], sibling))
        aways[i].start()
        if i > 0:
            mix(i - 1)
    near = sems.copy(p.at[ya, 1 - c], t.at[0], sibling)
    near.start()
    mix(5)

    def fetch(src, dst):
        copy = pltpu.make_async_copy(src, dst, local.at[3])
        copy.start()
        copy.wait()

    def add_into(total, term):
        def visit(at):
            total[at, :] = (total[at, :].astype(F32) + term[at, :].astype(F32)).astype(BF16)

        each_rows(64, visit)

    def fold_into(value, width, at, store):
        zb = lax.rem(at, 2)
        for part in range(4):
            z, yb = part // 2, part % 2
            row = part * 48
            pieces = [
                value[row + 12 * to : row + 12 * to + 12, width * quarter : width * quarter + width]
                for to in FOUR[yb]
                for quarter in range(4)
            ]
            folded = jnp.concatenate(pieces, axis=0).reshape(2, 6, 16, width)
            store((at // 4, lax.rem(at // 2, 2), zb, z + zb * (1 - 2 * z), yb), folded)

    def natural_rows(at):
        x = at // 2
        x = x + lax.rem(x // 2, 2) * (1 - 2 * lax.rem(x, 2))
        return pl.ds(pl.multiple_of(x * 384 + lax.rem(at, 2) * 192, 64), 192)

    loads["n2t"].wait()
    for pair in range(2):

        @pl.loop(0, 8)
        def _(at):
            rows = natural_rows(at)
            right = jnp.concatenate(
                [gu[quarter // 2, :, pl.ds((quarter % 2) * 512 + 256 * pair, 256)] for quarter in range(4)], axis=1
            )
            value = dot(n2t[rows, :], right).astype(BF16)

            def store(index, folded):
                folded = folded.reshape(12, 16, 256)
                halves = jnp.stack([folded[:, :, :128], folded[:, :, 128:]], axis=1)
                g_up[index + (pair,)] = halves.reshape(24, 16, 128)

            fold_into(value, 256, at, store)

        for job in up_jobs:
            job.firsts[pair].start()

    near.wait_recv()
    for copy in fars:
        copy.wait_recv()
    fetch(quad_got.at[5], t.at[1])
    loads["m"].wait()
    load("q", q_in, gu.at[0])
    dg[...] = jnp.zeros((8, D), F32)

    def back_two(at):
        value = dm[at, :]
        r = row_norm(value)
        xh = value * r
        dn = p[ya, c, at, :].astype(F32) + t[0, at, :].astype(F32) + t[1, at, :].astype(F32)
        dg[1:2, :] = dg[1:2, :] + jnp.sum(dn * xh, axis=0, keepdims=True)
        e = dn * gains[1:2, :]
        grad = dy[ya, c, at, :].astype(F32) + r * (e - xh * jnp.mean(xh * e, axis=-1, keepdims=True))
        dm[at, :] = grad
        low = grad.astype(BF16)
        for k in range(3):
            for quarter in range(4):
                start = quarter * 384 + k * 128
                rt[6 + k, at, 128 * quarter : 128 * quarter + 128] = low[:, start : start + 128]

    each_rows(32, back_two)
    load("x", x, dy.at[ya, c])

    y_away.wait_recv()
    load("y0", y_in.at[1 - ya, c], t.at[0])
    load("y1", quad_got.at[0], t.at[1])

    for i in range(4):
        fetch_wo(i).wait()
        left = jnp.concatenate(
            [rt[6 + k, :, 128 * quarter : 128 * quarter + 128] for quarter in range(4) for k in range(3)], axis=1
        )
        da = dot_t(left, wo_slots[i % 2]).astype(BF16)
        zt[256 * (i // 2) : 256 * (i // 2) + 256, 512 * (i % 2) : 512 * (i % 2) + 512] = dot(
            da, spread[...]
        ).astype(BF16)
        if i < 2:
            fetch_wo(i + 2).start()

    tile_copies = {}
    for number, (u, count, core, k, out) in enumerate(TILES):
        for at in range(4):
            lanes = pl.ds(0, 512 * count)
            tile_copies[number, at] = sems.copy(
                dw.at[at % 2, :, lanes], land.at[number % 3, pl.ds(384 * at, 384), lanes], sibling
            )
    sent = {0: [], 1: []}

    def tile_right(u, count):
        return jnp.concatenate(
            [rt[u + at, :, 128 * quarter : 128 * quarter + 128] for quarter in range(4) for at in range(count)], axis=1
        )

    def give(number):
        u, count, owner_core, k, out = TILES[number]
        core = 1 - owner_core

        @pl.when(c == core)
        def _():
            right = tile_right(u, count)
            for at in range(4):
                if len(sent[core]) >= 2:
                    sent[core][-2].wait_send()
                left = lhs[out, 384 * at : 384 * at + 384, :]
                dw[at % 2, :, 0 : 512 * count] = dot(left, right).astype(BF16)
                tile_copies[number, at].start()
                sent[core].append(tile_copies[number, at])

    takes = {0: (0, 1, 2), 1: (4, 5, 3)}

    def land_copies(number, place_at):
        lanes = pl.ds(0, 512 * TILES[number][1])
        halves = []
        for half in range(2):
            rows = pl.ds(768 * half, 768)
            ref = n2t.at[rows, lanes] if place_at == 0 else (zt.at[pl.ds(0, 768), lanes], gu.at[0, pl.ds(0, 768), lanes])[half]
            halves.append(
                pltpu.make_async_copy(land.at[number % 3, rows, lanes], ref, slot_sem.at[2 * place_at + half])
            )
        return halves

    def await_land(turn, core):
        number = takes[core][turn]
        for at in range(4):
            tile_copies[number, at].wait_recv()
        for copy in land_copies(number, turn % 2):
            copy.start()

    def take(turn, core):
        number = takes[core][turn]
        u, count, _, k, out = TILES[number]

        @pl.when(c == core)
        def _():
            if turn == 0:
                await_land(0, core)
            for copy in land_copies(number, turn % 2):
                copy.wait()
            if turn < 2:
                await_land(turn + 1, core)
            for half in range(2):

                @pl.loop(4 * half, 4 * half + 4)
                def _(at):
                    rows = natural_rows(at)
                    if turn % 2 == 0:
                        came = n2t[rows, 0 : 512 * count]
                    else:
                        start = pl.multiple_of(rows.start - 768 * half, 64)
                        came = (zt, gu.at[0])[half][pl.ds(start, 192), 0 : 512 * count]
                    value = dot(lhs[out, rows, :], tile_right(u, count)) + came.astype(F32)

                    def store(index, folded):
                        for spot_ya in range(2):
                            for part in range(count):
                                piece = folded[spot_ya, :, :, 128 * part : 128 * part + 128]
                                g_att[index + (spot_ya, slice(None), k + part)] = piece

                    fold_into(value.astype(BF16), 128 * count, at, store)

            if k + count in (2, 4, 5):
                for job in att_jobs:
                    job.firsts[(k + count) // 2 - 1 if k + count < 5 else 2].start()

    loads["at"].wait()
    loads["n1t"].wait()
    give(4)
    give(5)
    loads["y0"].wait()
    loads["y1"].wait()
    add_into(t.at[0], t.at[1])
    y_far = sems.copy(t.at[0], quad_got.at[2], across)
    y_far.start()
    first_adds(mlp_jobs, stage, stage_sem)
    loads["q"].wait()
    scale = 1.0 / math.sqrt(HD)

    @pl.loop(0, 8)
    def _(j):
        rows, lanes = cols(j // 4, 256), cols(lax.rem(j, 4), 256)
        pair = gu[0, rows, lanes]
        da = zt[rows, lanes]
        key = gu[0, 512:768, cols(j, 128)]
        value = gu[0, 768:1024, cols(j, 128)]
        dk = jnp.zeros((TOK, 128), F32)
        dv = jnp.zeros((TOK, 128), F32)
        for at in range(2):
            query = pair[:, 128 * at : 128 * at + 128]
            grad = da[:, 128 * at : 128 * at + 128]
            scores = dot_t(query, key) * scale + bias[...]
            exponent = jnp.exp(scores - jnp.max(scores, axis=-1, keepdims=True))
            weights = exponent / jnp.sum(exponent, axis=-1, keepdims=True)
            dv = dv + dot_first(weights.astype(BF16), grad)
            dp = dot_t(grad, value)
            ds = weights * (dp - jnp.sum(weights * dp, axis=-1, keepdims=True))
            ds = ds.astype(BF16)
            dq = dot(ds, key) * scale
            dk = dk + dot_first(ds, query)
            here = pl.ds(pl.multiple_of(lax.rem(j, 4) * 256 + 128 * at, 128), 128)
            gu[1, rows, here] = turn(dq, cos[...], -sin[...]).astype(BF16)
        gu[1, 512:768, cols(j, 128)] = turn(dk * scale, cos[...], -sin[...]).astype(BF16)
        gu[1, 768:1024, cols(j, 128)] = dv.astype(BF16)

    for job in mlp_jobs:
        job.step(2)
    @pl.loop(0, 8)
    def _(i):
        padded = gu[1, cols(i // 2, 256), cols(lax.rem(i, 2), 512)]
        flat = dot_t(padded, spread[...]).astype(BF16)
        for part in range(3):
            rt[lax.rem(i, 2) * 3 + part, :, cols(i // 2, 128)] = flat[:, 128 * part : 128 * part + 128]

    for number in (3, 0, 1, 2):
        give(number)
    for job in mlp_jobs:
        job.step(3)
    for number in range(3):
        for core in range(2):
            take(number, core)
    for job in mlp_jobs:
        job.step(4)
    def fetch_wq(i):
        slot = i % 2
        ref = (n2t, zt)[slot]
        return [
            pltpu.make_async_copy(
                wq_in.at[quarter, pl.ds(256 * i, 256)],
                ref.at[pl.ds(256 * quarter, 256), pl.ds(0, 768)],
                slot_sem.at[4 + 4 * slot + quarter],
            )
            for quarter in range(4)
        ]

    for i in range(6):
        for ahead in (0, 1) if i == 0 else (i + 1,):
            if ahead < 6:
                for copy in fetch_wq(ahead):
                    copy.start()
        for copy in fetch_wq(i):
            copy.wait()
        weight = (n2t, zt)[i % 2]
        total = jnp.zeros((TOK, 256), F32)
        for quarter in range(4):
            left = jnp.concatenate([rt[k, :, 128 * quarter : 128 * quarter + 128] for k in range(6)], axis=1)
            total = total + dot_t(left, weight[256 * quarter : 256 * quarter + 256, 0:768])
        dn1[:, 256 * i : 256 * i + 256] = total

    def back_one(at):
        value = dy[ya, c, at, :].astype(F32)
        r = row_norm(value)
        xh = value * r
        dn = dn1[at, :]
        dg[0:1, :] = dg[0:1, :] + jnp.sum(dn * xh, axis=0, keepdims=True)
        e = dn * gains[0:1, :]
        dn1[at, :] = dm[at, :] + r * (e - xh * jnp.mean(xh * e, axis=-1, keepdims=True))

    loads["x"].wait()
    each_rows(32, back_one)
    outs.put(dn1, grad_out)
    dg_copy = sems.copy(dg, dg_got, sibling)

    @pl.when(c == 0)
    def _():
        dg_copy.start()
        dg_copy.wait_send()

    @pl.when(c == 1)
    def _():
        g_att[(slice(None),) * 6 + (slice(None), 4)] = jnp.zeros(TWO6 + (6, 16, 128), BF16)
        dg_copy.wait_recv()
        lines = lax.broadcasted_iota(jnp.int32, (128, 16, 128), 1)
        tiles = jnp.zeros((128, 16, 128), F32)
        for number in range(2):
            vector = dg[number : number + 1, :] + dg_got[number : number + 1, :]
            spread_out = (owner[...].astype(F32) * vector).astype(BF16)
            line = dot_t(spread_out, pick[...])
            tiles = jnp.where(lines == number, line.reshape(128, 1, 128), tiles)
        tiles = tiles.astype(BF16).reshape(TWO7 + (16, 128))
        for core in range(2):
            g_att[(slice(None),) * 6 + (3 * core, 4)] = tiles[:, :, :, :, :, :, core]
        for job in att_jobs:
            job.firsts[2].start()

    for job in mlp_jobs:
        job.step(5)
    last = []
    for (dya, dc), device in quad.items():
        to = 2 * (1 - ya if dya else ya) + (1 - c if dc else c)
        src = g_up.at[home5 + (pl.ds(0, 2), pl.ds(pl.multiple_of(6 * to, 2), 6))]
        copy = sems.copy(src, up_land.at[rank], device)
        copy.start()
        last.append(copy)
    up_out[rank] = g_up[home5 + (slice(None), pl.ds(pl.multiple_of(6 * rank, 2), 6))].astype(F32)
    down_out[...] = g_down[home5].astype(F32)
    first_adds(att_jobs, stage, stage_sem)

    outs.end()
    for copy in aways + fars + [near]:
        copy.wait_send()
    y_far.wait_send()
    y_near.wait_recv()
    y_far.wait_recv()
    load("m2", m_in, dm)
    load("y2", y_in.at[ya, c], t.at[0])
    load("y3", quad_got.at[1], t.at[1])
    load("y4", quad_got.at[2], p.at[0, 0])
    for name in ("m2", "y2", "y3", "y4"):
        loads[name].wait()

    def add_y(at):
        total = dm[at, :] + t[0, at, :].astype(F32) + t[1, at, :].astype(F32) + p[0, 0, at, :].astype(F32)
        t[0, at, :] = total.astype(BF16)

    each_rows(64, add_y)
    outs.put(t.at[0], block_out)
    for number in range(2, 7):
        for job in att_jobs:
            job.step(number)
    att_last = sems.copy(g_att.at[home6 + (pl.ds(3 - 3 * c, 3),)], att_land, sibling)
    att_last.start()
    att_out[c] = g_att[home6 + (pl.ds(3 * c, 3),)].astype(F32)
    for copy in last:
        copy.wait()
    att_last.wait()
    for dya, dc in quad:
        to = 2 * (1 - ya if dya else ya) + (1 - c if dc else c)
        up_out[to] = up_land[to].astype(F32)
    att_out[1 - c] = att_land[...].astype(F32)
    for copy in (y_away, y_near):
        copy.wait_send()
    outs.end()
    for core in range(2):

        @pl.when(c == core)
        def _():
            for copy in sent[core][-2:]:
                copy.wait_send()

    for job in att_jobs + mlp_jobs:
        job.end()


ANY = pl.BlockSpec(memory_space=pl.ANY)
VMEM = pl.BlockSpec(memory_space=pltpu.VMEM)
TWO4 = (2,) * 4
TWO5 = (2,) * 5
TWO6 = (2,) * 6
TWO7 = (2,) * 7


def shape(dims, kind=BF16):
    return jax.ShapeDtypeStruct(dims, kind)


def vmem(dims, kind=BF16):
    return pltpu.VMEM(dims, kind)


def params(number, mib):
    return pltpu.CompilerParams(
        collective_id=number, has_side_effects=True, vmem_limit_bytes=mib * MIB
    )


def dma(count):
    return pltpu.SemaphoreType.DMA((count,))


def forward(*operands):
    return pl.pallas_call(
        forward_kernel,
        name="forward",
        out_shape=(
            shape(TWO5 + (24, 16, 128)),
            shape((4, D, 768)),
            shape((D, D)),
            shape((D, 2048)),
            shape((D, 1024)),
            shape((2, 2, TOK, D)),
            shape((1024, 1024)),
            shape((D, TOK)),
            shape((D, TOK)),
            shape((TOK, D), F32),
            shape((8, D), F32),
            shape((2, 1024, 1024)),
            shape((1024, 1024)),
            shape((2, 2, TOK, D)),
        ),
        in_specs=[ANY] * 3 + [VMEM, ANY] + [VMEM] * 6,
        out_specs=[ANY] * 14,
        scratch_shapes=[
            vmem(TWO6 + (6, 5, 16, 128)),
            vmem(TWO5 + (2, 24, 16, 128)),
            vmem(TWO5 + (24, 16, 128)),
            vmem((4, D, 768)),
            vmem((D, D)),
            vmem((D, 2048)),
            vmem((8, D), F32),
            vmem((TOK, D)),
            vmem((1024, 1024)),
            vmem((TOK, 2048)),
            vmem((TOK, D)),
            vmem((TOK, D), F32),
            vmem((2, 2, TOK, D)),
            vmem((512, 1024)),
            vmem((2, 512, 1024)),
            vmem((2, D, TOK)),
            vmem((D, 1024)),
            vmem((1024, 1024)),
            vmem((2, TOK, D)),
            dma(140),
            dma(140),
            dma(4),
            dma(20),
        ],
        compiler_params=params(0, 63),
    )(*operands)


def backward(*operands):
    return pl.pallas_call(
        backward_kernel,
        name="backward",
        out_shape=(
            shape((2, 3, 5, 16, 128), F32),
            shape((4, 2, 6, 16, 128), F32),
            shape((24, 16, 128), F32),
            shape((TOK, D)),
            shape((TOK, D), F32),
            shape(TWO6 + (6, 5, 16, 128)),
            shape(TWO5 + (2, 24, 16, 128)),
            shape(TWO5 + (24, 16, 128)),
            shape((3, D, 1024)),
            shape((6, TOK, D)),
        ),
        in_specs=[ANY] + [VMEM] * 7 + [ANY] * 14,
        out_specs=[VMEM] * 3 + [ANY] * 7,
        scratch_shapes=[
            vmem((D, 1024)),
            vmem((2, 2, TOK, D)),
            vmem((1024, 1024)),
            vmem((2, 1024, 1024)),
            vmem((2, 384, D)),
            vmem((2, 256, 2048)),
            vmem(TWO5 + (2, 24, 16, 128)),
            vmem((5,) + TWO4 + (2, 5, 16, 128)),
            vmem(TWO5 + (24, 16, 128)),
            vmem((5,) + TWO4 + (7, 16, 128)),
            vmem((640, 16, 128)),
            vmem(TWO6 + (6, 5, 16, 128)),
            vmem((6,) + TWO5 + (5, 16, 128)),
            vmem((2, 384, 1024)),
            vmem((9, TOK, 512)),
            vmem((2, D, TOK)),
            vmem((TOK, D), F32),
            vmem((TOK, D), F32),
            vmem((2, 2, TOK, D)),
            vmem((2, TOK, D)),
            vmem((8, D), F32),
            vmem((8, D), F32),
            vmem((4, 2, 6, 16, 128)),
            vmem((3, 5, 16, 128)),
            dma(200),
            dma(200),
            dma(4),
            dma(12),
            dma(20),
            dma(2),
            dma(9),
        ],
        compiler_params=params(1, 63),
    )(*operands)


def tables():
    spread = np.zeros((384, 512), np.float32)
    for head in range(4):
        for lane in range(96):
            spread[head * 96 + lane, head * 128 + lane + (16 if lane >= 48 else 0)] = 1
    pick = np.zeros((128, D), np.float32)
    pick[np.arange(D) % 12, np.arange(D)] = 1
    owner = np.zeros((128, D), np.float32)
    order = np.array(GRAY)
    for gx in range(4):
        for gz in range(4):
            for gy in range(4):
                for core in range(2):
                    at = ((gx * 4 + gz) * 4 + gy) * 2 + core
                    device = ((order[gx] * 4 + order[gz]) * 4 + order[gy]) * 2 + core
                    owner[at, device * 12 : device * 12 + 12] = 1
    return [jnp.asarray(table, BF16) for table in (spread, pick, owner)]


def adamw_step(weight, moment_one, moment_two, gradient, rate, decay):
    first_new = BETA_ONE * moment_one + (1.0 - BETA_ONE) * gradient
    second_new = BETA_TWO * moment_two + (1.0 - BETA_TWO) * gradient * gradient
    unbiased_one = first_new / (1.0 - BETA_ONE**STEP)
    unbiased_two = second_new / (1.0 - BETA_TWO**STEP)
    weight_new = weight - rate * (
        unbiased_one / (jnp.sqrt(unbiased_two) + ADAM_EPSILON) + decay * weight
    )
    return (weight_new, first_new, second_new)


def hidden_chunks():
    chunks = []
    for x in range(4):
        for z in range(4):
            for yb in range(2):
                gx, gz = GRAY[x], GRAY[z]
                xb, xa, zb, za = gx // 2, gx % 2, gz // 2, gz % 2
                pieces = []
                for low in range(2):
                    for core in range(2):
                        ya = 1 - low if yb else low
                        pieces.append((2 * ya + core, xb, 2 * xa + zb, 32 * (2 * za + yb)))
                chunks.append((128 * ((x * 4 + z) * 2 + yb), pieces))
    return chunks


ATT_SPOTS = ((0, 0), (0, 1), (0, 2), (0, 3), (0, 4), (1, 3), (1, 0), (1, 1), (1, 2))


def prepare_kernel(qkv, out, upw, downw, gains, seg_row, freq, pick, att, up, down, cos, sin, bias):
    for number, (part, k) in enumerate(ATT_SPOTS):
        ref, width, start = (qkv, 768, 128 * number) if number < 6 else (out, 384, 128 * number - 768)
        pieces = [ref[:, width * at + start : width * at + start + 128] for at in range(4)]
        att[part, :, k] = jnp.concatenate(pieces, axis=0).astype(BF16).reshape(3, 16, 128)
    lines = dot(gains[...].astype(BF16), pick[0:12, 0:128])
    lines = jnp.concatenate([lines, jnp.zeros((14, 128), F32)], axis=0).astype(BF16)
    att[1, 0, 4] = lines
    att[1, 1:3, 4] = jnp.zeros((2, 16, 128), BF16)
    sources = {}
    for start, pieces in hidden_chunks():
        for at, (rank, high, tile, lane) in enumerate(pieces):
            sources[rank, high, tile, lane] = start + 32 * at
    for rank in range(4):
        for tile in range(4):
            quarters = []
            for quarter in range(4):
                base = 4096 * (quarter // 2)
                lanes = [base + sources[rank, quarter % 2, tile, 32 * at] for at in range(4)]
                quarters.append(jnp.concatenate([upw[:, lane : lane + 32] for lane in lanes], axis=1))
            block = jnp.concatenate(quarters, axis=0).astype(BF16).reshape(3, 16, 128)
            for third in range(3):
                up[rank, tile // 2, 2 * third + tile % 2] = block[third]
    for at in range(12):
        down[2 * at : 2 * at + 2] = downw[:, 128 * at : 128 * at + 128].astype(BF16).reshape(2, 16, 128)
    places = lax.broadcasted_iota(jnp.int32, (TOK, TOK), 1)
    seg_line = seg_row[...].astype(F32)
    seg_column = jnp.transpose(jnp.broadcast_to(seg_line, (128, TOK)))[:, 0:1]
    same = seg_column == seg_line
    first = jnp.min(jnp.where(same, places, TOK).astype(F32), axis=1, keepdims=True)
    rows = lax.broadcasted_iota(jnp.int32, (TOK, 128), 0).astype(F32)
    angles = (rows - first) * freq[...]
    cos[...] = jnp.cos(angles)
    lanes = lax.broadcasted_iota(jnp.int32, (TOK, 128), 1)
    sine = jnp.sin(angles)
    sin[...] = jnp.where(lanes < 64, -sine, sine)
    bias[...] = mask_bias(seg_column, seg_line)


def prepare(qkv, out, up, down, gains, segment_ids, pick):
    steps = np.float32(THETA) ** (-np.arange(0, HD, 2, dtype=np.float32) / np.float32(HD))
    gap = np.zeros((16,), np.float32)
    freq = jnp.asarray(np.concatenate([steps, gap, steps, gap]).reshape(1, 128), F32)
    return pl.pallas_call(
        prepare_kernel,
        name="prepare",
        out_shape=(
            shape((2, 3, 5, 16, 128)),
            shape((4, 2, 6, 16, 128)),
            shape((24, 16, 128)),
            shape((TOK, 128), F32),
            shape((TOK, 128), F32),
            shape((TOK, TOK), F32),
        ),
        in_specs=[VMEM] * 8,
        out_specs=[VMEM] * 6,
        compiler_params=pltpu.CompilerParams(vmem_limit_bytes=62 * MIB),
    )(qkv, out, up, down, gains.T, segment_ids.reshape(1, TOK), freq, pick)


def finish_kernel(att, up, down, *refs):
    old, new = (refs[0:5], refs[5:10], refs[10:15]), (refs[15:20], refs[20:25], refs[25:30])

    def step(number, at, gradient):
        values = [group[number][at] for group in old]
        for group, value in zip(new, adamw_step(*values, gradient, RATES[number], DECAYS[number])):
            group[number][at] = value

    everything = slice(None)
    for number, (part, k) in enumerate(ATT_SPOTS):
        which, width, start = (0, 768, 128 * number) if number < 6 else (1, 384, 128 * number - 768)
        block = att[part, :, k].reshape(48, 128)
        for at in range(4):
            lane = width * at + start
            step(which, (everything, slice(lane, lane + 128)), block[12 * at : 12 * at + 12])
    blocks = {}
    for rank in range(4):
        for tile in range(4):
            units = [up[rank, tile // 2, 2 * third + tile % 2] for third in range(3)]
            block = jnp.concatenate(units, axis=0)
            for quarter in range(4):
                blocks[rank, quarter, tile] = block[12 * quarter : 12 * quarter + 12]
    for start, pieces in hidden_chunks():
        for half in range(2):
            parts = [
                blocks[rank, 2 * half + high, tile][:, lane : lane + 32] for rank, high, tile, lane in pieces
            ]
            lane = 4096 * half + start
            step(2, (everything, slice(lane, lane + 128)), jnp.concatenate(parts, axis=1))
    for at in range(12):
        step(3, (everything, slice(128 * at, 128 * at + 128)), down[2 * at : 2 * at + 2].reshape(32, 128))
    step(4, (everything, everything), att[1, 0, 4][0:2, 0:12])


def finish(sums, masters, firsts, seconds):
    kinds = [shape(master.shape, F32) for master in masters]
    return pl.pallas_call(
        finish_kernel,
        name="finish",
        out_shape=kinds * 3,
        in_specs=[VMEM] * 18,
        out_specs=[VMEM] * 15,
        compiler_params=pltpu.CompilerParams(vmem_limit_bytes=62 * MIB),
    )(*sums, *masters, *firsts, *seconds)


def body(
    tokens_in,
    cotangent,
    segment_ids,
    proj_qkv,
    proj_out,
    proj_up,
    proj_down,
    norm_gains,
    first_qkv,
    first_out,
    first_up,
    first_down,
    first_gains,
    second_qkv,
    second_out,
    second_up,
    second_down,
    second_gains,
):
    spread, pick, owner = tables()
    att_units, up_units, down_units, cos, sin, bias = prepare(
        proj_qkv, proj_out, proj_up, proj_down, norm_gains, segment_ids, pick
    )
    (
        down_all, wq, wo, wgu, n2t, dy_all, heads, a_t, n1_t, middle, gains, gate_up, z_t, y_part,
    ) = forward(
        att_units, up_units, down_units, tokens_in, cotangent, bias, cos, sin, spread, pick, owner
    )
    att_sum, up_sum, down_sum, block_output, input_grad, *_ = backward(
        tokens_in, cos, sin, bias, spread, pick, owner, gains, cotangent,
        down_all, wq, wo, wgu, n2t, dy_all, heads, a_t, n1_t, middle, gate_up, z_t, y_part,
    )
    updated = finish(
        (att_sum, up_sum, down_sum),
        (proj_qkv, proj_out, proj_up, proj_down, norm_gains.T),
        (first_qkv, first_out, first_up, first_down, first_gains.T),
        (second_qkv, second_out, second_up, second_down, second_gains.T),
    )
    updated = [value.T if number % 5 == 4 else value for number, value in enumerate(updated)]
    return (block_output, input_grad, *updated)


def solution(mesh):
    rows = P("fsdp", None)
    return jax.shard_map(
        body,
        mesh=mesh,
        in_specs=(rows, rows, P("fsdp")) + (rows,) * 15,
        out_specs=(rows,) * 17,
        check_vma=False,
    )
```

```python
import functools
import math

import jax
import jax.numpy as jnp
import numpy as np
from jax import lax
from jax.experimental import pallas as pl
from jax.experimental.pallas import tpu as pltpu
from jax.sharding import PartitionSpec as P

H = 16
KVH = 8
HD = 96
FF = 4096
STEP = 10
D = 1536
TOK = 256


EPSILON = 1e-05
THETA = 100000.0
BETA_ONE = 0.9
BETA_TWO = 0.95
ADAM_EPSILON = 1e-08
RATES = (0.08, 0.3, 0.08, 0.05, 1.0)
DECAYS = (0.1, 0.1, 0.1, 0.1, 0.0)
MASKED = -1e30

MESH = pl.DeviceIdType.MESH
BF16 = jnp.bfloat16
F32 = jnp.float32
MIB = 1024 * 1024
LAG = 3

CUBE = ("xb", "xa", "zb", "za", "yb", "ya")
LINKS = ("xa", "xb", "za", "zb", "ya", "yb")
QUAD_LINKS = ("xa", "xb", "za", "zb", "yb")
GRAY = (0, 1, 3, 2)
FOUR = ((0, 1, 2, 3), (2, 3, 0, 1))


class Place:
    def __init__(self):
        me = lax.axis_index("fsdp")
        self.me = me
        self.c = lax.rem(me, 2)
        self.y = lax.rem(me // 2, 4)
        self.z = lax.rem(me // 8, 4)
        self.x = me // 32
        self.bit = {"c": self.c}
        for name in "xyz":
            at = getattr(self, name)
            self.bit[name + "b"] = at // 2
            self.bit[name + "a"] = lax.rem(at + at // 2, 2)

    def partner(self, *dims):
        at = {"x": self.x, "y": self.y, "z": self.z, "c": self.c}
        for dim in dims:
            name = dim[0]
            if dim == "c":
                at["c"] = 1 - at["c"]
            elif dim[1] == "a":
                at[name] = at[name] + 1 - 2 * lax.rem(at[name], 2)
            else:
                at[name] = 3 - at[name]
        return ((at["x"] * 4 + at["z"]) * 4 + at["y"]) * 2 + at["c"]


def greet(devices):
    barrier = pltpu.get_barrier_semaphore()
    for device in devices:
        pl.semaphore_signal(barrier, inc=1, device_id=(device,), device_id_type=MESH)
    pl.semaphore_wait(barrier, len(devices))


class Sems:
    def __init__(self, send, recv):
        self.send, self.recv, self.used = send, recv, 0

    def copy(self, src, dst, device):
        at = self.used
        self.used += 1
        assert at < self.send.shape[0]
        return pltpu.make_async_remote_copy(
            src_ref=src,
            dst_ref=dst,
            send_sem=self.send.at[at],
            recv_sem=self.recv.at[at],
            device_id=(device,),
            device_id_type=MESH,
        )


def spot(place, dims, done=(), flip=None):
    return tuple(
        pl.ds(0, 2) if dim in done else (1 - place.bit[dim] if dim == flip else place.bit[dim])
        for dim in dims
    )


def rotated(links, by):
    return links[by:] + links[:by]


UP_PARTS = ((0, 5), (5, 5), (10, 5), (15, 5), (20, 4))
DOWN_PARTS = ((0, 4), (4, 4), (8, 5), (13, 4), (17, 7))
TILES = ((0, 2, 0, 0, 0), (2, 2, 0, 2, 0), (4, 1, 0, 4, 0), (5, 1, 1, 3, 0), (6, 2, 1, 0, 1), (8, 1, 1, 2, 1))


class Gather:
    def __init__(self, place, sems, ref, dims, links, rotation, cut):
        self.place, self.sems, self.ref, self.dims, self.cut = place, sems, ref, dims, cut
        self.order, self.copies = rotated(links, rotation), []

    def step(self, number):
        if number > 0:
            self.copies[number - 1].wait_recv()
        if number < len(self.order):
            view = self.ref.at[spot(self.place, self.dims, self.order[:number]) + self.cut]
            copy = self.sems.copy(view, view, self.place.partner(self.order[number]))
            copy.start()
            self.copies.append(copy)

    def end(self):
        for copy in self.copies:
            copy.wait_send()


def each_block(place, dims, free, whole, visit):
    looped = tuple(dim for dim in free if dim not in whole)
    count = 2 ** len(looped)

    def at(i):
        index = []
        weight = count
        for dim in dims:
            if dim in whole:
                index.append(slice(None))
            elif dim in looped:
                weight //= 2
                index.append(lax.rem(i // weight, 2))
            else:
                index.append(place.bit[dim])
        return tuple(index)

    if count == 1:
        visit(at(0))
    else:
        pl.loop(0, count)(lambda i: visit(at(i)))


class Scatter:
    def __init__(self, place, sems, ref, far, got, dims, links, rotation, cuts, cut, counts):
        self.place, self.sems, self.ref, self.far, self.got = place, sems, ref, far, got
        self.dims, self.cut, self.counts = dims, cut, counts
        self.order = tuple(reversed(rotated(links, rotation)))
        self.rest = tuple(dim for dim in dims if dim != self.order[0])
        link, free = self.order[0], self.order[1:]
        there = spot(place, dims, free, flip=link)
        here = spot(place, dims, free)
        self.firsts = [sems.copy(ref.at[there + at], far.at[here + at], place.partner(link)) for at in cuts]
        self.size = math.prod(counts) * 2 ** len(free)
        self.copies = [None]

    def prepare(self, number):
        link = self.order[number]
        free = self.order[number + 1 :]
        src = self.ref.at[spot(self.place, self.dims, free, flip=link) + self.cut]
        dst = self.got.at[spot(self.place, self.rest, free)]
        self.copies.append(self.sems.copy(src, dst, self.place.partner(link)))

    def fetch(self, stage, sem):
        for copy in self.firsts:
            copy.wait_recv()
        link, free = self.order[0], self.order[1:]
        here = self.far.at[spot(self.place, self.dims, free, flip=link) + self.cut]
        self.stage = stage.reshape(*(2,) * len(free), *self.counts, 16, 128)
        self.staged = pltpu.make_async_copy(here, self.stage, sem)
        self.staged.start()

    def add(self, number):
        link = self.order[number]
        free = tuple(dim for dim in self.dims if dim in self.order[number + 1 :])
        whole = free[-2:]

        def visit(index):
            bits = dict(zip(self.dims, index))
            own = index + self.cut
            if number == 0:
                other = self.stage[tuple(bits[dim] for dim in self.rest)]
            else:
                other = self.got[tuple(1 - bits[dim] if dim == link else bits[dim] for dim in self.rest)]
            self.ref[own] = (self.ref[own].astype(F32) + other.astype(F32)).astype(BF16)

        each_block(self.place, self.dims, free, whole, visit)

    def step(self, number):
        if number == 1:
            self.staged.wait()
        elif number > 1:
            self.copies[number - 1].wait_recv()
        if number > 0:
            self.add(number - 1)
        if number < len(self.order):
            self.prepare(number)
            self.copies[number].start()

    def end(self):
        for copy in self.firsts + self.copies[1:]:
            copy.wait_send()


def first_adds(jobs, stage, sems):
    at = 0
    while at < len(jobs):
        batch, units = [], 0
        while at < len(jobs) and len(batch) < 9:
            if units + jobs[at].size > 640:
                break
            jobs[at].fetch(stage.at[pl.ds(units, jobs[at].size)], sems.at[len(batch)])
            batch.append(jobs[at])
            units += jobs[at].size
            at += 1
        for job in batch:
            job.step(1)


def natural_group(g):
    xb, xa = lax.rem(g // 16, 2), lax.rem(g // 8, 2)
    zb, za = lax.rem(g // 4, 2), lax.rem(g // 2, 2)
    yb = lax.rem(g, 2)
    x = 2 * xb + lax.rem(xa + xb, 2)
    z = 2 * zb + lax.rem(za + zb, 2)
    return (xb, xa, zb, za, yb), (x * 4 + z) * 2 + yb


def dot(left, right):
    return lax.dot_general(left, right, (((1,), (0,)), ((), ())), preferred_element_type=F32)


def dot_t(left, right):
    return lax.dot_general(left, right, (((1,), (1,)), ((), ())), preferred_element_type=F32)


def cols(i, width):
    return pl.ds(pl.multiple_of(i * width, width), width)


def head_pad(value, spread):
    high = value.astype(BF16)
    low = (value - high.astype(F32)).astype(BF16)
    return dot(high, spread) + dot(low, spread)


def turn(value, cos, sin):
    return value * cos + pltpu.roll(value, 64, 1) * sin


def mask_bias(seg_col, seg_row):
    rows = lax.broadcasted_iota(jnp.int32, (TOK, TOK), 0)
    columns = lax.broadcasted_iota(jnp.int32, (TOK, TOK), 1)
    allowed = jnp.logical_and(seg_col == seg_row, columns <= rows)
    return jnp.where(allowed, 0.0, MASKED).astype(F32)


def row_norm(value):
    return lax.rsqrt(jnp.mean(value * value, axis=-1, keepdims=True) + EPSILON)


def each_rows(step, visit, rows=TOK):
    @pl.loop(0, rows // step)
    def _(i):
        visit(pl.ds(pl.multiple_of(i * step, step), step))


def open_quarter(block, yb, quarter):
    pieces = [block[48 * at + 12 * quarter : 48 * at + 12 * quarter + 12] for at in FOUR[yb]]
    return jnp.concatenate(pieces, axis=0)


def sigmoid(value):
    return 1.0 / (1.0 + jnp.exp(-value))


def dot_first(left, right):
    return lax.dot_general(left, right, (((0,), (0,)), ((), ())), preferred_element_type=F32)


class Outs:
    def __init__(self, sems):
        self.sems, self.copies, self.ended = sems, [], 0

    def put(self, src, dst):
        assert len(self.copies) < self.sems.shape[0]
        copy = pltpu.make_async_copy(src, dst, self.sems.at[len(self.copies)])
        copy.start()
        self.copies.append(copy)

    def end(self):
        for copy in self.copies[self.ended :]:
            copy.wait()
        self.ended = len(self.copies)


def quad_of(place):
    return {(0, 1): place.partner("c"), (1, 0): place.partner("ya"), (1, 1): place.partner("ya", "c")}


def forward_kernel(
    att_in, up_in, down_in, x, dy, bias, cos, sin, spread, pick, owner,
    down_out, wq_out, wo_out, wgu_out, n2t_out, dy_all, q_out, at_out, n1t_out, m_out, g_out, gu_out, zt_out,
    y_out,
    att, up, down, wq, wo, wgu, gains, n1, q, apad, a, m, n2_all, z, gu, turned, n2t, zt, y,
    send, recv, local, out_sem,
):
    place = Place()
    sems = Sems(send, recv)
    outs = Outs(out_sem)
    quad = quad_of(place)
    sibling, across = quad[0, 1], quad[1, 0]
    greet([place.partner(link) for link in LINKS] + [quad[0, 1], quad[1, 1]])
    dims5 = CUBE[:5]
    home6 = spot(place, CUBE)
    home5 = spot(place, dims5)
    ya, c = place.bit["ya"], place.c
    rank = 2 * ya + c
    mine = pl.ds(3 * c, 3)
    six = pl.ds(pl.multiple_of(6 * rank, 2), 6)
    swap = sems.copy(att_in.at[1 - c], att.at[home6 + (mine,)], sibling)
    swap.start()
    starts = [
        pltpu.make_async_copy(att_in.at[c], att.at[home6 + (mine,)], local.at[0]),
        pltpu.make_async_copy(down_in, down.at[home5], local.at[1]),
        pltpu.make_async_copy(up_in.at[rank], up.at[home5 + (pl.ds(0, 2), six)], local.at[2]),
    ]
    for copy in starts:
        copy.start()
    scatter = []
    for (dya, dc), device in quad.items():
        to = 2 * (1 - ya if dya else ya) + (1 - c if dc else c)
        copy = sems.copy(up_in.at[to], up.at[home5 + (pl.ds(0, 2), six)], device)
        copy.start()
        scatter.append(copy)
    for copy in starts:
        copy.wait()
    swap.wait()
    first = [Gather(place, sems, att, CUBE, LINKS, by, (by,)) for by in range(6)]
    ups = [
        Gather(place, sems, up, dims5, QUAD_LINKS, by, (pl.ds(0, 2), pl.ds(*at)))
        for by, at in enumerate(UP_PARTS)
    ]
    downs = [Gather(place, sems, down, dims5, QUAD_LINKS, by, (pl.ds(*at),)) for by, at in enumerate(DOWN_PARTS)]
    second = ups + downs
    for number in range(7):
        for job in first:
            job.step(number)
        if number == 0:
            for copy in scatter:
                copy.wait()
        if number >= LAG:
            for job in second:
                job.step(number - LAG)
    dy_near = sems.copy(dy, dy_all.at[ya, c], sibling)
    dy_near.start()
    dy_far = sems.copy(dy, dy_all.at[ya, c], across)
    dy_far.start()

    wide, narrow = pl.ds(0, 640), pl.ds(640, 128)
    shared = {0: [], 1: []}
    for at in range(4):
        rows = pl.ds(GRAY[at] * 384, 384)
        for core, refs in ((0, [wq.at[:, rows, wide]]), (1, [wq.at[:, rows, narrow], wo.at[rows]])):
            shared[core].append([sems.copy(ref, ref, sibling) for ref in refs])
    gain_share = sems.copy(gains, gains, sibling)

    @pl.when(c == 1)
    def _():
        tiles = jnp.stack([att[..., 3 * core, 4, :, :].reshape(64, 16, 128) for core in range(2)], axis=1)
        tiles = tiles.reshape(128, 16, 128).astype(F32)
        lines = lax.broadcasted_iota(jnp.int32, (128, 16, 128), 1)
        for number in range(2):
            line = jnp.sum(jnp.where(lines == number, tiles, 0.0), axis=1).astype(BF16)
            vector = jnp.sum(dot(line, pick[...]) * owner[...].astype(F32), axis=0, keepdims=True)
            gains[number : number + 1, :] = vector
        gains[2:8, :] = jnp.zeros((6, D), F32)
        gain_share.start()

    for at in range(4):

        @pl.loop(0, 8)
        def _(part):
            bits, n = natural_group(at * 8 + part)
            rows = pl.ds(pl.multiple_of(n * 48, 16), 48)
            block = jnp.concatenate([att[bits][:, :, k].reshape(192, 128) for k in range(5)], axis=1)
            for yb in range(2):

                @pl.when(jnp.logical_and(bits[4] == yb, c == 0))
                def _():
                    for quarter in range(4):
                        wq[quarter, rows, 0:640] = open_quarter(block, yb, quarter)

                @pl.when(jnp.logical_and(bits[4] == yb, c == 1))
                def _():
                    for quarter in range(4):
                        piece = open_quarter(block[:, :512], yb, quarter)
                        wq[quarter, rows, 640:768] = piece[:, 384:]
                        wo[rows, 384 * quarter : 384 * quarter + 384] = piece[:, :384]

        for core in range(2):

            @pl.when(c == core)
            def _():
                for copy in shared[core][at]:
                    copy.start()


    @pl.when(c == 0)
    def _():
        gain_share.wait_recv()

    def norm_one(at):
        value = x[at, :].astype(F32)
        n1[at, :] = (value * row_norm(value) * gains[0:1, :]).astype(BF16)

    each_rows(64, norm_one)
    for core in range(2):

        @pl.when(c == core)
        def _():
            for at in range(4):
                for copy in shared[1 - core][at]:
                    copy.wait_recv()

    outs.put(wq, wq_out)
    outs.put(wo, wo_out)

    def heads(i, rotated_too):
        value = dot(n1[...], wq[i // 2, :, cols(lax.rem(i, 2), 384)])
        padded = head_pad(value, spread[...])
        for at in range(4):
            head = padded[:, 128 * at : 128 * at + 128]
            if rotated_too:
                head = turn(head, cos[...], sin[...])
            lanes = pl.ds(pl.multiple_of(lax.rem(i, 2) * 512 + 128 * at, 128), 128)
            q[cols(i // 2, 256), lanes] = head.astype(BF16)

    pl.loop(0, 4)(lambda i: heads(i, True))
    for job in ups:
        job.step(4)
    pl.loop(4, 6)(lambda i: heads(i, True))
    pl.loop(6, 8)(lambda i: heads(i, False))
    for job in downs:
        job.step(4)
    outs.put(q, q_out)

    own = n2_all.at[ya, c]
    near, far = [], []
    for half in range(2):
        start, seen = 128 * half, 128 * half + 128
        rows = pl.ds(start, 128)

        @pl.loop(0, 8)
        def _(j):
            pair = q[pl.ds(pl.multiple_of(j // 4 * 256 + start, 128), 128), cols(lax.rem(j, 4), 256)]
            both = jnp.concatenate([pair[:, :128], pair[:, 128:]], axis=0)
            key = q[512 : 512 + seen, cols(j, 128)]
            value = q[768 : 768 + seen, cols(j, 128)]
            mask = bias[rows, 0:seen]
            scores = dot_t(both, key) * (1.0 / math.sqrt(HD)) + jnp.concatenate([mask, mask], axis=0)
            exponent = jnp.exp(scores - jnp.max(scores, axis=-1, keepdims=True))
            weights = exponent / jnp.sum(exponent, axis=-1, keepdims=True)
            result = dot(weights.astype(BF16), value).astype(BF16)
            for at in range(2):
                lanes = pl.ds(pl.multiple_of(j * 256 + 128 * at, 128), 128)
                apad[rows, lanes] = result[128 * at : 128 * at + 128]

        @pl.loop(0, 4)
        def _(i):
            a[rows, cols(i, 384)] = dot_t(apad[rows, cols(i, 512)], spread[...]).astype(BF16)

        @pl.loop(0, 3)
        def _(i):
            m[rows, cols(i, 512)] = x[rows, cols(i, 512)].astype(F32) + dot(a[rows, :], wo[:, cols(i, 512)])

        def norm_two(i):
            at = pl.ds(pl.multiple_of(start + i * 64, 64), 64)
            value = m[at, :]
            own[at, :] = (value * row_norm(value) * gains[1:2, :]).astype(BF16)

        pl.loop(0, 2)(norm_two)
        near.append(sems.copy(own.at[rows], own.at[rows], sibling))
        near[half].start()
        far.append(sems.copy(own.at[rows], own.at[rows], across))
        far[half].start()
    outs.put(m, m_out)
    outs.put(gains, g_out)

    @pl.loop(0, 6)
    def _(i):
        turned[0, cols(i, 256), :] = jnp.transpose(n1[:, cols(i, 256)])
        turned[1, cols(i, 256), :] = jnp.transpose(a[:, cols(i, 256)])

    outs.put(turned.at[0], n1t_out)
    outs.put(turned.at[1], at_out)

    for job in ups:
        job.step(5)

    @pl.loop(0, 32)
    def _(g):
        bits, n = natural_group(g)
        rows = pl.ds(pl.multiple_of(n * 48, 16), 48)
        block = jnp.concatenate(
            [up[bits + (k // 2,)].reshape(12, 2, 16, 128)[:, k % 2].reshape(192, 128) for k in range(4)], axis=1
        )
        for yb in range(2):

            @pl.when(bits[4] == yb)
            def _():
                for quarter in range(4):
                    wgu[rows, 512 * quarter : 512 * quarter + 512] = open_quarter(block, yb, quarter)

    outs.put(wgu, wgu_out)
    for job in downs:
        job.step(5)
    outs.put(down, down_out)
    for copy in near:
        copy.wait_recv()

    def mlp(pair):
        rows = cols(pair, 512)

        @pl.loop(0, 4)
        def _(i):
            left = n2_all[pair].reshape(512, D)
            gate = dot(left, wgu[:, cols(i, 256)])
            upward = dot(left, wgu[:, cols(i + 4, 256)])
            hidden = gate * sigmoid(gate) * upward
            z[:, cols(i, 256)] = hidden.astype(BF16)
            gu[0, :, cols(i, 256)] = gate.astype(BF16)
            gu[1, :, cols(i, 256)] = upward.astype(BF16)

        outs.put(gu, gu_out.at[:, rows])

        @pl.loop(0, 6)
        def _(i):
            right = jnp.concatenate(
                [down[..., pl.ds(4 * i + 2 * at, 2), :, :].reshape(1024, 128) for at in range(2)], axis=1
            )
            y[:, :, cols(i, 256)] = dot(z[...], right).astype(BF16).reshape(2, TOK, 256)

        outs.put(y, y_out.at[pair])

        @pl.loop(0, 6)
        def _(i):
            n2t[cols(i, 256), rows] = jnp.transpose(n2_all[pair, :, :, cols(i, 256)].reshape(512, 256))

        outs.put(n2t.at[:, rows], n2t_out.at[:, rows])

        @pl.loop(0, 4)
        def _(i):
            zt[cols(i, 256), rows] = jnp.transpose(z[:, cols(i, 256)])

        outs.put(zt.at[:, rows], zt_out.at[:, rows])

    def pass_on(half):
        far[half].wait_recv()
        there = n2_all.at[1 - ya, c, pl.ds(128 * half, 128)]
        copy = sems.copy(there, there, sibling)
        copy.start()
        return copy

    mlp(ya)
    onward = [pass_on(0)]

    dy_far.wait_recv()
    dy_onward = sems.copy(dy_all.at[1 - ya, c], dy_all.at[1 - ya, c], sibling)
    dy_onward.start()
    onward.append(pass_on(1))
    for copy in onward:
        copy.wait_recv()
    outs.end()
    mlp(1 - ya)
    for copy in near + far + onward:
        copy.wait_send()
    dy_near.wait()
    dy_far.wait_send()
    dy_onward.wait()
    for core in range(2):

        @pl.when(c == core)
        def _():
            for at in range(4):
                for copy in shared[core][at]:
                    copy.wait_send()

    @pl.when(c == 1)
    def _():
        gain_share.wait_send()

    for job in first + second:
        job.end()
    outs.end()


def backward_kernel(
    x, cos, sin, bias, spread, pick, owner, gains, cotangent,
    down_in, wq_in, wo_in, wgu_in, n2t_in, dy_in, q_in, at_in, n1t_in, m_in, gu_in, zt_in, y_in,
    att_out, up_out, down_out, block_out, grad_out,
    far_att, far_up, far_down, land, quad_got,
    n2t, dy, zt, gu, wo_slots, wgu_slots, g_up, got_up, g_down, got_down, stage, g_att, got_att,
    dw, rt, lhs, dm, dn1, p, t, dg, dg_got, up_land, att_land,
    send, recv, local, slot_sem, load_sem, out_sem, stage_sem,
):
    place = Place()
    sems = Sems(send, recv)
    outs = Outs(out_sem)
    quad = quad_of(place)
    sibling, across = quad[0, 1], quad[1, 0]
    greet([place.partner(link) for link in LINKS] + [quad[0, 1], quad[1, 1]])
    dims5 = CUBE[:5]
    home6 = spot(place, CUBE)
    home5 = spot(place, dims5)
    ya, c = place.bit["ya"], place.c
    rank = 2 * ya + c
    loads = {}

    def load(name, src, dst):
        assert len(loads) < load_sem.shape[0]
        copy = pltpu.make_async_copy(src, dst, load_sem.at[len(loads)])
        copy.start()
        loads[name] = copy

    load("zt", zt_in, zt)
    load("dy", cotangent, dy.at[ya, c])
    load("dy1", dy_in.at[ya, 1 - c], dy.at[ya, 1 - c])
    load("dy2", dy_in.at[1 - ya], dy.at[1 - ya])
    load("gu", gu_in, gu)

    wd_slots = [stage.at[pl.ds(192 * slot, 192)].reshape(2, 2, 2, 24, 16, 128) for slot in range(2)]

    def fetch_wd(i):
        slot = i % 2
        whole = (pl.ds(0, 2),) * 3 + (pl.ds(0, 24), pl.ds(0, 16), pl.ds(0, 128))
        return pltpu.make_async_copy(down_in.at[(i // 2, i % 2) + whole], wd_slots[slot], slot_sem.at[slot])

    fetch_wd(0).start()
    fetch_wd(1).start()

    y_away = sems.copy(y_in.at[1 - ya, 1 - c], quad_got.at[0], sibling)
    y_away.start()
    y_near = sems.copy(y_in.at[ya, 1 - c], quad_got.at[1], sibling)
    y_near.start()

    up_jobs = [
        Scatter(
            place, sems, g_up, far_up, got_up.at[by, :, :, :, :, :, pl.ds(0, at[1])], dims5, QUAD_LINKS, by,
            [(pair, pl.ds(*at)) for pair in range(2)], (pl.ds(0, 2), pl.ds(*at)), (2, at[1]),
        )
        for by, at in enumerate(UP_PARTS)
    ]
    down_jobs = [
        Scatter(
            place, sems, g_down, far_down, got_down.at[by, :, :, :, :, pl.ds(0, at[1])], dims5, QUAD_LINKS, by,
            [(pl.ds(*at),)], (pl.ds(*at),), (at[1],),
        )
        for by, at in enumerate(DOWN_PARTS)
    ]
    att_jobs = [
        Scatter(
            place, sems, g_att, far_att, got_att.at[by], CUBE, LINKS, by,
            [(by, pl.ds(0, 2)), (by, pl.ds(2, 2)), (by, pl.ds(4, 1))], (by, pl.ds(0, 5)), (5,),
        )
        for by in range(6)
    ]
    mlp_jobs = up_jobs + down_jobs

    for name in ("zt", "dy", "dy1", "dy2"):
        loads[name].wait()
    for i in range(6):

        @pl.loop(0, 4)
        def _(at):
            right = dy[:, :, :, pl.ds(256 * i, 256)].reshape(1024, 256)
            value = dot(zt[cols(at, 256), :], right).astype(BF16)
            for part in range(2):
                piece = value[:, 128 * part : 128 * part + 128].reshape(2, 2, 2, 2, 16, 128)
                g_down[at // 2, lax.rem(at, 2), :, :, :, pl.ds(4 * i + 2 * part, 2)] = piece

        for job, (start, count) in zip(down_jobs, DOWN_PARTS):
            if 4 * i < start + count <= 4 * i + 4:
                job.firsts[0].start()

    def fetch_wo(i):
        slot = i % 2
        return pltpu.make_async_copy(wo_in.at[pl.ds(384 * i, 384)], wo_slots.at[slot], slot_sem.at[4 + slot])

    def fetch_wgu(i, slot):
        return pltpu.make_async_copy(wgu_in.at[cols(i, 256)], wgu_slots.at[slot], slot_sem.at[2 + slot])

    fetch_wgu(0, 0).start()
    fetch_wgu(1, 1).start()
    fetch_wo(0).start()
    fetch_wo(1).start()
    loads["gu"].wait()
    load("n2t", n2t_in, n2t)
    load("m", m_in, dm)
    load("n1t", n1t_in, lhs.at[0])
    load("at", at_in, lhs.at[1])
    for i in range(4):
        fetch_wd(i).wait()

        @pl.loop(0, 2)
        def _(pair):
            rows = cols(pair, 512)
            lanes = pl.ds(256 * i, 256)
            right = jnp.concatenate(
                [wd_slots[i % 2][:, :, :, 2 * at : 2 * at + 2].reshape(256, 128) for at in range(12)], axis=1
            )
            dz = dot_t(dy[pair].reshape(512, D), right)
            gate = gu[0, rows, lanes].astype(F32)
            upward = gu[1, rows, lanes].astype(F32)
            sg = sigmoid(gate)
            gu[0, rows, lanes] = (dz * upward * sg * (1.0 + gate * (1.0 - sg))).astype(BF16)
            gu[1, rows, lanes] = (dz * gate * sg).astype(BF16)

        if i < 2:
            fetch_wd(i + 2).start()

    aways, fars = [], []

    def mix(i):
        lanes = pl.ds(256 * i, 256)
        aways[i].wait_recv()

        def visit(at):
            total = p[1 - ya, c, at, lanes].astype(F32) + t[1, at, lanes].astype(F32)
            p[1 - ya, c, at, lanes] = total.astype(BF16)

        each_rows(128, visit)
        fars.append(sems.copy(p.at[1 - ya, c, :, lanes], quad_got.at[5, :, lanes], across))
        fars[i].start()

    for i in range(6):
        slot = i % 2
        lanes = pl.ds(256 * i, 256)
        fetch_wgu(i, slot).wait()

        @pl.loop(0, 2)
        def _(pair):
            rows = cols(pair, 512)
            part = dot_t(gu[0, rows, :], wgu_slots[slot, :, 0:1024])
            part = part + dot_t(gu[1, rows, :], wgu_slots[slot, :, 1024:2048])
            p[pair, :, :, lanes] = part.astype(BF16).reshape(2, TOK, 256)

        if i < 4:
            fetch_wgu(i + 2, slot).start()
        aways.append(sems.copy(p.at[1 - ya, 1 - c, :, lanes], t.at[1, :, lanes], sibling))
        aways[i].start()
        if i > 0:
            mix(i - 1)
    near = sems.copy(p.at[ya, 1 - c], t.at[0], sibling)
    near.start()
    mix(5)

    def fetch(src, dst):
        copy = pltpu.make_async_copy(src, dst, local.at[3])
        copy.start()
        copy.wait()

    def add_into(total, term):
        def visit(at):
            total[at, :] = (total[at, :].astype(F32) + term[at, :].astype(F32)).astype(BF16)

        each_rows(64, visit)

    def fold_into(value, width, at, store):
        zb = lax.rem(at, 2)
        for part in range(4):
            z, yb = part // 2, part % 2
            row = part * 48
            pieces = [
                value[row + 12 * to : row + 12 * to + 12, width * quarter : width * quarter + width]
                for to in FOUR[yb]
                for quarter in range(4)
            ]
            folded = jnp.concatenate(pieces, axis=0).reshape(2, 6, 16, width)
            store((at // 4, lax.rem(at // 2, 2), zb, z + zb * (1 - 2 * z), yb), folded)

    def natural_rows(at):
        x = at // 2
        x = x + lax.rem(x // 2, 2) * (1 - 2 * lax.rem(x, 2))
        return pl.ds(pl.multiple_of(x * 384 + lax.rem(at, 2) * 192, 64), 192)

    loads["n2t"].wait()
    for pair in range(2):

        @pl.loop(0, 8)
        def _(at):
            rows = natural_rows(at)
            right = jnp.concatenate(
                [gu[quarter // 2, :, pl.ds((quarter % 2) * 512 + 256 * pair, 256)] for quarter in range(4)], axis=1
            )
            value = dot(n2t[rows, :], right).astype(BF16)

            def store(index, folded):
                folded = folded.reshape(12, 16, 256)
                halves = jnp.stack([folded[:, :, :128], folded[:, :, 128:]], axis=1)
                g_up[index + (pair,)] = halves.reshape(24, 16, 128)

            fold_into(value, 256, at, store)

        for job in up_jobs:
            job.firsts[pair].start()

    near.wait_recv()
    for copy in fars:
        copy.wait_recv()
    fetch(quad_got.at[5], t.at[1])
    loads["m"].wait()
    load("q", q_in, gu.at[0])
    dg[...] = jnp.zeros((8, D), F32)

    def back_two(at):
        value = dm[at, :]
        r = row_norm(value)
        xh = value * r
        dn = p[ya, c, at, :].astype(F32) + t[0, at, :].astype(F32) + t[1, at, :].astype(F32)
        dg[1:2, :] = dg[1:2, :] + jnp.sum(dn * xh, axis=0, keepdims=True)
        e = dn * gains[1:2, :]
        grad = dy[ya, c, at, :].astype(F32) + r * (e - xh * jnp.mean(xh * e, axis=-1, keepdims=True))
        dm[at, :] = grad
        low = grad.astype(BF16)
        for k in range(3):
            for quarter in range(4):
                start = quarter * 384 + k * 128
                rt[6 + k, at, 128 * quarter : 128 * quarter + 128] = low[:, start : start + 128]

    each_rows(32, back_two)
    load("x", x, dy.at[ya, c])

    y_away.wait_recv()
    load("y0", y_in.at[1 - ya, c], t.at[0])
    load("y1", quad_got.at[0], t.at[1])

    for i in range(4):
        fetch_wo(i).wait()
        left = jnp.concatenate(
            [rt[6 + k, :, 128 * quarter : 128 * quarter + 128] for quarter in range(4) for k in range(3)], axis=1
        )
        da = dot_t(left, wo_slots[i % 2]).astype(BF16)
        zt[256 * (i // 2) : 256 * (i // 2) + 256, 512 * (i % 2) : 512 * (i % 2) + 512] = dot(
            da, spread[...]
        ).astype(BF16)
        if i < 2:
            fetch_wo(i + 2).start()

    tile_copies = {}
    for number, (u, count, core, k, out) in enumerate(TILES):
        for at in range(4):
            lanes = pl.ds(0, 512 * count)
            tile_copies[number, at] = sems.copy(
                dw.at[at % 2, :, lanes], land.at[number % 3, pl.ds(384 * at, 384), lanes], sibling
            )
    sent = {0: [], 1: []}

    def tile_right(u, count):
        return jnp.concatenate(
            [rt[u + at, :, 128 * quarter : 128 * quarter + 128] for quarter in range(4) for at in range(count)], axis=1
        )

    def give(number):
        u, count, owner_core, k, out = TILES[number]
        core = 1 - owner_core

        @pl.when(c == core)
        def _():
            right = tile_right(u, count)
            for at in range(4):
                if len(sent[core]) >= 2:
                    sent[core][-2].wait_send()
                left = lhs[out, 384 * at : 384 * at + 384, :]
                dw[at % 2, :, 0 : 512 * count] = dot(left, right).astype(BF16)
                tile_copies[number, at].start()
                sent[core].append(tile_copies[number, at])

    takes = {0: (0, 1, 2), 1: (4, 5, 3)}

    def land_copies(number, place_at):
        lanes = pl.ds(0, 512 * TILES[number][1])
        halves = []
        for half in range(2):
            rows = pl.ds(768 * half, 768)
            ref = n2t.at[rows, lanes] if place_at == 0 else (zt.at[pl.ds(0, 768), lanes], gu.at[0, pl.ds(0, 768), lanes])[half]
            halves.append(
                pltpu.make_async_copy(land.at[number % 3, rows, lanes], ref, slot_sem.at[2 * place_at + half])
            )
        return halves

    def await_land(turn, core):
        number = takes[core][turn]
        for at in range(4):
            tile_copies[number, at].wait_recv()
        for copy in land_copies(number, turn % 2):
            copy.start()

    def take(turn, core):
        number = takes[core][turn]
        u, count, _, k, out = TILES[number]

        @pl.when(c == core)
        def _():
            if turn == 0:
                await_land(0, core)
            for copy in land_copies(number, turn % 2):
                copy.wait()
            if turn < 2:
                await_land(turn + 1, core)
            for half in range(2):

                @pl.loop(4 * half, 4 * half + 4)
                def _(at):
                    rows = natural_rows(at)
                    if turn % 2 == 0:
                        came = n2t[rows, 0 : 512 * count]
                    else:
                        start = pl.multiple_of(rows.start - 768 * half, 64)
                        came = (zt, gu.at[0])[half][pl.ds(start, 192), 0 : 512 * count]
                    value = dot(lhs[out, rows, :], tile_right(u, count)) + came.astype(F32)

                    def store(index, folded):
                        for spot_ya in range(2):
                            for part in range(count):
                                piece = folded[spot_ya, :, :, 128 * part : 128 * part + 128]
                                g_att[index + (spot_ya, slice(None), k + part)] = piece

                    fold_into(value.astype(BF16), 128 * count, at, store)

            if k + count in (2, 4, 5):
                for job in att_jobs:
                    job.firsts[(k + count) // 2 - 1 if k + count < 5 else 2].start()

    loads["at"].wait()
    loads["n1t"].wait()
    give(4)
    give(5)
    loads["y0"].wait()
    loads["y1"].wait()
    add_into(t.at[0], t.at[1])
    y_far = sems.copy(t.at[0], quad_got.at[2], across)
    y_far.start()
    first_adds(mlp_jobs, stage, stage_sem)
    loads["q"].wait()
    scale = 1.0 / math.sqrt(HD)

    @pl.loop(0, 8)
    def _(j):
        rows, lanes = cols(j // 4, 256), cols(lax.rem(j, 4), 256)
        pair = gu[0, rows, lanes]
        da = zt[rows, lanes]
        key = gu[0, 512:768, cols(j, 128)]
        value = gu[0, 768:1024, cols(j, 128)]
        dk = jnp.zeros((TOK, 128), F32)
        dv = jnp.zeros((TOK, 128), F32)
        for at in range(2):
            query = pair[:, 128 * at : 128 * at + 128]
            grad = da[:, 128 * at : 128 * at + 128]
            scores = dot_t(query, key) * scale + bias[...]
            exponent = jnp.exp(scores - jnp.max(scores, axis=-1, keepdims=True))
            weights = exponent / jnp.sum(exponent, axis=-1, keepdims=True)
            dv = dv + dot_first(weights.astype(BF16), grad)
            dp = dot_t(grad, value)
            ds = weights * (dp - jnp.sum(weights * dp, axis=-1, keepdims=True))
            ds = ds.astype(BF16)
            dq = dot(ds, key) * scale
            dk = dk + dot_first(ds, query)
            here = pl.ds(pl.multiple_of(lax.rem(j, 4) * 256 + 128 * at, 128), 128)
            gu[1, rows, here] = turn(dq, cos[...], -sin[...]).astype(BF16)
        gu[1, 512:768, cols(j, 128)] = turn(dk * scale, cos[...], -sin[...]).astype(BF16)
        gu[1, 768:1024, cols(j, 128)] = dv.astype(BF16)

    for job in mlp_jobs:
        job.step(2)
    @pl.loop(0, 8)
    def _(i):
        padded = gu[1, cols(i // 2, 256), cols(lax.rem(i, 2), 512)]
        flat = dot_t(padded, spread[...]).astype(BF16)
        for part in range(3):
            rt[lax.rem(i, 2) * 3 + part, :, cols(i // 2, 128)] = flat[:, 128 * part : 128 * part + 128]

    for number in (3, 0, 1, 2):
        give(number)
    for job in mlp_jobs:
        job.step(3)
    for number in range(3):
        for core in range(2):
            take(number, core)
    for job in mlp_jobs:
        job.step(4)
    def fetch_wq(i):
        slot = i % 2
        ref = (n2t, zt)[slot]
        return [
            pltpu.make_async_copy(
                wq_in.at[quarter, pl.ds(256 * i, 256)],
                ref.at[pl.ds(256 * quarter, 256), pl.ds(0, 768)],
                slot_sem.at[4 + 4 * slot + quarter],
            )
            for quarter in range(4)
        ]

    for i in range(6):
        for ahead in (0, 1) if i == 0 else (i + 1,):
            if ahead < 6:
                for copy in fetch_wq(ahead):
                    copy.start()
        for copy in fetch_wq(i):
            copy.wait()
        weight = (n2t, zt)[i % 2]
        total = jnp.zeros((TOK, 256), F32)
        for quarter in range(4):
            left = jnp.concatenate([rt[k, :, 128 * quarter : 128 * quarter + 128] for k in range(6)], axis=1)
            total = total + dot_t(left, weight[256 * quarter : 256 * quarter + 256, 0:768])
        dn1[:, 256 * i : 256 * i + 256] = total

    def back_one(at):
        value = dy[ya, c, at, :].astype(F32)
        r = row_norm(value)
        xh = value * r
        dn = dn1[at, :]
        dg[0:1, :] = dg[0:1, :] + jnp.sum(dn * xh, axis=0, keepdims=True)
        e = dn * gains[0:1, :]
        dn1[at, :] = dm[at, :] + r * (e - xh * jnp.mean(xh * e, axis=-1, keepdims=True))

    loads["x"].wait()
    each_rows(32, back_one)
    outs.put(dn1, grad_out)
    dg_copy = sems.copy(dg, dg_got, sibling)

    @pl.when(c == 0)
    def _():
        dg_copy.start()
        dg_copy.wait_send()

    @pl.when(c == 1)
    def _():
        g_att[(slice(None),) * 6 + (slice(None), 4)] = jnp.zeros(TWO6 + (6, 16, 128), BF16)
        dg_copy.wait_recv()
        lines = lax.broadcasted_iota(jnp.int32, (128, 16, 128), 1)
        tiles = jnp.zeros((128, 16, 128), F32)
        for number in range(2):
            vector = dg[number : number + 1, :] + dg_got[number : number + 1, :]
            spread_out = (owner[...].astype(F32) * vector).astype(BF16)
            line = dot_t(spread_out, pick[...])
            tiles = jnp.where(lines == number, line.reshape(128, 1, 128), tiles)
        tiles = tiles.astype(BF16).reshape(TWO7 + (16, 128))
        for core in range(2):
            g_att[(slice(None),) * 6 + (3 * core, 4)] = tiles[:, :, :, :, :, :, core]
        for job in att_jobs:
            job.firsts[2].start()

    for job in mlp_jobs:
        job.step(5)
    last = []
    for (dya, dc), device in quad.items():
        to = 2 * (1 - ya if dya else ya) + (1 - c if dc else c)
        src = g_up.at[home5 + (pl.ds(0, 2), pl.ds(pl.multiple_of(6 * to, 2), 6))]
        copy = sems.copy(src, up_land.at[rank], device)
        copy.start()
        last.append(copy)
    up_out[rank] = g_up[home5 + (slice(None), pl.ds(pl.multiple_of(6 * rank, 2), 6))].astype(F32)
    down_out[...] = g_down[home5].astype(F32)
    first_adds(att_jobs, stage, stage_sem)

    outs.end()
    for copy in aways + fars + [near]:
        copy.wait_send()
    y_far.wait_send()
    y_near.wait_recv()
    y_far.wait_recv()
    load("m2", m_in, dm)
    load("y2", y_in.at[ya, c], t.at[0])
    load("y3", quad_got.at[1], t.at[1])
    load("y4", quad_got.at[2], p.at[0, 0])
    for name in ("m2", "y2", "y3", "y4"):
        loads[name].wait()

    def add_y(at):
        total = dm[at, :] + t[0, at, :].astype(F32) + t[1, at, :].astype(F32) + p[0, 0, at, :].astype(F32)
        t[0, at, :] = total.astype(BF16)

    each_rows(64, add_y)
    outs.put(t.at[0], block_out)
    for number in range(2, 7):
        for job in att_jobs:
            job.step(number)
    att_last = sems.copy(g_att.at[home6 + (pl.ds(3 - 3 * c, 3),)], att_land, sibling)
    att_last.start()
    att_out[c] = g_att[home6 + (pl.ds(3 * c, 3),)].astype(F32)
    for copy in last:
        copy.wait()
    att_last.wait()
    for dya, dc in quad:
        to = 2 * (1 - ya if dya else ya) + (1 - c if dc else c)
        up_out[to] = up_land[to].astype(F32)
    att_out[1 - c] = att_land[...].astype(F32)
    for copy in (y_away, y_near):
        copy.wait_send()
    outs.end()
    for core in range(2):

        @pl.when(c == core)
        def _():
            for copy in sent[core][-2:]:
                copy.wait_send()

    for job in att_jobs + mlp_jobs:
        job.end()


ANY = pl.BlockSpec(memory_space=pl.ANY)
VMEM = pl.BlockSpec(memory_space=pltpu.VMEM)
TWO4 = (2,) * 4
TWO5 = (2,) * 5
TWO6 = (2,) * 6
TWO7 = (2,) * 7


def shape(dims, kind=BF16):
    return jax.ShapeDtypeStruct(dims, kind)


def vmem(dims, kind=BF16):
    return pltpu.VMEM(dims, kind)


def params(number, mib):
    return pltpu.CompilerParams(
        collective_id=number, has_side_effects=True, vmem_limit_bytes=mib * MIB
    )


def dma(count):
    return pltpu.SemaphoreType.DMA((count,))


def forward(*operands):
    return pl.pallas_call(
        forward_kernel,
        name="forward",
        out_shape=(
            shape(TWO5 + (24, 16, 128)),
            shape((4, D, 768)),
            shape((D, D)),
            shape((D, 2048)),
            shape((D, 1024)),
            shape((2, 2, TOK, D)),
            shape((1024, 1024)),
            shape((D, TOK)),
            shape((D, TOK)),
            shape((TOK, D), F32),
            shape((8, D), F32),
            shape((2, 1024, 1024)),
            shape((1024, 1024)),
            shape((2, 2, TOK, D)),
        ),
        in_specs=[ANY] * 3 + [VMEM, ANY] + [VMEM] * 6,
        out_specs=[ANY] * 14,
        scratch_shapes=[
            vmem(TWO6 + (6, 5, 16, 128)),
            vmem(TWO5 + (2, 24, 16, 128)),
            vmem(TWO5 + (24, 16, 128)),
            vmem((4, D, 768)),
            vmem((D, D)),
            vmem((D, 2048)),
            vmem((8, D), F32),
            vmem((TOK, D)),
            vmem((1024, 1024)),
            vmem((TOK, 2048)),
            vmem((TOK, D)),
            vmem((TOK, D), F32),
            vmem((2, 2, TOK, D)),
            vmem((512, 1024)),
            vmem((2, 512, 1024)),
            vmem((2, D, TOK)),
            vmem((D, 1024)),
            vmem((1024, 1024)),
            vmem((2, TOK, D)),
            dma(140),
            dma(140),
            dma(4),
            dma(20),
        ],
        compiler_params=params(0, 63),
    )(*operands)


def backward(*operands):
    return pl.pallas_call(
        backward_kernel,
        name="backward",
        out_shape=(
            shape((2, 3, 5, 16, 128), F32),
            shape((4, 2, 6, 16, 128), F32),
            shape((24, 16, 128), F32),
            shape((TOK, D)),
            shape((TOK, D), F32),
            shape(TWO6 + (6, 5, 16, 128)),
            shape(TWO5 + (2, 24, 16, 128)),
            shape(TWO5 + (24, 16, 128)),
            shape((3, D, 1024)),
            shape((6, TOK, D)),
        ),
        in_specs=[ANY] + [VMEM] * 7 + [ANY] * 14,
        out_specs=[VMEM] * 3 + [ANY] * 7,
        scratch_shapes=[
            vmem((D, 1024)),
            vmem((2, 2, TOK, D)),
            vmem((1024, 1024)),
            vmem((2, 1024, 1024)),
            vmem((2, 384, D)),
            vmem((2, 256, 2048)),
            vmem(TWO5 + (2, 24, 16, 128)),
            vmem((5,) + TWO4 + (2, 5, 16, 128)),
            vmem(TWO5 + (24, 16, 128)),
            vmem((5,) + TWO4 + (7, 16, 128)),
            vmem((640, 16, 128)),
            vmem(TWO6 + (6, 5, 16, 128)),
            vmem((6,) + TWO5 + (5, 16, 128)),
            vmem((2, 384, 1024)),
            vmem((9, TOK, 512)),
            vmem((2, D, TOK)),
            vmem((TOK, D), F32),
            vmem((TOK, D), F32),
            vmem((2, 2, TOK, D)),
            vmem((2, TOK, D)),
            vmem((8, D), F32),
            vmem((8, D), F32),
            vmem((4, 2, 6, 16, 128)),
            vmem((3, 5, 16, 128)),
            dma(200),
            dma(200),
            dma(4),
            dma(12),
            dma(20),
            dma(2),
            dma(9),
        ],
        compiler_params=params(1, 63),
    )(*operands)


def tables():
    spread = np.zeros((384, 512), np.float32)
    for head in range(4):
        for lane in range(96):
            spread[head * 96 + lane, head * 128 + lane + (16 if lane >= 48 else 0)] = 1
    pick = np.zeros((128, D), np.float32)
    pick[np.arange(D) % 12, np.arange(D)] = 1
    owner = np.zeros((128, D), np.float32)
    order = np.array(GRAY)
    for gx in range(4):
        for gz in range(4):
            for gy in range(4):
                for core in range(2):
                    at = ((gx * 4 + gz) * 4 + gy) * 2 + core
                    device = ((order[gx] * 4 + order[gz]) * 4 + order[gy]) * 2 + core
                    owner[at, device * 12 : device * 12 + 12] = 1
    return [jnp.asarray(table, BF16) for table in (spread, pick, owner)]


def adamw_step(weight, moment_one, moment_two, gradient, rate, decay):
    first_new = BETA_ONE * moment_one + (1.0 - BETA_ONE) * gradient
    second_new = BETA_TWO * moment_two + (1.0 - BETA_TWO) * gradient * gradient
    unbiased_one = first_new / (1.0 - BETA_ONE**STEP)
    unbiased_two = second_new / (1.0 - BETA_TWO**STEP)
    weight_new = weight - rate * (
        unbiased_one / (jnp.sqrt(unbiased_two) + ADAM_EPSILON) + decay * weight
    )
    return (weight_new, first_new, second_new)


def hidden_chunks():
    chunks = []
    for x in range(4):
        for z in range(4):
            for yb in range(2):
                gx, gz = GRAY[x], GRAY[z]
                xb, xa, zb, za = gx // 2, gx % 2, gz // 2, gz % 2
                pieces = []
                for low in range(2):
                    for core in range(2):
                        ya = 1 - low if yb else low
                        pieces.append((2 * ya + core, xb, 2 * xa + zb, 32 * (2 * za + yb)))
                chunks.append((128 * ((x * 4 + z) * 2 + yb), pieces))
    return chunks


ATT_SPOTS = ((0, 0), (0, 1), (0, 2), (0, 3), (0, 4), (1, 3), (1, 0), (1, 1), (1, 2))


def prepare_kernel(qkv, out, upw, downw, gains, seg_row, freq, pick, att, up, down, cos, sin, bias):
    for number, (part, k) in enumerate(ATT_SPOTS):
        ref, width, start = (qkv, 768, 128 * number) if number < 6 else (out, 384, 128 * number - 768)
        pieces = [ref[:, width * at + start : width * at + start + 128] for at in range(4)]
        att[part, :, k] = jnp.concatenate(pieces, axis=0).astype(BF16).reshape(3, 16, 128)
    lines = dot(gains[...].astype(BF16), pick[0:12, 0:128])
    lines = jnp.concatenate([lines, jnp.zeros((14, 128), F32)], axis=0).astype(BF16)
    att[1, 0, 4] = lines
    att[1, 1:3, 4] = jnp.zeros((2, 16, 128), BF16)
    sources = {}
    for start, pieces in hidden_chunks():
        for at, (rank, high, tile, lane) in enumerate(pieces):
            sources[rank, high, tile, lane] = start + 32 * at
    for rank in range(4):
        for tile in range(4):
            quarters = []
            for quarter in range(4):
                base = 4096 * (quarter // 2)
                lanes = [base + sources[rank, quarter % 2, tile, 32 * at] for at in range(4)]
                quarters.append(jnp.concatenate([upw[:, lane : lane + 32] for lane in lanes], axis=1))
            block = jnp.concatenate(quarters, axis=0).astype(BF16).reshape(3, 16, 128)
            for third in range(3):
                up[rank, tile // 2, 2 * third + tile % 2] = block[third]
    for at in range(12):
        down[2 * at : 2 * at + 2] = downw[:, 128 * at : 128 * at + 128].astype(BF16).reshape(2, 16, 128)
    places = lax.broadcasted_iota(jnp.int32, (TOK, TOK), 1)
    seg_line = seg_row[...].astype(F32)
    seg_column = jnp.transpose(jnp.broadcast_to(seg_line, (128, TOK)))[:, 0:1]
    same = seg_column == seg_line
    first = jnp.min(jnp.where(same, places, TOK).astype(F32), axis=1, keepdims=True)
    rows = lax.broadcasted_iota(jnp.int32, (TOK, 128), 0).astype(F32)
    angles = (rows - first) * freq[...]
    cos[...] = jnp.cos(angles)
    lanes = lax.broadcasted_iota(jnp.int32, (TOK, 128), 1)
    sine = jnp.sin(angles)
    sin[...] = jnp.where(lanes < 64, -sine, sine)
    bias[...] = mask_bias(seg_column, seg_line)


def prepare(qkv, out, up, down, gains, segment_ids, pick):
    steps = np.float32(THETA) ** (-np.arange(0, HD, 2, dtype=np.float32) / np.float32(HD))
    gap = np.zeros((16,), np.float32)
    freq = jnp.asarray(np.concatenate([steps, gap, steps, gap]).reshape(1, 128), F32)
    return pl.pallas_call(
        prepare_kernel,
        name="prepare",
        out_shape=(
            shape((2, 3, 5, 16, 128)),
            shape((4, 2, 6, 16, 128)),
            shape((24, 16, 128)),
            shape((TOK, 128), F32),
            shape((TOK, 128), F32),
            shape((TOK, TOK), F32),
        ),
        in_specs=[VMEM] * 8,
        out_specs=[VMEM] * 6,
        compiler_params=pltpu.CompilerParams(vmem_limit_bytes=62 * MIB),
    )(qkv, out, up, down, gains.T, segment_ids.reshape(1, TOK), freq, pick)


def finish_kernel(att, up, down, block, grad, *refs):
    old, new = (refs[0:5], refs[5:10], refs[10:15]), (refs[17:22], refs[22:27], refs[27:32])
    for src, dst in ((block, refs[15]), (grad, refs[16])):

        def move(at, src=src, dst=dst):
            dst[at, :] = src[at, :]

        each_rows(64, move)


    def step(number, at, gradient):
        values = [group[number][at] for group in old]
        for group, value in zip(new, adamw_step(*values, gradient, RATES[number], DECAYS[number])):
            group[number][at] = value

    everything = slice(None)
    for number, (part, k) in enumerate(ATT_SPOTS):
        which, width, start = (0, 768, 128 * number) if number < 6 else (1, 384, 128 * number - 768)
        block = att[part, :, k].reshape(48, 128)
        for at in range(4):
            lane = width * at + start
            step(which, (everything, slice(lane, lane + 128)), block[12 * at : 12 * at + 12])
    blocks = {}
    for rank in range(4):
        for tile in range(4):
            units = [up[rank, tile // 2, 2 * third + tile % 2] for third in range(3)]
            block = jnp.concatenate(units, axis=0)
            for quarter in range(4):
                blocks[rank, quarter, tile] = block[12 * quarter : 12 * quarter + 12]
    for start, pieces in hidden_chunks():
        for half in range(2):
            parts = [
                blocks[rank, 2 * half + high, tile][:, lane : lane + 32] for rank, high, tile, lane in pieces
            ]
            lane = 4096 * half + start
            step(2, (everything, slice(lane, lane + 128)), jnp.concatenate(parts, axis=1))
    for at in range(12):
        step(3, (everything, slice(128 * at, 128 * at + 128)), down[2 * at : 2 * at + 2].reshape(32, 128))
    step(4, (everything, everything), att[1, 0, 4][0:2, 0:12])


def finish(sums, results, masters, firsts, seconds):
    kinds = [shape(master.shape, F32) for master in masters]
    return pl.pallas_call(
        finish_kernel,
        name="finish",
        out_shape=[shape((TOK, D)), shape((TOK, D), F32)] + kinds * 3,
        in_specs=[VMEM] * 20,
        out_specs=[VMEM] * 17,
        compiler_params=pltpu.CompilerParams(vmem_limit_bytes=62 * MIB),
    )(*sums, *results, *masters, *firsts, *seconds)


def body(
    tokens_in,
    cotangent,
    segment_ids,
    proj_qkv,
    proj_out,
    proj_up,
    proj_down,
    norm_gains,
    first_qkv,
    first_out,
    first_up,
    first_down,
    first_gains,
    second_qkv,
    second_out,
    second_up,
    second_down,
    second_gains,
):
    spread, pick, owner = tables()
    att_units, up_units, down_units, cos, sin, bias = prepare(
        proj_qkv, proj_out, proj_up, proj_down, norm_gains, segment_ids, pick
    )
    (
        down_all, wq, wo, wgu, n2t, dy_all, heads, a_t, n1_t, middle, gains, gate_up, z_t, y_part,
    ) = forward(
        att_units, up_units, down_units, tokens_in, cotangent, bias, cos, sin, spread, pick, owner
    )
    att_sum, up_sum, down_sum, block_output, input_grad, *_ = backward(
        tokens_in, cos, sin, bias, spread, pick, owner, gains, cotangent,
        down_all, wq, wo, wgu, n2t, dy_all, heads, a_t, n1_t, middle, gate_up, z_t, y_part,
    )
    block_output, input_grad, *updated = finish(
        (att_sum, up_sum, down_sum),
        (block_output, input_grad),
        (proj_qkv, proj_out, proj_up, proj_down, norm_gains.T),
        (first_qkv, first_out, first_up, first_down, first_gains.T),
        (second_qkv, second_out, second_up, second_down, second_gains.T),
    )
    updated = [value.T if number % 5 == 4 else value for number, value in enumerate(updated)]
    return (block_output, input_grad, *updated)


def solution(mesh):
    rows = P("fsdp", None)
    return jax.shard_map(
        body,
        mesh=mesh,
        in_specs=(rows, rows, P("fsdp")) + (rows,) * 15,
        out_specs=(rows,) * 17,
        check_vma=False,
    )
```
